128 devices in a mesh: img: 8 (over y, x_lo), seq: 16 (over z, x_hi, core).
Axes of the slice: x: 4 (x_hi: 2, x_lo: 2; x = x_hi * 2 + x_lo), y: 4, z: 4, core: 2. Of those that a mesh axis runs over, the one named last changes fastest.
Arguments:
- image_query: bfloat16 [8, 2048, 1280], P('img', 'seq'), may hold values from -7 to 7
- image_key: bfloat16 [8, 2048, 1280], P('img', 'seq'), may hold values from -7 to 7
- image_value: bfloat16 [8, 2048, 1280], P('img', 'seq'), may hold values from -3 to 3
- image_output: bfloat16 [8, 2048, 1280], P('img', 'seq'), may hold values from -0.875 to 0.875
- output_grad: bfloat16 [8, 2048, 2432], P('img', 'seq'), may hold values from -48 to 48
- image_logsum: float32 [8, 2048, 20], P('img', 'seq'), may hold values from 8 to 9
- text_query: bfloat16 [8, 333, 1280], P('img'), may hold values from -7 to 7
- text_key: bfloat16 [8, 333, 1280], P('img'), may hold values from -7 to 7
- text_value: bfloat16 [8, 333, 1280], P('img'), may hold values from -3 to 3
- text_output: bfloat16 [8, 333, 1280], P('img'), may hold values from -0.875 to 0.875
- text_grad: bfloat16 [8, 333, 1280], P('img'), may hold values from -48 to 48
- text_logsum: float32 [8, 333, 20], P('img'), may hold values from 8 to 9
- out_weight: bfloat16 [2432, 1280], replicated, may hold values from -0.125 to 0.125
Outputs:
- query_grad: bfloat16 [8, 2048, 1280], P('img', 'seq')
- key_grad: bfloat16 [8, 2048, 1280], P('img', 'seq')
- value_grad: bfloat16 [8, 2048, 1280], P('img', 'seq')
- text_query_grad: bfloat16 [8, 333, 1280], P('img')
- text_key_grad: bfloat16 [8, 333, 1280], P('img')
- text_value_grad: bfloat16 [8, 333, 1280], P('img')
- weight_grad: float32 [2432, 1280], P('seq')
The draws below stay inside these ranges and needn't reach their ends.
All inputs are finite; a program needn't handle non-finite values.
Results may differ from the reference program's by a relative error of at most 0.017.
Values may be sent and summed in bfloat16 or wider, within the bound.
No kernel may reach another device: no remote copies, remote signals or barrier semaphores. Data moves between devices by JAX's collectives and lax.ppermute only.
A program may use at most 192 MiB of HBM per device.

```python
import jax
import jax.numpy as jnp
from jax import lax

D = 2432
HEADS = 20
TXT = 333
TOK_DEV = 128
HD = 1280
S = 2048
IMAGES = 8
N_SEQ = 16


def levels(key, extent, cuts, low, largest):
    factor_of, own = 1.0, jax.random.fold_in(key, 6)
    for axis_at, parts in cuts:
        steps = jnp.exp(jax.random.uniform(jax.random.fold_in(own, axis_at), (parts,), jnp.float32, low / len(cuts), largest / len(cuts)))
        factor_of = factor_of * jnp.repeat(steps, extent[axis_at] // parts).reshape([-1 if axis == axis_at else 1 for axis in range(len(extent))])
    return factor_of


def centred(own_key, shape, spread, limit, split=(), dtype=jnp.bfloat16):
    result = jax.random.normal(own_key, shape, jnp.float32) * spread
    if len(split) > 0:
        result = levels(own_key, shape, split, -0.22, 0.18) * result
    return jnp.clip(result, min=-limit, max=limit).astype(dtype)


def setup_inputs(seed: int = 0) -> dict:
    keys = jax.random.split(jax.random.key(seed), 14)
    return {
        "image_query": centred(keys[0], (IMAGES, S, HD), 1.1, 7.0, ((0, 8), (1, 16))),
        "image_key": centred(keys[1], (IMAGES, S, HD), 1.1, 7.0, ((0, 8), (1, 16))),
        "image_value": centred(keys[2], (IMAGES, S, HD), 0.5, 3.0, ((0, 8), (1, 16))),
        "image_output": centred(keys[3], (IMAGES, S, HD), 0.15, 0.875, ((0, 8), (1, 16))),
        "output_grad": centred(keys[4], (IMAGES, S, D), 8.0, 48.0, ((0, 8), (1, 16))),
        "image_logsum": jnp.clip(8.0 + 1.0 * jax.random.uniform(keys[5], (IMAGES, S, HEADS), jnp.float32) ** levels(keys[5], (IMAGES, S, HEADS), ((0, 8), (1, 16)), -0.2, 0.2), 8.0, 9.0),
        "text_query": centred(keys[6], (IMAGES, TXT, HD), 1.1, 7.0, ((0, 8),)),
        "text_key": centred(keys[7], (IMAGES, TXT, HD), 1.1, 7.0, ((0, 8),)),
        "text_value": centred(keys[8], (IMAGES, TXT, HD), 0.5, 3.0, ((0, 8),)),
        "text_output": centred(keys[9], (IMAGES, TXT, HD), 0.15, 0.875, ((0, 8),)),
        "text_grad": centred(keys[10], (IMAGES, TXT, HD), 8.0, 48.0, ((0, 8),)),
        "text_logsum": jnp.clip(8.0 + 1.0 * jax.random.uniform(keys[11], (IMAGES, TXT, HEADS), jnp.float32) ** levels(keys[11], (IMAGES, TXT, HEADS), ((0, 8),), -0.2, 0.2), 8.0, 9.0),
        "out_weight": centred(keys[12], (D, HD), D ** -0.5, 0.125),
    }


def row_dot(grads_out, outputs, head_count):
    product = grads_out.astype(jnp.float32) * outputs.astype(jnp.float32)
    return product.reshape(product.shape[0], head_count, -1).sum(axis=-1)


def pair_grads(queries, grads_out, log_sum, row_dots, key_rows, value_rows):
    head_count = log_sum.shape[1]
    query_count = queries.shape[0]
    key_count = key_rows.shape[0]
    head_width = queries.shape[1] // head_count
    scaling = head_width ** -0.5
    query_heads = queries.astype(jnp.float32).reshape(query_count, head_count, head_width)
    grad_heads = grads_out.astype(jnp.float32).reshape(query_count, head_count, head_width)
    key_heads = key_rows.astype(jnp.float32).reshape(key_count, head_count, head_width)
    value_heads = value_rows.astype(jnp.float32).reshape(key_count, head_count, head_width)
    scores = jnp.einsum("qhe,khe->hqk", query_heads, key_heads) * scaling
    weights = jnp.exp(scores - log_sum.T[:, :, None])
    grad_weights = jnp.einsum("qhe,khe->hqk", grad_heads, value_heads)
    grad_scores = weights * (grad_weights - row_dots.T[:, :, None])
    weights_low = lax.optimization_barrier(weights.astype(jnp.bfloat16)).astype(jnp.float32)
    scores_low = lax.optimization_barrier(grad_scores.astype(jnp.bfloat16)).astype(jnp.float32)
    query_part = jnp.einsum("hqk,khe->qhe", scores_low, key_heads) * scaling
    key_part = jnp.einsum("hqk,qhe->khe", scores_low, query_heads) * scaling
    value_part = jnp.einsum("hqk,qhe->khe", weights_low, grad_heads)
    return (query_part.reshape(query_count, -1), key_part.reshape(key_count, -1),
            value_part.reshape(key_count, -1))


def reference(image_query, image_key, image_value, image_output, output_grad, image_logsum,
              text_query, text_key, text_value, text_output, text_grad, text_logsum, out_weight):
    head_count = image_logsum.shape[-1]

    def one_image(inputs):
        (queries, key_rows, value_rows, outputs, upstream, log_sum,
         text_queries, text_keys, text_values, text_outs, text_dout, text_lsum) = inputs
        image_dout = jnp.dot(upstream, out_weight, preferred_element_type=jnp.float32).astype(jnp.bfloat16)
        image_dots = row_dot(image_dout, outputs, head_count)
        text_dots = row_dot(text_dout, text_outs, head_count)
        all_keys = jnp.concatenate([key_rows, text_keys], axis=0)
        all_values = jnp.concatenate([value_rows, text_values], axis=0)
        feature = queries.shape[1]
        length = queries.shape[0]

        def query_block(running, section):
            block_query, block_dout, block_lsum, block_dots = section
            query_part, key_part, value_part = pair_grads(block_query, block_dout, block_lsum, block_dots,
                                                          all_keys, all_values)
            return (running[0] + key_part, running[1] + value_part), query_part

        zeros_grad = jnp.zeros(all_keys.shape, jnp.float32)
        sections = (queries.reshape(N_SEQ, TOK_DEV, feature), image_dout.reshape(N_SEQ, TOK_DEV, feature),
                    log_sum.reshape(N_SEQ, TOK_DEV, head_count), image_dots.reshape(N_SEQ, TOK_DEV, head_count))
        (key_total, value_total), query_blocks = lax.scan(query_block, (zeros_grad, zeros_grad), sections)
        text_qpart, text_kpart, text_vpart = pair_grads(text_queries, text_dout, text_lsum, text_dots,
                                                        all_keys, all_values)
        key_total = key_total + text_kpart
        value_total = value_total + text_vpart

        def weight_block(running, section):
            block_grad, block_out = section
            term = jnp.dot(block_grad.T, block_out, preferred_element_type=jnp.float32)
            return running + lax.optimization_barrier(term.astype(jnp.bfloat16)).astype(jnp.float32), None

        weight_total, ignored = lax.scan(
            weight_block, jnp.zeros((upstream.shape[1], feature), jnp.float32),
            (upstream.reshape(N_SEQ, TOK_DEV, upstream.shape[1]), outputs.reshape(N_SEQ, TOK_DEV, feature)))
        return (query_blocks.reshape(length, feature).astype(jnp.bfloat16),
                key_total[:length].astype(jnp.bfloat16), value_total[:length].astype(jnp.bfloat16),
                text_qpart.astype(jnp.bfloat16), key_total[length:].astype(jnp.bfloat16),
                value_total[length:].astype(jnp.bfloat16), weight_total)

    results = lax.map(one_image, (image_query, image_key, image_value, image_output, output_grad, image_logsum,
                                  text_query, text_key, text_value, text_output, text_grad, text_logsum))
    return (results[0], results[1], results[2], results[3], results[4], results[5],
            jnp.sum(results[6], axis=0))
```

```python
import jax
import jax.numpy as jnp
from jax import lax
from jax.experimental import pallas as pl
from jax.experimental.pallas import tpu as pltpu
from jax.sharding import Mesh
from jax.sharding import PartitionSpec as P

SEQ = ("z", "xh", "core")
CHIPS = ("z", "xh")
IMG = ("y", "xl")
BF = jnp.bfloat16
F32 = jnp.float32
NT = (((1,), (1,)), ((), ()))

N = 16
TOK = 128
S = N * TOK
TXT = 333
TXT_Q = 384
TXT_K = 336
HALF = 176
HALF_Q = 256
SH = N * TOK // 2
W_ROWS = S + TXT_Q
L_ROWS = SH + HALF_Q
SCALE = 0.125
MSG = 400
OUT = 288
TOUT = TXT_K + HALF + TXT_K
VMEM_LIMIT = 56 * 2**20


def iota(shape, dim):
    return lax.broadcasted_iota(jnp.int32, shape, dim)


def thirds(x):
    high = x.astype(BF).astype(F32)
    rest = x - high
    middle = rest.astype(BF).astype(F32)
    return high, middle, rest - middle


def dot(a, b):
    return jnp.dot(a, b, preferred_element_type=F32)


def dot_nt(a, b):
    return lax.dot_general(a, b, NT, preferred_element_type=F32)


def swap_halves(x):
    return pltpu.roll(x, 64, 1)


def picked_sum(pick, x):
    a, b, c = thirds(x)
    pick = pick.astype(BF)
    return dot_nt(pick, a.astype(BF)) + dot_nt(pick, b.astype(BF)) + dot_nt(pick, c.astype(BF))


def stat_rows(lsum, delta, base, row):
    width = lsum.shape[1]
    rows = iota((16, width), 0)
    tile = jnp.zeros((16, width), F32)
    for k, part in enumerate(thirds(lsum)):
        tile = jnp.where(rows == base + k, part[row : row + 1, :], tile)
    for k, part in enumerate(thirds(delta)):
        tile = jnp.where(rows == 8 + base + k, part[row : row + 1, :], tile)
    return tile


def pack_kernel(index, og, w, q, k, v, o, l, send):
    j = pl.program_id(0)
    g = dot(og[...], w[...]).astype(BF).astype(F32)
    qf, kf, vf = q[...].astype(F32), k[...].astype(F32), v[...].astype(F32)
    delta = picked_sum(
        jnp.where(iota((8, 256), 1) // 64 == iota((8, 256), 0), 1.0, 0.0),
        g * o[...].astype(F32),
    )
    lsum = picked_sum(
        jnp.where(iota((8, 20), 1) == 4 * j + iota((8, 20), 0), 1.0, 0.0), l[...]
    )
    low = iota((TOK, 128), 1) < 64

    def packed(a, b, r):
        t = 128 * (r // 2)
        a, b = a[:, t : t + 128], b[:, t : t + 128]
        if r % 2 == 0:
            return jnp.where(low, a, swap_halves(b)).astype(BF)
        return jnp.where(low, swap_halves(a), b).astype(BF)

    @pl.when(j < 4)
    def whole():
        for r in range(4):
            d = 4 * j + r
            send[d, 0:128, :] = packed(qf, g, r)
            send[d, 128:256, :] = packed(kf, vf, r)
            send[d, 384:400, :] = stat_rows(lsum, delta, 0, r).astype(BF)

    @pl.when(j == 4)
    def shared():
        parity = index[0] % 2
        here = iota((16, 128), 1) // 64 == parity
        for r in range(4):
            qg, kv = packed(qf, g, r), packed(kf, vf, r)
            stat = stat_rows(lsum, delta, 4, r)
            moved = swap_halves(stat)
            for qi in range(2):
                mine = jnp.where(here, jnp.where(parity == qi, stat, moved), 0.0)
                for ki in range(2):
                    d = 4 * r + 2 * qi + ki
                    send[d, 256:320, :] = qg[64 * qi : 64 * qi + 64]
                    send[d, 320:384, :] = kv[64 * ki : 64 * ki + 64]
                    send[d, 384:400, :] = (send[d, 384:400, :].astype(F32) + mine).astype(BF)


def pack(index, og, w, q, k, v, o, l):
    depth = og.shape[1]
    column = pl.BlockSpec((TOK, 256), lambda j, s: (0, j))
    return pl.pallas_call(
        pack_kernel,
        grid_spec=pltpu.PrefetchScalarGridSpec(
            num_scalar_prefetch=1,
            grid=(5,),
            in_specs=[
                pl.BlockSpec((TOK, depth), lambda j, s: (0, 0)),
                pl.BlockSpec((depth, 256), lambda j, s: (0, j)),
                column,
                column,
                column,
                column,
                pl.BlockSpec((TOK, 20), lambda j, s: (0, 0)),
            ],
            out_specs=pl.BlockSpec((N, MSG, 128), lambda j, s: (0, 0, 0)),
        ),
        out_shape=jax.ShapeDtypeStruct((N, MSG, 128), BF),
        compiler_params=pltpu.CompilerParams(vmem_limit_bytes=VMEM_LIMIT),
        name="pack",
    )(index, og, w, q, k, v, o, l)


def text_kernel(
    index, wq, wk, wv, wo, wg, lq, lk, lv, lo, lg, l, wqg, wkv, wst, lqg, lkv, lst, buf, lbuf
):
    d = index[0]
    for n, ref in enumerate((wq, wk, wv, wo, wg, lq, lk, lv, lo, lg)):
        buf[n] = jnp.zeros(buf.shape[1:], F32)
        buf[n, 0:TXT, :] = ref[...].astype(F32)
    lbuf[...] = jnp.zeros(lbuf.shape, F32)
    lbuf[0:TXT, :] = l[...]

    def gather(first, odd, q_rows, k_rows):
        q, k, v = buf[first, q_rows, :], buf[first + 1, k_rows, :], buf[first + 2, k_rows, :]
        o, g = buf[first + 3, q_rows, :], buf[first + 4, q_rows, :]

        def pair(a, b):
            low = iota(a.shape, 1) < 64
            left = jnp.where(odd, swap_halves(a), a)
            right = jnp.where(odd, b, swap_halves(b))
            return jnp.where(low, left, right)

        product = o * g
        mine = (iota(product.shape, 1) >= 64) == odd
        return pair(q, g), pair(k, v), jnp.where(mine, product, 0.0)

    qg, kv, product = gather(0, d % 2 == 1, slice(0, TXT_Q), slice(0, TXT_Q))
    ones = jnp.ones((8, 128), F32)
    pick = jnp.where(iota((8, 20), 1) == d, 1.0, 0.0)
    wqg[...] = qg.astype(BF)
    wkv[...] = kv.astype(BF)
    wst[...] = stat_rows(
        picked_sum(pick, lbuf[0:TXT_Q, :]), picked_sum(ones, product), 0, 0
    ).astype(BF)

    head = 16 + d // 4
    q_rows = pl.ds(pl.multiple_of(HALF * ((d % 4) // 2), 16), HALF_Q)
    k_rows = pl.ds(pl.multiple_of(HALF * (d % 2), 16), HALF_Q)
    qg, kv, product = gather(5, head % 2 == 1, q_rows, k_rows)
    inside = iota((HALF_Q, 128), 0) < HALF
    pick = jnp.where(iota((8, 20), 1) == head, 1.0, 0.0)
    lqg[...] = jnp.where(inside, qg, 0.0).astype(BF)
    lkv[...] = jnp.where(inside, kv, 0.0).astype(BF)
    lst[...] = stat_rows(
        picked_sum(pick, lbuf[q_rows, :]),
        picked_sum(ones, jnp.where(inside, product, 0.0)),
        4,
        0,
    ).astype(BF)


def text_prep(index, q, k, v, o, g, l):
    whole = pl.BlockSpec((TXT, 128), lambda i, s: (0, s[0] // 2))
    shared = pl.BlockSpec((TXT, 128), lambda i, s: (0, 8 + s[0] // 8))
    shapes = [
        (TXT_Q, 128), (TXT_Q, 128), (16, TXT_Q), (HALF_Q, 128), (HALF_Q, 128), (16, HALF_Q)
    ]
    return pl.pallas_call(
        text_kernel,
        grid_spec=pltpu.PrefetchScalarGridSpec(
            num_scalar_prefetch=1,
            grid=(1,),
            in_specs=[whole] * 5 + [shared] * 5 + [pl.BlockSpec((TXT, 20), lambda i, s: (0, 0))],
            out_specs=[pl.BlockSpec(s, lambda i, s_: (0, 0)) for s in shapes],
            scratch_shapes=[
                pltpu.VMEM((10, HALF + HALF_Q, 128), F32),
                pltpu.VMEM((HALF + HALF_Q, 20), F32),
            ],
        ),
        out_shape=[jax.ShapeDtypeStruct(s, BF) for s in shapes],
        compiler_params=pltpu.CompilerParams(vmem_limit_bytes=VMEM_LIMIT),
        name="text_prep",
    )(index, q, k, v, o, g, q, k, v, o, g, l)


def transposed(x):
    return x.astype(F32).T.astype(BF)


class Head:
    def __init__(self, refs):
        self.ka, self.va, self.b0, self.b1, self.qta, self.gta, self.kt, self.dkv, self.dqt = refs

    @staticmethod
    def scratch(rows):
        return [pltpu.VMEM((rows, 128), BF)] * 4 + [
            pltpu.VMEM((128, rows), BF),
            pltpu.VMEM((128, rows), BF),
            pltpu.VMEM((64, rows), BF),
            pltpu.VMEM((rows, 128), F32),
            pltpu.VMEM((64, rows), F32),
        ]

    def fill(self, at, qg, kv, stat, base):
        rows = qg.shape[0]
        lane = iota((rows, 128), 1)
        low = lane < 64
        zero = jnp.zeros((rows, 128), BF)
        here = pl.ds(at, rows)
        kf = kv.astype(F32)
        off = lane - 64 - base
        ka = jnp.where(low, kf * SCALE, jnp.where((off >= 0) & (off < 3), -1.0, 0.0))
        off = lane - 8 - base
        va = jnp.where(low, jnp.where((off >= 0) & (off < 3), -1.0, 0.0), kf)
        self.ka[here, :] = ka.astype(BF)
        self.va[here, :] = va.astype(BF)
        self.b0[here, :] = jnp.where(low, zero, qg)
        self.b1[here, :] = jnp.where(low, qg, zero)
        qgt = transposed(qg)
        self.qta[0:64, here] = qgt[0:64]
        self.qta[64:80, here] = stat
        self.qta[80:128, here] = jnp.zeros((48, rows), BF)
        self.gta[0:16, here] = stat
        self.gta[16:64, here] = jnp.zeros((48, rows), BF)
        self.gta[64:128, here] = qgt[64:128]
        self.kt[:, here] = transposed(kv)[0:64]

    def zero(self):
        self.dkv[...] = jnp.zeros(self.dkv.shape, F32)
        self.dqt[...] = jnp.zeros(self.dqt.shape, F32)

    def block(self, k0, kb, q0, qb):
        ks, qs = pl.ds(k0, kb), pl.ds(q0, qb)
        p = jnp.exp(dot(self.ka[ks, :], self.qta[:, qs]))
        ds = p * dot(self.va[ks, :], self.gta[:, qs])
        p, ds = p.astype(BF), ds.astype(BF)
        self.dkv[ks, :] += dot(p, self.b0[qs, :]) + dot(ds, self.b1[qs, :])
        self.dqt[:, qs] += dot(self.kt[:, ks], ds)

    def blocks(self, k_all, kb, q_all, qb):
        def q_step(i, _):
            q0 = pl.multiple_of(i * qb, 128)

            def k_step(n, _):
                self.block(pl.multiple_of(n * kb, 128), kb, q0, qb)
                return 0

            return lax.fori_loop(0, k_all // kb, k_step, 0)

        lax.fori_loop(0, q_all // qb, q_step, 0)


def attend_kernel(recv, wqg, wkv, wst, lqg, lkv, lst, out, tout, *refs):
    w, h = Head(refs[:9]), Head(refs[9:])
    for s in range(N):
        w.fill(TOK * s, recv[s, 0:128, :], recv[s, 128:256, :], recv[s, 384:400, :], 0)
    for m in range(N // 2):
        a, b = 2 * m, 2 * m + 1
        stat = jnp.where(
            iota((16, 128), 1) < 64, recv[a, 384:400, :], recv[b, 384:400, :]
        )
        h.fill(
            128 * m,
            jnp.concatenate([recv[a, 256:320, :], recv[b, 256:320, :]], 0),
            jnp.concatenate([recv[a, 320:384, :], recv[b, 320:384, :]], 0),
            stat,
            4,
        )
    for m in range(TXT_Q // 128):
        t = slice(128 * m, 128 * m + 128)
        w.fill(S + 128 * m, wqg[t, :], wkv[t, :], wst[:, t], 0)
    for m in range(HALF_Q // 128):
        t = slice(128 * m, 128 * m + 128)
        h.fill(SH + 128 * m, lqg[t, :], lkv[t, :], lst[:, t], 4)
    w.zero()
    h.zero()

    w.block(S, TXT_K, S, TXT_Q)

    def whole_text(n, _):
        at = pl.multiple_of(n * 512, 512)
        w.block(at, 512, S, TXT_Q)
        w.block(S, TXT_K, at, 512)
        return 0

    lax.fori_loop(0, S // 512, whole_text, 0)
    h.block(SH, HALF, SH, HALF_Q)

    def shared_text(n, _):
        at = pl.multiple_of(n * 512, 512)
        h.block(at, 512, SH, HALF_Q)
        h.block(SH, HALF, at, 512)
        return 0

    lax.fori_loop(0, SH // 512, shared_text, 0)

    h.blocks(SH, 256, SH, 512)
    w.blocks(S, 256, S, 512)

    factor = jnp.where(iota((128, 128), 1) < 64, SCALE, 1.0)
    for m in range(TXT_Q // 128):
        rows = min(128, TXT_K - 128 * m)
        tout[128 * m : 128 * m + rows, :] = (
            w.dkv[S + 128 * m : S + 128 * m + rows, :] * factor[:rows]
        ).astype(BF)
        lower = h.dqt[:, SH + 128 * m : SH + 128 * m + 128] if m < 2 else jnp.zeros((64, 128), F32)
        both = jnp.concatenate([w.dqt[:, S + 128 * m : S + 128 * m + 128], lower], 0)
        at = TXT_K + HALF + 128 * m
        tout[at : at + rows, :] = (both * SCALE).T[:rows].astype(BF)
    tout[TXT_K : TXT_K + 128, :] = (h.dkv[SH : SH + 128, :] * factor).astype(BF)
    tout[TXT_K + 128 : TXT_K + HALF, :] = (
        h.dkv[SH + 128 : SH + HALF, :] * factor[: HALF - 128]
    ).astype(BF)

    for s in range(N):
        out[s, 0:128, :] = (w.dkv[128 * s : 128 * s + 128, :] * factor).astype(BF)
        out[s, 128:192, :] = (h.dkv[64 * s : 64 * s + 64, :] * factor[:64]).astype(BF)
        a = w.dqt[:, 128 * s : 128 * s + 128] * SCALE
        both = jnp.concatenate([a, swap_halves(a)], 0).T
        out[s, 192:256, :] = both[0:64].astype(BF)
    for m in range(N // 2):
        a = h.dqt[:, 128 * m : 128 * m + 128] * SCALE
        both = jnp.concatenate([a, pltpu.roll(a, 96, 1)], 0).T
        out[2 * m, 256:288, :] = both[0:32].astype(BF)
        out[2 * m + 1, 256:288, :] = both[64:96].astype(BF)


def attend(recv, texts):
    full = pl.BlockSpec(memory_space=pltpu.VMEM)
    return pl.pallas_call(
        attend_kernel,
        in_specs=[full] * 7,
        out_specs=[full] * 2,
        out_shape=[
            jax.ShapeDtypeStruct((N, OUT, 128), BF),
            jax.ShapeDtypeStruct((TOUT, 128), BF),
        ],
        scratch_shapes=Head.scratch(W_ROWS) + Head.scratch(L_ROWS),
        compiler_params=pltpu.CompilerParams(vmem_limit_bytes=VMEM_LIMIT),
        name="attend",
    )(recv, *texts)


def lane_pair(even, odd):
    low = iota(even.shape, 1) < 64
    return (
        jnp.where(low, even, swap_halves(odd)),
        jnp.where(low, swap_halves(even), odd),
    )


def unpack_kernel(recv, dq, dk, dv):
    def part(d, rows):
        return recv[d, rows, :].astype(F32)

    for t in range(N // 2):
        lanes = slice(128 * t, 128 * t + 128)
        keys, values = lane_pair(part(2 * t, slice(0, 128)), part(2 * t + 1, slice(0, 128)))
        dk[:, lanes] = keys.astype(BF)
        dv[:, lanes] = values.astype(BF)
        first, second = lane_pair(part(2 * t, slice(192, 256)), part(2 * t + 1, slice(192, 256)))
        dq[0:64, lanes] = first.astype(BF)
        dq[64:128, lanes] = second.astype(BF)
    for t in range(2):
        lanes = slice(1024 + 128 * t, 1024 + 128 * t + 128)
        for half in range(2):
            rows = slice(64 * half, 64 * half + 64)
            keys, values = lane_pair(
                *(
                    part(4 * r + half, slice(128, 192)) + part(4 * r + 2 + half, slice(128, 192))
                    for r in (2 * t, 2 * t + 1)
                )
            )
            dk[rows, lanes] = keys.astype(BF)
            dv[rows, lanes] = values.astype(BF)
            first, second = lane_pair(
                *(
                    part(4 * r + 2 * half, slice(256, 288))
                    + part(4 * r + 2 * half + 1, slice(256, 288))
                    for r in (2 * t, 2 * t + 1)
                )
            )
            dq[64 * half : 64 * half + 32, lanes] = first.astype(BF)
            dq[64 * half + 32 : 64 * half + 64, lanes] = second.astype(BF)


def unpack(recv):
    full = pl.BlockSpec(memory_space=pltpu.VMEM)
    return pl.pallas_call(
        unpack_kernel,
        in_specs=[full],
        out_specs=[full] * 3,
        out_shape=[jax.ShapeDtypeStruct((TOK, 1280), BF)] * 3,
        compiler_params=pltpu.CompilerParams(vmem_limit_bytes=VMEM_LIMIT),
        name="unpack",
    )(recv)


def unpack_text_kernel(core, mine, other, dq, dk, dv):
    odd_core = core[0] == 1

    def part(d, rows):
        a, b = mine[d // 2, rows, :].astype(F32), other[d // 2, rows, :].astype(F32)
        return jnp.where(odd_core, b, a) if d % 2 == 0 else jnp.where(odd_core, a, b)

    at = TXT_K + HALF
    for t in range(N // 2):
        lanes = slice(128 * t, 128 * t + 128)
        keys, values = lane_pair(part(2 * t, slice(0, TXT_K)), part(2 * t + 1, slice(0, TXT_K)))
        dk[:, lanes] = keys[:TXT].astype(BF)
        dv[:, lanes] = values[:TXT].astype(BF)
        queries, _ = lane_pair(part(2 * t, slice(at, TOUT)), part(2 * t + 1, slice(at, TOUT)))
        dq[:, lanes] = queries[:TXT].astype(BF)
    shared = slice(TXT_K, TXT_K + HALF)
    shared_q = slice(at, at + HALF)
    for t in range(2):
        lanes = slice(1024 + 128 * t, 1024 + 128 * t + 128)
        for half in range(2):
            size = min(HALF, TXT - HALF * half)
            rows = slice(HALF * half, HALF * half + size)
            keys, values = lane_pair(
                *(
                    part(4 * r + half, shared) + part(4 * r + 2 + half, shared)
                    for r in (2 * t, 2 * t + 1)
                )
            )
            dk[rows, lanes] = keys[:size].astype(BF)
            dv[rows, lanes] = values[:size].astype(BF)
            _, queries = lane_pair(
                *(
                    part(4 * r + 2 * half, shared_q) + part(4 * r + 2 * half + 1, shared_q)
                    for r in (2 * t, 2 * t + 1)
                )
            )
            dq[rows, lanes] = queries[:size].astype(BF)


def unpack_text(core, mine, other):
    full = pl.BlockSpec(memory_space=pltpu.VMEM)
    return pl.pallas_call(
        unpack_text_kernel,
        in_specs=[pl.BlockSpec(memory_space=pltpu.SMEM), full, full],
        out_specs=[full] * 3,
        out_shape=[jax.ShapeDtypeStruct((TXT, 1280), BF)] * 3,
        compiler_params=pltpu.CompilerParams(vmem_limit_bytes=VMEM_LIMIT),
        name="unpack_text",
    )(core, mine, other)


def exchange(x, axes):
    return lax.all_to_all(x, axes, 0, 0, tiled=True)


def other_core(x):
    return lax.ppermute(x, "core", [(0, 1), (1, 0)])


def spread(x, axes):
    return exchange(jnp.broadcast_to(x[None], (lax.axis_size(axes), *x.shape)), axes)


def weight_gradient(og, o):
    chips = lax.axis_size(CHIPS)
    quarters = lax.axis_size("y")
    core = lax.axis_index("core")
    blocks = og.T.reshape(chips, 2, -1, og.shape[0])
    rows = blocks.shape[2]
    mine = lax.dynamic_index_in_dim(blocks, core, 1, False)
    theirs = lax.dynamic_index_in_dim(blocks, 1 - core, 1, False)
    left = jnp.concatenate([mine, other_core(theirs)], 2)
    right = jnp.concatenate([o, other_core(o)], 0)
    term = jnp.einsum("prt,tc->prc", left, right, preferred_element_type=F32).astype(BF)
    padded = -(-rows // (8 * quarters)) * 8 * quarters
    term = jnp.pad(term, ((0, 0), (0, padded - rows), (0, 0)))
    term = term.reshape(chips, quarters, padded // quarters, -1).swapaxes(0, 1)
    part = exchange(term, "y").astype(F32).sum(0).astype(BF)
    part = exchange(part, CHIPS).astype(F32).sum(0).astype(BF)
    part = spread(part, IMG).reshape(quarters, -1, *part.shape).astype(F32).sum(1)
    return part.reshape(padded, -1)[:rows]


def shards(
    image_query,
    image_key,
    image_value,
    image_output,
    output_grad,
    image_logsum,
    text_query,
    text_key,
    text_value,
    text_output,
    text_grad,
    text_logsum,
    out_weight,
):
    device = lax.axis_index(SEQ).astype(jnp.int32).reshape(1)
    core = lax.axis_index("core").astype(jnp.int32).reshape(1)
    send = pack(
        device,
        output_grad[0],
        out_weight,
        image_query[0],
        image_key[0],
        image_value[0],
        image_output[0],
        image_logsum[0],
    )
    recv = exchange(send, SEQ)
    texts = text_prep(
        device,
        text_query[0],
        text_key[0],
        text_value[0],
        text_output[0],
        text_grad[0],
        text_logsum[0],
    )
    out, text_out = attend(recv, texts)
    mine = spread(text_out, CHIPS)
    text_grads = unpack_text(core, mine, other_core(mine))
    grads = unpack(exchange(out, SEQ))
    weight_grad = weight_gradient(output_grad[0], image_output[0])
    return (*(g[None] for g in grads), *(g[None] for g in text_grads), weight_grad)


def solution(mesh):
    pairs = 2 if mesh.shape["img"] > 1 else 1
    finer = Mesh(
        mesh.devices.reshape(mesh.shape["img"] // pairs, pairs, 4, 2, 2),
        ("y", "xl", "z", "xh", "core"),
    )
    image = P(IMG, SEQ, None)
    text = P(IMG, None, None)
    return jax.shard_map(
        shards,
        mesh=finer,
        in_specs=(image,) * 6 + (text,) * 6 + (P(),),
        out_specs=(image,) * 3 + (text,) * 3 + (P(SEQ, None),),
        check_vma=False,
    )
```

```python
import jax
import jax.numpy as jnp
from jax import lax
from jax.experimental import pallas as pl
from jax.experimental.pallas import tpu as pltpu
from jax.sharding import Mesh
from jax.sharding import PartitionSpec as P

SEQ = ("z", "xh", "core")
CHIPS = ("z", "xh")
IMG = ("y", "xl")
BF = jnp.bfloat16
F32 = jnp.float32
NT = (((1,), (1,)), ((), ()))

N = 16
TOK = 128
S = N * TOK
TXT = 333
TXT_Q = 384
TXT_K = 336
HALF = 176
HALF_Q = 256
SH = N * TOK // 2
W_ROWS = S + TXT_Q
L_ROWS = SH + HALF_Q
SCALE = 0.125
MSG = 400
OUT = 288
TOUT = TXT_K + HALF + TXT_K
VMEM_LIMIT = 56 * 2**20


def iota(shape, dim):
    return lax.broadcasted_iota(jnp.int32, shape, dim)


def thirds(x):
    high = x.astype(BF).astype(F32)
    rest = x - high
    middle = rest.astype(BF).astype(F32)
    return high, middle, rest - middle


def dot(a, b):
    return jnp.dot(a, b, preferred_element_type=F32)


def dot_nt(a, b):
    return lax.dot_general(a, b, NT, preferred_element_type=F32)


def swap_halves(x):
    return pltpu.roll(x, 64, 1)


def picked_sum(pick, x):
    a, b, c = thirds(x)
    pick = pick.astype(BF)
    return dot_nt(pick, a.astype(BF)) + dot_nt(pick, b.astype(BF)) + dot_nt(pick, c.astype(BF))


def picked_rows(pick, x):
    a, b, c = thirds(x)
    pick = pick.astype(BF)
    return dot(pick, a.astype(BF)) + dot(pick, b.astype(BF)) + dot(pick, c.astype(BF))


def stat_rows(lsum, delta, base, row):
    width = lsum.shape[1]
    rows = iota((16, width), 0)
    tile = jnp.zeros((16, width), F32)
    for k, part in enumerate(thirds(lsum)):
        tile = jnp.where(rows == base + k, part[row : row + 1, :], tile)
    for k, part in enumerate(thirds(delta)):
        tile = jnp.where(rows == 8 + base + k, part[row : row + 1, :], tile)
    return tile


def pack_kernel(index, og, w, q, k, v, o, l, send):
    j = pl.program_id(0)
    g = dot(og[...], w[...]).astype(BF).astype(F32)
    qf, kf, vf = q[...].astype(F32), k[...].astype(F32), v[...].astype(F32)
    delta = picked_sum(
        jnp.where(iota((8, 256), 1) // 64 == iota((8, 256), 0), 1.0, 0.0),
        g * o[...].astype(F32),
    )
    lsum = picked_rows(
        jnp.where(iota((8, 20), 1) == 4 * j + iota((8, 20), 0), 1.0, 0.0), l[...]
    )
    low = iota((TOK, 128), 1) < 64

    def packed(a, b, r):
        t = 128 * (r // 2)
        a, b = a[:, t : t + 128], b[:, t : t + 128]
        if r % 2 == 0:
            return jnp.where(low, a, swap_halves(b)).astype(BF)
        return jnp.where(low, swap_halves(a), b).astype(BF)

    @pl.when(j < 4)
    def whole():
        for r in range(4):
            d = 4 * j + r
            send[d, 0:128, :] = packed(qf, g, r)
            send[d, 128:256, :] = packed(kf, vf, r)
            send[d, 384:400, :] = stat_rows(lsum, delta, 0, r).astype(BF)

    @pl.when(j == 4)
    def shared():
        parity = index[0] % 2
        here = iota((16, 128), 1) // 64 == parity
        for r in range(4):
            qg, kv = packed(qf, g, r), packed(kf, vf, r)
            stat = stat_rows(lsum, delta, 4, r)
            moved = swap_halves(stat)
            for qi in range(2):
                mine = jnp.where(here, jnp.where(parity == qi, stat, moved), 0.0)
                for ki in range(2):
                    d = 4 * r + 2 * qi + ki
                    send[d, 256:320, :] = qg[64 * qi : 64 * qi + 64]
                    send[d, 320:384, :] = kv[64 * ki : 64 * ki + 64]
                    send[d, 384:400, :] = (send[d, 384:400, :].astype(F32) + mine).astype(BF)


def pack(index, og, w, q, k, v, o, l):
    depth = og.shape[1]
    column = pl.BlockSpec((TOK, 256), lambda j, s: (0, j))
    return pl.pallas_call(
        pack_kernel,
        grid_spec=pltpu.PrefetchScalarGridSpec(
            num_scalar_prefetch=1,
            grid=(5,),
            in_specs=[
                pl.BlockSpec((TOK, depth), lambda j, s: (0, 0)),
                pl.BlockSpec((depth, 256), lambda j, s: (0, j)),
                column,
                column,
                column,
                column,
                pl.BlockSpec((20, TOK), lambda j, s: (0, 0)),
            ],
            out_specs=pl.BlockSpec((N, MSG, 128), lambda j, s: (0, 0, 0)),
        ),
        out_shape=jax.ShapeDtypeStruct((N, MSG, 128), BF),
        compiler_params=pltpu.CompilerParams(vmem_limit_bytes=VMEM_LIMIT),
        name="pack",
    )(index, og, w, q, k, v, o, l)


def text_kernel(
    index, wq, wk, wv, wo, wg, lq, lk, lv, lo, lg, l, wqg, wkv, wst, lqg, lkv, lst, buf, lbuf
):
    d = index[0]
    for n, ref in enumerate((wq, wk, wv, wo, wg, lq, lk, lv, lo, lg)):
        buf[n] = jnp.zeros(buf.shape[1:], F32)
        buf[n, 0:TXT, :] = ref[...].astype(F32)
    lbuf[...] = jnp.zeros(lbuf.shape, F32)
    lbuf[:, 0:TXT] = l[...]

    def gather(first, odd, q_rows, k_rows):
        q, k, v = buf[first, q_rows, :], buf[first + 1, k_rows, :], buf[first + 2, k_rows, :]
        o, g = buf[first + 3, q_rows, :], buf[first + 4, q_rows, :]

        def pair(a, b):
            low = iota(a.shape, 1) < 64
            left = jnp.where(odd, swap_halves(a), a)
            right = jnp.where(odd, b, swap_halves(b))
            return jnp.where(low, left, right)

        product = o * g
        mine = (iota(product.shape, 1) >= 64) == odd
        return pair(q, g), pair(k, v), jnp.where(mine, product, 0.0)

    qg, kv, product = gather(0, d % 2 == 1, slice(0, TXT_Q), slice(0, TXT_Q))
    ones = jnp.ones((8, 128), F32)
    pick = jnp.where(iota((8, 20), 1) == d, 1.0, 0.0)
    wqg[...] = qg.astype(BF)
    wkv[...] = kv.astype(BF)
    wst[...] = stat_rows(
        picked_rows(pick, lbuf[:, 0:TXT_Q]), picked_sum(ones, product), 0, 0
    ).astype(BF)

    head = 16 + d // 4
    q_rows = pl.ds(pl.multiple_of(HALF * ((d % 4) // 2), 16), HALF_Q)
    k_rows = pl.ds(pl.multiple_of(HALF * (d % 2), 16), HALF_Q)
    qg, kv, product = gather(5, head % 2 == 1, q_rows, k_rows)
    inside = iota((HALF_Q, 128), 0) < HALF
    pick = jnp.where(iota((8, 20), 1) == head, 1.0, 0.0)
    lqg[...] = jnp.where(inside, qg, 0.0).astype(BF)
    lkv[...] = jnp.where(inside, kv, 0.0).astype(BF)
    lsum = picked_rows(pick, lbuf[...])
    lst[...] = stat_rows(
        jnp.where(
            d % 4 < 2, lsum[:, 0:HALF_Q], pltpu.roll(lsum, lsum.shape[1] - HALF, 1)[:, 0:HALF_Q]
        ),
        picked_sum(ones, jnp.where(inside, product, 0.0)),
        4,
        0,
    ).astype(BF)


def text_prep(index, q, k, v, o, g, l):
    whole = pl.BlockSpec((TXT, 128), lambda i, s: (0, s[0] // 2))
    shared = pl.BlockSpec((TXT, 128), lambda i, s: (0, 8 + s[0] // 8))
    shapes = [
        (TXT_Q, 128), (TXT_Q, 128), (16, TXT_Q), (HALF_Q, 128), (HALF_Q, 128), (16, HALF_Q)
    ]
    return pl.pallas_call(
        text_kernel,
        grid_spec=pltpu.PrefetchScalarGridSpec(
            num_scalar_prefetch=1,
            grid=(1,),
            in_specs=[whole] * 5 + [shared] * 5 + [pl.BlockSpec((20, TXT), lambda i, s: (0, 0))],
            out_specs=[pl.BlockSpec(s, lambda i, s_: (0, 0)) for s in shapes],
            scratch_shapes=[
                pltpu.VMEM((10, HALF + HALF_Q, 128), F32),
                pltpu.VMEM((20, 512), F32),
            ],
        ),
        out_shape=[jax.ShapeDtypeStruct(s, BF) for s in shapes],
        compiler_params=pltpu.CompilerParams(vmem_limit_bytes=VMEM_LIMIT),
        name="text_prep",
    )(index, q, k, v, o, g, q, k, v, o, g, l)


def transposed(x):
    return x.astype(F32).T.astype(BF)


class Head:
    def __init__(self, refs):
        self.ka, self.va, self.b0, self.b1, self.qta, self.gta, self.kt, self.dkv, self.dqt = refs

    @staticmethod
    def scratch(rows):
        return [pltpu.VMEM((rows, 128), BF)] * 4 + [
            pltpu.VMEM((128, rows), BF),
            pltpu.VMEM((128, rows), BF),
            pltpu.VMEM((64, rows), BF),
            pltpu.VMEM((rows, 128), F32),
            pltpu.VMEM((64, rows), F32),
        ]

    def fill(self, at, qg, kv, stat, base):
        rows = qg.shape[0]
        lane = iota((rows, 128), 1)
        low = lane < 64
        zero = jnp.zeros((rows, 128), BF)
        here = pl.ds(at, rows)
        kf = kv.astype(F32)
        off = lane - 64 - base
        ka = jnp.where(low, kf * SCALE, jnp.where((off >= 0) & (off < 3), -1.0, 0.0))
        off = lane - 8 - base
        va = jnp.where(low, jnp.where((off >= 0) & (off < 3), -1.0, 0.0), kf)
        self.ka[here, :] = ka.astype(BF)
        self.va[here, :] = va.astype(BF)
        self.b0[here, :] = jnp.where(low, zero, qg)
        self.b1[here, :] = jnp.where(low, qg, zero)
        qgt = transposed(qg)
        self.qta[0:64, here] = qgt[0:64]
        self.qta[64:80, here] = stat
        self.qta[80:128, here] = jnp.zeros((48, rows), BF)
        self.gta[0:16, here] = stat
        self.gta[16:64, here] = jnp.zeros((48, rows), BF)
        self.gta[64:128, here] = qgt[64:128]
        self.kt[:, here] = transposed(kv)[0:64]

    def zero(self):
        self.dkv[...] = jnp.zeros(self.dkv.shape, F32)
        self.dqt[...] = jnp.zeros(self.dqt.shape, F32)

    def block(self, k0, kb, q0, qb):
        ks, qs = pl.ds(k0, kb), pl.ds(q0, qb)
        p = jnp.exp(dot(self.ka[ks, :], self.qta[:, qs]))
        ds = p * dot(self.va[ks, :], self.gta[:, qs])
        p, ds = p.astype(BF), ds.astype(BF)
        self.dkv[ks, :] += dot(p, self.b0[qs, :]) + dot(ds, self.b1[qs, :])
        self.dqt[:, qs] += dot(self.kt[:, ks], ds)

    def blocks(self, k_all, kb, q_all, qb):
        def q_step(i, _):
            q0 = pl.multiple_of(i * qb, 128)

            def k_step(n, _):
                self.block(pl.multiple_of(n * kb, 128), kb, q0, qb)
                return 0

            return lax.fori_loop(0, k_all // kb, k_step, 0)

        lax.fori_loop(0, q_all // qb, q_step, 0)


def fill_whole(w, recv):
    for s in range(N):
        w.fill(TOK * s, recv[s, 0:128, :], recv[s, 128:256, :], recv[s, 384:400, :], 0)


def fill_shared(h, recv):
    for m in range(N // 2):
        a, b = 2 * m, 2 * m + 1
        stat = jnp.where(iota((16, 128), 1) < 64, recv[a, 384:400, :], recv[b, 384:400, :])
        h.fill(
            128 * m,
            jnp.concatenate([recv[a, 256:320, :], recv[b, 256:320, :]], 0),
            jnp.concatenate([recv[a, 320:384, :], recv[b, 320:384, :]], 0),
            stat,
            4,
        )


def text_pairs_kernel(
    recv, wqg, wkv, wst, lqg, lkv, lst, tout, w_dkv, w_dqt, h_dkv, h_dqt, *refs
):
    w, h = Head(refs[:9]), Head(refs[9:])
    fill_whole(w, recv)
    fill_shared(h, recv)
    for m in range(TXT_Q // 128):
        t = slice(128 * m, 128 * m + 128)
        w.fill(S + 128 * m, wqg[t, :], wkv[t, :], wst[:, t], 0)
    for m in range(HALF_Q // 128):
        t = slice(128 * m, 128 * m + 128)
        h.fill(SH + 128 * m, lqg[t, :], lkv[t, :], lst[:, t], 4)
    w.zero()
    h.zero()

    w.block(S, TXT_K, S, TXT_Q)

    def whole_text(n, _):
        at = pl.multiple_of(n * 1024, 1024)
        w.block(at, 1024, S, TXT_Q)
        w.block(S, TXT_K, at, 1024)
        return 0

    lax.fori_loop(0, S // 1024, whole_text, 0)
    h.block(SH, HALF, SH, HALF_Q)
    h.block(0, SH, SH, HALF_Q)
    h.block(SH, HALF, 0, SH)

    w_dkv[...] = w.dkv[0:S, :]
    w_dqt[...] = w.dqt[:, 0:S]
    h_dkv[...] = h.dkv[0:SH, :]
    h_dqt[...] = h.dqt[:, 0:SH]

    factor = jnp.where(iota((128, 128), 1) < 64, SCALE, 1.0)

    def put(at, value):
        value = value.astype(BF)
        for n in range(N // 2):
            tout[n, at : at + value.shape[0], :] = value

    for m in range(TXT_Q // 128):
        rows = min(128, TXT_K - 128 * m)
        put(128 * m, w.dkv[S + 128 * m : S + 128 * m + rows, :] * factor[:rows])
        lower = h.dqt[:, SH + 128 * m : SH + 128 * m + 128] if m < 2 else jnp.zeros((64, 128), F32)
        both = jnp.concatenate([w.dqt[:, S + 128 * m : S + 128 * m + 128], lower], 0)
        put(TXT_K + HALF + 128 * m, (both * SCALE).T[:rows])
    put(TXT_K, h.dkv[SH : SH + 128, :] * factor)
    put(TXT_K + 128, h.dkv[SH + 128 : SH + HALF, :] * factor[: HALF - 128])


STATE = [(S, 128), (64, S), (SH, 128), (64, SH)]


def text_pairs(recv, texts):
    full = pl.BlockSpec(memory_space=pltpu.VMEM)
    return pl.pallas_call(
        text_pairs_kernel,
        in_specs=[full] * 7,
        out_specs=[full] * 5,
        out_shape=[jax.ShapeDtypeStruct((N // 2, TOUT, 128), BF)]
        + [jax.ShapeDtypeStruct(s, F32) for s in STATE],
        scratch_shapes=Head.scratch(W_ROWS) + Head.scratch(L_ROWS),
        compiler_params=pltpu.CompilerParams(vmem_limit_bytes=VMEM_LIMIT),
        name="text_pairs",
    )(recv, *texts)


def scales():
    return jnp.where(iota((128, 128), 1) < 64, SCALE, 1.0)


def image_pairs_kernel(recv, a, b, c, d, out, *refs):
    w, h = Head(refs[:9]), Head(refs[9:])
    fill_whole(w, recv)
    fill_shared(h, recv)
    for source, target in ((a, w.dkv), (b, w.dqt), (c, h.dkv), (d, h.dqt)):
        target[...] = source[...]
    h.blocks(SH, 1024, SH, 512)
    w.blocks(S, 1024, S, 512)
    factor = scales()
    for s in range(N):
        out[s, 0:128, :] = (w.dkv[128 * s : 128 * s + 128, :] * factor).astype(BF)
        part = w.dqt[:, 128 * s : 128 * s + 128] * SCALE
        both = jnp.concatenate([part, swap_halves(part)], 0).T
        out[s, 128:192, :] = both[0:64].astype(BF)
        out[s, 192:256, :] = (h.dkv[64 * s : 64 * s + 64, :] * factor[:64]).astype(BF)
    for m in range(N // 2):
        part = h.dqt[:, 128 * m : 128 * m + 128] * SCALE
        both = jnp.concatenate([part, pltpu.roll(part, 96, 1)], 0).T
        out[2 * m, 256:288, :] = both[0:32].astype(BF)
        out[2 * m + 1, 256:288, :] = both[64:96].astype(BF)


def image_pairs(recv, state):
    full = pl.BlockSpec(memory_space=pltpu.VMEM)
    return pl.pallas_call(
        image_pairs_kernel,
        in_specs=[full] * 5,
        out_specs=full,
        out_shape=jax.ShapeDtypeStruct((N, OUT, 128), BF),
        scratch_shapes=Head.scratch(S) + Head.scratch(SH),
        compiler_params=pltpu.CompilerParams(vmem_limit_bytes=VMEM_LIMIT),
        name="image_pairs",
    )(recv, *state)


def lane_pair(even, odd):
    low = iota(even.shape, 1) < 64
    return (
        jnp.where(low, even, swap_halves(odd)),
        jnp.where(low, swap_halves(even), odd),
    )


def unpack_kernel(recv, dq, dk, dv):
    def part(d, rows):
        return recv[d, rows, :].astype(F32)

    for t in range(N // 2):
        lanes = slice(128 * t, 128 * t + 128)
        keys, values = lane_pair(part(2 * t, slice(0, 128)), part(2 * t + 1, slice(0, 128)))
        dk[:, lanes] = keys.astype(BF)
        dv[:, lanes] = values.astype(BF)
        first, second = lane_pair(part(2 * t, slice(128, 192)), part(2 * t + 1, slice(128, 192)))
        dq[0:64, lanes] = first.astype(BF)
        dq[64:128, lanes] = second.astype(BF)
    for t in range(2):
        lanes = slice(1024 + 128 * t, 1024 + 128 * t + 128)
        for half in range(2):
            rows = slice(64 * half, 64 * half + 64)
            keys, values = lane_pair(
                *(
                    part(4 * r + half, slice(192, 256)) + part(4 * r + 2 + half, slice(192, 256))
                    for r in (2 * t, 2 * t + 1)
                )
            )
            dk[rows, lanes] = keys.astype(BF)
            dv[rows, lanes] = values.astype(BF)
            first, second = lane_pair(
                *(
                    part(4 * r + 2 * half, slice(256, 288))
                    + part(4 * r + 2 * half + 1, slice(256, 288))
                    for r in (2 * t, 2 * t + 1)
                )
            )
            dq[64 * half : 64 * half + 32, lanes] = first.astype(BF)
            dq[64 * half + 32 : 64 * half + 64, lanes] = second.astype(BF)


def unpack(recv):
    full = pl.BlockSpec(memory_space=pltpu.VMEM)
    return pl.pallas_call(
        unpack_kernel,
        in_specs=[full],
        out_specs=[full] * 3,
        out_shape=[jax.ShapeDtypeStruct((TOK, 1280), BF)] * 3,
        compiler_params=pltpu.CompilerParams(vmem_limit_bytes=VMEM_LIMIT),
        name="unpack",
    )(recv)


def unpack_text_kernel(core, mine, other, dq, dk, dv):
    odd_core = core[0] == 1

    def part(d, rows):
        a, b = mine[d // 2, rows, :].astype(F32), other[d // 2, rows, :].astype(F32)
        return jnp.where(odd_core, b, a) if d % 2 == 0 else jnp.where(odd_core, a, b)

    at = TXT_K + HALF
    for t in range(N // 2):
        lanes = slice(128 * t, 128 * t + 128)
        keys, values = lane_pair(part(2 * t, slice(0, TXT_K)), part(2 * t + 1, slice(0, TXT_K)))
        dk[:, lanes] = keys[:TXT].astype(BF)
        dv[:, lanes] = values[:TXT].astype(BF)
        queries, _ = lane_pair(part(2 * t, slice(at, TOUT)), part(2 * t + 1, slice(at, TOUT)))
        dq[:, lanes] = queries[:TXT].astype(BF)
    shared = slice(TXT_K, TXT_K + HALF)
    shared_q = slice(at, at + HALF)
    for t in range(2):
        lanes = slice(1024 + 128 * t, 1024 + 128 * t + 128)
        for half in range(2):
            size = min(HALF, TXT - HALF * half)
            rows = slice(HALF * half, HALF * half + size)
            keys, values = lane_pair(
                *(
                    part(4 * r + half, shared) + part(4 * r + 2 + half, shared)
                    for r in (2 * t, 2 * t + 1)
                )
            )
            dk[rows, lanes] = keys[:size].astype(BF)
            dv[rows, lanes] = values[:size].astype(BF)
            _, queries = lane_pair(
                *(
                    part(4 * r + 2 * half, shared_q) + part(4 * r + 2 * half + 1, shared_q)
                    for r in (2 * t, 2 * t + 1)
                )
            )
            dq[rows, lanes] = queries[:size].astype(BF)


def unpack_text(core, mine, other):
    full = pl.BlockSpec(memory_space=pltpu.VMEM)
    return pl.pallas_call(
        unpack_text_kernel,
        in_specs=[pl.BlockSpec(memory_space=pltpu.SMEM), full, full],
        out_specs=[full] * 3,
        out_shape=[jax.ShapeDtypeStruct((TXT, 1280), BF)] * 3,
        compiler_params=pltpu.CompilerParams(vmem_limit_bytes=VMEM_LIMIT),
        name="unpack_text",
    )(core, mine, other)


def exchange(x, axes):
    return lax.all_to_all(x, axes, 0, 0, tiled=True)


def other_core(x):
    return lax.ppermute(x, "core", [(0, 1), (1, 0)])


def shifted(x, axis, by):
    size = lax.axis_size(axis)
    return lax.ppermute(x, axis, [(i, (i + by) % size) for i in range(size)])


def scattered_sum(x, axis, after=()):
    size, me = lax.axis_size(axis), lax.axis_index(axis)
    pieces = [
        shifted(lax.dynamic_index_in_dim(x, (me + by) % size, 0, False), axis, by)
        for by in range(1, size)
    ]
    pieces, _ = lax.optimization_barrier((pieces, after))
    own = lax.dynamic_index_in_dim(x, me, 0, False).astype(F32)
    for piece in pieces:
        own = own + piece.astype(F32)
    return own.astype(BF)


def gathered(x, axis):
    size, me = lax.axis_size(axis), lax.axis_index(axis)
    out = jnp.zeros((size, *x.shape), x.dtype)
    for by in range(size):
        piece = shifted(x, axis, by) if by else x
        out = lax.dynamic_update_index_in_dim(out, piece, (me - by) % size, 0)
    return out


def weight_gradient(og, o, before, after):
    z, xh, y = (lax.axis_size(a) for a in ("z", "xh", "y"))
    core = lax.axis_index("core")
    tokens = og.shape[0]
    rows = og.shape[1] // (2 * z * xh)
    padded = -(-rows // (8 * y)) * 8 * y
    blocks = og.T.reshape(z, xh, 2, rows, tokens)
    blocks = jnp.pad(blocks, ((0, 0),) * 3 + ((0, padded - rows), (0, 0)))
    blocks = blocks.reshape(z, xh, 2, y, padded // y, tokens).transpose(2, 3, 1, 0, 4, 5)
    mine = lax.dynamic_index_in_dim(blocks, core, 0, False)
    theirs = lax.dynamic_index_in_dim(blocks, 1 - core, 0, False)
    left = jnp.concatenate([mine, other_core(theirs)], 4)
    right = jnp.concatenate([o, other_core(o)], 0)
    part = jnp.dot(left.reshape(-1, 2 * tokens), right, preferred_element_type=F32).astype(BF)
    part = part.reshape(y, xh, z, padded // y, -1)
    part, _ = lax.optimization_barrier((part, before))
    part = scattered_sum(part, "y", after)
    for axis in ("xh", "z"):
        part = scattered_sum(part, axis)
    if lax.axis_size("xl") > 1:
        part = (part.astype(F32) + shifted(part, "xl", 1).astype(F32)).astype(BF)
    part = gathered(part, "y").astype(F32)
    return part.reshape(padded, -1)[:rows]


def shards(
    image_query,
    image_key,
    image_value,
    image_output,
    output_grad,
    image_logsum,
    text_query,
    text_key,
    text_value,
    text_output,
    text_grad,
    text_logsum,
    out_weight,
):
    device = lax.axis_index(SEQ).astype(jnp.int32).reshape(1)
    core = lax.axis_index("core").astype(jnp.int32).reshape(1)
    send = pack(
        device,
        output_grad[0],
        out_weight,
        image_query[0],
        image_key[0],
        image_value[0],
        image_output[0],
        image_logsum[0].T,
    )
    send, upstream, outputs = lax.optimization_barrier((send, output_grad[0], image_output[0]))
    recv = exchange(send, SEQ)
    texts = text_prep(
        device,
        text_query[0],
        text_key[0],
        text_value[0],
        text_output[0],
        text_grad[0],
        text_logsum[0].T,
    )
    text_out, *state = text_pairs(recv, texts)
    mine = exchange(text_out, CHIPS)
    text_grads = unpack_text(core, mine, other_core(mine))
    out = image_pairs(recv, state)
    grads = unpack(exchange(out, SEQ))
    weight_grad = weight_gradient(upstream, outputs, texts, (out, mine))
    return (*(g[None] for g in grads), *(g[None] for g in text_grads), weight_grad)


def solution(mesh):
    pairs = 2 if mesh.shape["img"] > 1 else 1
    finer = Mesh(
        mesh.devices.reshape(mesh.shape["img"] // pairs, pairs, 4, 2, 2),
        ("y", "xl", "z", "xh", "core"),
    )
    image = P(IMG, SEQ, None)
    text = P(IMG, None, None)
    return jax.shard_map(
        shards,
        mesh=finer,
        in_specs=(image,) * 6 + (text,) * 6 + (P(),),
        out_specs=(image,) * 3 + (text,) * 3 + (P(SEQ, None),),
        check_vma=False,
    )
```

```python
import jax
import jax.numpy as jnp
from jax import lax
from jax.experimental import pallas as pl
from jax.experimental.pallas import tpu as pltpu
from jax.sharding import Mesh
from jax.sharding import PartitionSpec as P

SEQ = ("z", "xh", "core")
CHIPS = ("z", "xh")
IMG = ("y", "xl")
BF = jnp.bfloat16
F32 = jnp.float32
NT = (((1,), (1,)), ((), ()))

N = 16
TOK = 128
S = N * TOK
TXT = 333
TXT_Q = 384
TXT_K = 336
HALF = 176
HALF_Q = 256
SH = N * TOK // 2
W_ROWS = S + TXT_Q
L_ROWS = SH + HALF_Q
SCALE = 0.125
MSG = 400
OUT = 288
TOUT = TXT_K + HALF + TXT_K
WOUT = 400
VMEM_LIMIT = 56 * 2**20


def iota(shape, dim):
    return lax.broadcasted_iota(jnp.int32, shape, dim)


def thirds(x):
    high = x.astype(BF).astype(F32)
    rest = x - high
    middle = rest.astype(BF).astype(F32)
    return high, middle, rest - middle


def dot(a, b):
    return jnp.dot(a, b, preferred_element_type=F32)


def dot_nt(a, b):
    return lax.dot_general(a, b, NT, preferred_element_type=F32)


def swap_halves(x):
    return pltpu.roll(x, 64, 1)


def picked_sum(pick, x):
    a, b, c = thirds(x)
    pick = pick.astype(BF)
    return dot_nt(pick, a.astype(BF)) + dot_nt(pick, b.astype(BF)) + dot_nt(pick, c.astype(BF))


def picked_rows(pick, x):
    a, b, c = thirds(x)
    pick = pick.astype(BF)
    return dot(pick, a.astype(BF)) + dot(pick, b.astype(BF)) + dot(pick, c.astype(BF))


def stat_rows(lsum, delta, base, row):
    width = lsum.shape[1]
    rows = iota((16, width), 0)
    tile = jnp.zeros((16, width), F32)
    for k, part in enumerate(thirds(lsum)):
        tile = jnp.where(rows == base + k, part[row : row + 1, :], tile)
    for k, part in enumerate(thirds(delta)):
        tile = jnp.where(rows == 8 + base + k, part[row : row + 1, :], tile)
    return tile


def pack_kernel(index, og, w, q, k, v, o, l, send):
    j = pl.program_id(0)
    g = dot(og[...], w[...]).astype(BF).astype(F32)
    qf, kf, vf = q[...].astype(F32), k[...].astype(F32), v[...].astype(F32)
    delta = picked_sum(
        jnp.where(iota((8, 256), 1) // 64 == iota((8, 256), 0), 1.0, 0.0),
        g * o[...].astype(F32),
    )
    lsum = picked_rows(
        jnp.where(iota((8, 20), 1) == 4 * j + iota((8, 20), 0), 1.0, 0.0), l[...]
    )
    low = iota((TOK, 128), 1) < 64

    def packed(a, b, r):
        t = 128 * (r // 2)
        a, b = a[:, t : t + 128], b[:, t : t + 128]
        if r % 2 == 0:
            return jnp.where(low, a, swap_halves(b)).astype(BF)
        return jnp.where(low, swap_halves(a), b).astype(BF)

    @pl.when(j < 4)
    def whole():
        for r in range(4):
            d = 4 * j + r
            send[d, 0:128, :] = packed(qf, g, r)
            send[d, 128:256, :] = packed(kf, vf, r)
            send[d, 384:400, :] = stat_rows(lsum, delta, 0, r).astype(BF)

    @pl.when(j == 4)
    def shared():
        parity = index[0] % 2
        here = iota((16, 128), 1) // 64 == parity
        for r in range(4):
            qg, kv = packed(qf, g, r), packed(kf, vf, r)
            stat = stat_rows(lsum, delta, 4, r)
            moved = swap_halves(stat)
            for qi in range(2):
                mine = jnp.where(here, jnp.where(parity == qi, stat, moved), 0.0)
                for ki in range(2):
                    d = 4 * r + 2 * qi + ki
                    send[d, 256:320, :] = qg[64 * qi : 64 * qi + 64]
                    send[d, 320:384, :] = kv[64 * ki : 64 * ki + 64]
                    send[d, 384:400, :] = (send[d, 384:400, :].astype(F32) + mine).astype(BF)


def pack(index, og, w, q, k, v, o, l):
    depth = og.shape[1]
    column = pl.BlockSpec((TOK, 256), lambda j, s: (0, j))
    return pl.pallas_call(
        pack_kernel,
        grid_spec=pltpu.PrefetchScalarGridSpec(
            num_scalar_prefetch=1,
            grid=(5,),
            in_specs=[
                pl.BlockSpec((TOK, depth), lambda j, s: (0, 0)),
                pl.BlockSpec((depth, 256), lambda j, s: (0, j)),
                column,
                column,
                column,
                column,
                pl.BlockSpec((20, TOK), lambda j, s: (0, 0)),
            ],
            out_specs=pl.BlockSpec((N, MSG, 128), lambda j, s: (0, 0, 0)),
        ),
        out_shape=jax.ShapeDtypeStruct((N, MSG, 128), BF),
        compiler_params=pltpu.CompilerParams(vmem_limit_bytes=VMEM_LIMIT),
        name="pack",
    )(index, og, w, q, k, v, o, l)


def text_kernel(
    index, wq, wk, wv, wo, wg, lq, lk, lv, lo, lg, l, wqg, wkv, wst, lqg, lkv, lst, buf, lbuf
):
    d = index[0]
    for n, ref in enumerate((wq, wk, wv, wo, wg, lq, lk, lv, lo, lg)):
        buf[n] = jnp.zeros(buf.shape[1:], F32)
        buf[n, 0:TXT, :] = ref[...].astype(F32)
    lbuf[...] = jnp.zeros(lbuf.shape, F32)
    lbuf[:, 0:TXT] = l[...]

    def gather(first, odd, q_rows, k_rows):
        q, k, v = buf[first, q_rows, :], buf[first + 1, k_rows, :], buf[first + 2, k_rows, :]
        o, g = buf[first + 3, q_rows, :], buf[first + 4, q_rows, :]

        def pair(a, b):
            low = iota(a.shape, 1) < 64
            left = jnp.where(odd, swap_halves(a), a)
            right = jnp.where(odd, b, swap_halves(b))
            return jnp.where(low, left, right)

        product = o * g
        mine = (iota(product.shape, 1) >= 64) == odd
        return pair(q, g), pair(k, v), jnp.where(mine, product, 0.0)

    qg, kv, product = gather(0, d % 2 == 1, slice(0, TXT_Q), slice(0, TXT_Q))
    ones = jnp.ones((8, 128), F32)
    pick = jnp.where(iota((8, 20), 1) == d, 1.0, 0.0)
    wqg[...] = qg.astype(BF)
    wkv[...] = kv.astype(BF)
    wst[...] = stat_rows(
        picked_rows(pick, lbuf[:, 0:TXT_Q]), picked_sum(ones, product), 0, 0
    ).astype(BF)

    head = 16 + d // 4
    q_rows = pl.ds(pl.multiple_of(HALF * ((d % 4) // 2), 16), HALF_Q)
    k_rows = pl.ds(pl.multiple_of(HALF * (d % 2), 16), HALF_Q)
    qg, kv, product = gather(5, head % 2 == 1, q_rows, k_rows)
    inside = iota((HALF_Q, 128), 0) < HALF
    pick = jnp.where(iota((8, 20), 1) == head, 1.0, 0.0)
    lqg[...] = jnp.where(inside, qg, 0.0).astype(BF)
    lkv[...] = jnp.where(inside, kv, 0.0).astype(BF)
    lsum = picked_rows(pick, lbuf[...])
    lst[...] = stat_rows(
        jnp.where(
            d % 4 < 2, lsum[:, 0:HALF_Q], pltpu.roll(lsum, lsum.shape[1] - HALF, 1)[:, 0:HALF_Q]
        ),
        picked_sum(ones, jnp.where(inside, product, 0.0)),
        4,
        0,
    ).astype(BF)


def text_prep(index, q, k, v, o, g, l):
    whole = pl.BlockSpec((TXT, 128), lambda i, s: (0, s[0] // 2))
    shared = pl.BlockSpec((TXT, 128), lambda i, s: (0, 8 + s[0] // 8))
    shapes = [
        (TXT_Q, 128), (TXT_Q, 128), (16, TXT_Q), (HALF_Q, 128), (HALF_Q, 128), (16, HALF_Q)
    ]
    return pl.pallas_call(
        text_kernel,
        grid_spec=pltpu.PrefetchScalarGridSpec(
            num_scalar_prefetch=1,
            grid=(1,),
            in_specs=[whole] * 5 + [shared] * 5 + [pl.BlockSpec((20, TXT), lambda i, s: (0, 0))],
            out_specs=[pl.BlockSpec(s, lambda i, s_: (0, 0)) for s in shapes],
            scratch_shapes=[
                pltpu.VMEM((10, HALF + HALF_Q, 128), F32),
                pltpu.VMEM((20, 512), F32),
            ],
        ),
        out_shape=[jax.ShapeDtypeStruct(s, BF) for s in shapes],
        compiler_params=pltpu.CompilerParams(vmem_limit_bytes=VMEM_LIMIT),
        name="text_prep",
    )(index, q, k, v, o, g, q, k, v, o, g, l)


def transposed(x):
    return x.astype(F32).T.astype(BF)


class Head:
    def __init__(self, refs):
        self.ka, self.va, self.b0, self.b1, self.qta, self.gta, self.kt, self.dkv, self.dqt = refs

    @staticmethod
    def scratch(rows):
        return [pltpu.VMEM((rows, 128), BF)] * 4 + [
            pltpu.VMEM((128, rows), BF),
            pltpu.VMEM((128, rows), BF),
            pltpu.VMEM((64, rows), BF),
            pltpu.VMEM((rows, 128), F32),
            pltpu.VMEM((64, rows), F32),
        ]

    def fill(self, at, qg, kv, stat, base):
        rows = qg.shape[0]
        lane = iota((rows, 128), 1)
        low = lane < 64
        zero = jnp.zeros((rows, 128), BF)
        here = pl.ds(at, rows)
        kf = kv.astype(F32)
        off = lane - 64 - base
        ka = jnp.where(low, kf * SCALE, jnp.where((off >= 0) & (off < 3), -1.0, 0.0))
        off = lane - 8 - base
        va = jnp.where(low, jnp.where((off >= 0) & (off < 3), -1.0, 0.0), kf)
        self.ka[here, :] = ka.astype(BF)
        self.va[here, :] = va.astype(BF)
        self.b0[here, :] = jnp.where(low, zero, qg)
        self.b1[here, :] = jnp.where(low, qg, zero)
        qgt = transposed(qg)
        self.qta[0:64, here] = qgt[0:64]
        self.qta[64:80, here] = stat
        self.qta[80:128, here] = jnp.zeros((48, rows), BF)
        self.gta[0:16, here] = stat
        self.gta[16:64, here] = jnp.zeros((48, rows), BF)
        self.gta[64:128, here] = qgt[64:128]
        self.kt[:, here] = transposed(kv)[0:64]

    def zero(self):
        self.dkv[...] = jnp.zeros(self.dkv.shape, F32)
        self.dqt[...] = jnp.zeros(self.dqt.shape, F32)

    def block(self, k0, kb, q0, qb):
        ks, qs = pl.ds(k0, kb), pl.ds(q0, qb)
        p = jnp.exp(dot(self.ka[ks, :], self.qta[:, qs]))
        ds = p * dot(self.va[ks, :], self.gta[:, qs])
        p, ds = p.astype(BF), ds.astype(BF)
        self.dkv[ks, :] += dot(p, self.b0[qs, :]) + dot(ds, self.b1[qs, :])
        self.dqt[:, qs] += dot(self.kt[:, ks], ds)

    def blocks(self, k_all, kb, q_all, qb):
        def q_step(i, _):
            q0 = pl.multiple_of(i * qb, 128)

            def k_step(n, _):
                self.block(pl.multiple_of(n * kb, 128), kb, q0, qb)
                return 0

            return lax.fori_loop(0, k_all // kb, k_step, 0)

        lax.fori_loop(0, q_all // qb, q_step, 0)


def fill_whole(w, recv):
    for s in range(N):
        w.fill(TOK * s, recv[s, 0:128, :], recv[s, 128:256, :], recv[s, 384:400, :], 0)


def fill_shared(h, recv):
    for m in range(N // 2):
        a, b = 2 * m, 2 * m + 1
        stat = jnp.where(iota((16, 128), 1) < 64, recv[a, 384:400, :], recv[b, 384:400, :])
        h.fill(
            128 * m,
            jnp.concatenate([recv[a, 256:320, :], recv[b, 256:320, :]], 0),
            jnp.concatenate([recv[a, 320:384, :], recv[b, 320:384, :]], 0),
            stat,
            4,
        )


def text_pairs_kernel(
    recv, wqg, wkv, wst, lqg, lkv, lst, tout, w_dkv, w_dqt, h_dkv, h_dqt, *refs
):
    w, h = Head(refs[:9]), Head(refs[9:])
    fill_whole(w, recv)
    fill_shared(h, recv)
    for m in range(TXT_Q // 128):
        t = slice(128 * m, 128 * m + 128)
        w.fill(S + 128 * m, wqg[t, :], wkv[t, :], wst[:, t], 0)
    for m in range(HALF_Q // 128):
        t = slice(128 * m, 128 * m + 128)
        h.fill(SH + 128 * m, lqg[t, :], lkv[t, :], lst[:, t], 4)
    w.zero()
    h.zero()

    w.block(S, TXT_K, S, TXT_Q)

    def whole_text(n, _):
        at = pl.multiple_of(n * 1024, 1024)
        w.block(at, 1024, S, TXT_Q)
        w.block(S, TXT_K, at, 1024)
        return 0

    lax.fori_loop(0, S // 1024, whole_text, 0)
    h.block(SH, HALF, SH, HALF_Q)
    h.block(0, SH, SH, HALF_Q)
    h.block(SH, HALF, 0, SH)

    tout[:, 0:WOUT, :] = jnp.zeros((N // 2, WOUT, 128), BF)
    w_dkv[...] = w.dkv[0:S, :]
    w_dqt[...] = w.dqt[:, 0:S]
    h_dkv[...] = h.dkv[0:SH, :]
    h_dqt[...] = h.dqt[:, 0:SH]

    factor = jnp.where(iota((128, 128), 1) < 64, SCALE, 1.0)

    def put(at, value):
        value = value.astype(BF)
        for n in range(N // 2):
            tout[n, WOUT + at : WOUT + at + value.shape[0], :] = value

    for m in range(TXT_Q // 128):
        rows = min(128, TXT_K - 128 * m)
        put(128 * m, w.dkv[S + 128 * m : S + 128 * m + rows, :] * factor[:rows])
        lower = h.dqt[:, SH + 128 * m : SH + 128 * m + 128] if m < 2 else jnp.zeros((64, 128), F32)
        both = jnp.concatenate([w.dqt[:, S + 128 * m : S + 128 * m + 128], lower], 0)
        put(TXT_K + HALF + 128 * m, (both * SCALE).T[:rows])
    put(TXT_K, h.dkv[SH : SH + 128, :] * factor)
    put(TXT_K + 128, h.dkv[SH + 128 : SH + HALF, :] * factor[: HALF - 128])


STATE = [(S, 128), (64, S), (SH, 128), (64, SH)]


def text_pairs(recv, texts):
    full = pl.BlockSpec(memory_space=pltpu.VMEM)
    return pl.pallas_call(
        text_pairs_kernel,
        in_specs=[full] * 7,
        out_specs=[full] * 5,
        out_shape=[jax.ShapeDtypeStruct((N // 2, WOUT + TOUT, 128), BF)]
        + [jax.ShapeDtypeStruct(s, F32) for s in STATE],
        scratch_shapes=Head.scratch(W_ROWS) + Head.scratch(L_ROWS),
        compiler_params=pltpu.CompilerParams(vmem_limit_bytes=VMEM_LIMIT),
        name="text_pairs",
    )(recv, *texts)


def scales():
    return jnp.where(iota((128, 128), 1) < 64, SCALE, 1.0)


def image_pairs_kernel(recv, a, b, c, d, out, *refs):
    w, h = Head(refs[:9]), Head(refs[9:])
    fill_whole(w, recv)
    fill_shared(h, recv)
    for source, target in ((a, w.dkv), (b, w.dqt), (c, h.dkv), (d, h.dqt)):
        target[...] = source[...]
    h.blocks(SH, 1024, SH, 512)
    w.blocks(S, 1024, S, 512)
    factor = scales()
    for s in range(N):
        out[s, 0:128, :] = (w.dkv[128 * s : 128 * s + 128, :] * factor).astype(BF)
        part = w.dqt[:, 128 * s : 128 * s + 128] * SCALE
        both = jnp.concatenate([part, swap_halves(part)], 0).T
        out[s, 128:192, :] = both[0:64].astype(BF)
        out[s, 192:256, :] = (h.dkv[64 * s : 64 * s + 64, :] * factor[:64]).astype(BF)
    for m in range(N // 2):
        part = h.dqt[:, 128 * m : 128 * m + 128] * SCALE
        both = jnp.concatenate([part, pltpu.roll(part, 96, 1)], 0).T
        out[2 * m, 256:288, :] = both[0:32].astype(BF)
        out[2 * m + 1, 256:288, :] = both[64:96].astype(BF)


def image_pairs(recv, state):
    full = pl.BlockSpec(memory_space=pltpu.VMEM)
    return pl.pallas_call(
        image_pairs_kernel,
        in_specs=[full] * 5,
        out_specs=full,
        out_shape=jax.ShapeDtypeStruct((N, OUT, 128), BF),
        scratch_shapes=Head.scratch(S) + Head.scratch(SH),
        compiler_params=pltpu.CompilerParams(vmem_limit_bytes=VMEM_LIMIT),
        name="image_pairs",
    )(recv, *state)


def lane_pair(even, odd):
    low = iota(even.shape, 1) < 64
    return (
        jnp.where(low, even, swap_halves(odd)),
        jnp.where(low, swap_halves(even), odd),
    )


def unpack_kernel(recv, dq, dk, dv):
    def part(d, rows):
        return recv[d, rows, :].astype(F32)

    for t in range(N // 2):
        lanes = slice(128 * t, 128 * t + 128)
        keys, values = lane_pair(part(2 * t, slice(0, 128)), part(2 * t + 1, slice(0, 128)))
        dk[:, lanes] = keys.astype(BF)
        dv[:, lanes] = values.astype(BF)
        first, second = lane_pair(part(2 * t, slice(128, 192)), part(2 * t + 1, slice(128, 192)))
        dq[0:64, lanes] = first.astype(BF)
        dq[64:128, lanes] = second.astype(BF)
    for t in range(2):
        lanes = slice(1024 + 128 * t, 1024 + 128 * t + 128)
        for half in range(2):
            rows = slice(64 * half, 64 * half + 64)
            keys, values = lane_pair(
                *(
                    part(4 * r + half, slice(192, 256)) + part(4 * r + 2 + half, slice(192, 256))
                    for r in (2 * t, 2 * t + 1)
                )
            )
            dk[rows, lanes] = keys.astype(BF)
            dv[rows, lanes] = values.astype(BF)
            first, second = lane_pair(
                *(
                    part(4 * r + 2 * half, slice(256, 288))
                    + part(4 * r + 2 * half + 1, slice(256, 288))
                    for r in (2 * t, 2 * t + 1)
                )
            )
            dq[64 * half : 64 * half + 32, lanes] = first.astype(BF)
            dq[64 * half + 32 : 64 * half + 64, lanes] = second.astype(BF)


def unpack(recv):
    full = pl.BlockSpec(memory_space=pltpu.VMEM)
    return pl.pallas_call(
        unpack_kernel,
        in_specs=[full],
        out_specs=[full] * 3,
        out_shape=[jax.ShapeDtypeStruct((TOK, 1280), BF)] * 3,
        compiler_params=pltpu.CompilerParams(vmem_limit_bytes=VMEM_LIMIT),
        name="unpack",
    )(recv)


def unpack_text_kernel(core, mine, other, dq, dk, dv):
    odd_core = core[0] == 1

    def part(d, rows):
        rows = slice(WOUT + rows.start, WOUT + rows.stop)
        a, b = mine[d // 2, rows, :].astype(F32), other[d // 2, rows, :].astype(F32)
        return jnp.where(odd_core, b, a) if d % 2 == 0 else jnp.where(odd_core, a, b)

    at = TXT_K + HALF
    for t in range(N // 2):
        lanes = slice(128 * t, 128 * t + 128)
        keys, values = lane_pair(part(2 * t, slice(0, TXT_K)), part(2 * t + 1, slice(0, TXT_K)))
        dk[:, lanes] = keys[:TXT].astype(BF)
        dv[:, lanes] = values[:TXT].astype(BF)
        queries, _ = lane_pair(part(2 * t, slice(at, TOUT)), part(2 * t + 1, slice(at, TOUT)))
        dq[:, lanes] = queries[:TXT].astype(BF)
    shared = slice(TXT_K, TXT_K + HALF)
    shared_q = slice(at, at + HALF)
    for t in range(2):
        lanes = slice(1024 + 128 * t, 1024 + 128 * t + 128)
        for half in range(2):
            size = min(HALF, TXT - HALF * half)
            rows = slice(HALF * half, HALF * half + size)
            keys, values = lane_pair(
                *(
                    part(4 * r + half, shared) + part(4 * r + 2 + half, shared)
                    for r in (2 * t, 2 * t + 1)
                )
            )
            dk[rows, lanes] = keys[:size].astype(BF)
            dv[rows, lanes] = values[:size].astype(BF)
            _, queries = lane_pair(
                *(
                    part(4 * r + 2 * half, shared_q) + part(4 * r + 2 * half + 1, shared_q)
                    for r in (2 * t, 2 * t + 1)
                )
            )
            dq[rows, lanes] = queries[:size].astype(BF)


def unpack_text(core, mine, other):
    full = pl.BlockSpec(memory_space=pltpu.VMEM)
    return pl.pallas_call(
        unpack_text_kernel,
        in_specs=[pl.BlockSpec(memory_space=pltpu.SMEM), full, full],
        out_specs=[full] * 3,
        out_shape=[jax.ShapeDtypeStruct((TXT, 1280), BF)] * 3,
        compiler_params=pltpu.CompilerParams(vmem_limit_bytes=VMEM_LIMIT),
        name="unpack_text",
    )(core, mine, other)


def exchange(x, axes):
    return lax.all_to_all(x, axes, 0, 0, tiled=True)


def other_core(x):
    return lax.ppermute(x, "core", [(0, 1), (1, 0)])


def shifted(x, axis, by):
    size = lax.axis_size(axis)
    return lax.ppermute(x, axis, [(i, (i + by) % size) for i in range(size)])


def gathered(x, axis):
    size, me = lax.axis_size(axis), lax.axis_index(axis)
    out = jnp.zeros((size, *x.shape), x.dtype)
    for by in range(size):
        piece = shifted(x, axis, by) if by else x
        out = lax.dynamic_update_index_in_dim(out, piece, (me - by) % size, 0)
    return out


def weight_operands(og, o):
    z, xh, y = (lax.axis_size(a) for a in ("z", "xh", "y"))
    core, me = lax.axis_index("core"), lax.axis_index("y")
    tokens = og.shape[0]
    rows = og.shape[1] // (2 * z * xh)
    padded = -(-rows // (8 * y)) * 8 * y
    blocks = og.T.reshape(z * xh, 2, rows, tokens)
    blocks = jnp.pad(blocks, ((0, 0),) * 2 + ((0, padded - rows), (0, 0)))
    blocks = blocks.reshape(z * xh, 2, y, padded // y, tokens).transpose(1, 2, 0, 3, 4)
    blocks = blocks.reshape(2, y, -1, tokens)
    mine = lax.dynamic_index_in_dim(blocks, core, 0, False)
    theirs = other_core(lax.dynamic_index_in_dim(blocks, 1 - core, 0, False))
    both = jnp.concatenate([mine, theirs], 2)
    left = [lax.dynamic_index_in_dim(both, me, 0, False)]
    right = [o]
    for by in range(1, y):
        left.append(shifted(lax.dynamic_index_in_dim(both, (me + by) % y, 0, False), "y", by))
        right.append(shifted(o, "y", by))
    return left, right, [other_core(x) for x in right]


def weight_kernel(*refs):
    count = (len(refs) - 3) // 3
    left, own, cross = refs[:count], refs[count : 2 * count], refs[2 * count : 3 * count]
    out, scratch = refs[-2:]
    total = None
    for l, a, b in zip(left, own, cross):
        term = dot(l[:, 0:TOK], a[...]) + dot(l[:, TOK:], b[...])
        total = term if total is None else total + term
    each = total.shape[0] // (N // 2)
    for p in range(N // 2):
        for t in range(WOUT // each):
            scratch[p, each * t : each * t + each, :] = total[
                each * p : each * p + each, 128 * t : 128 * t + 128
            ]
        out[p] = scratch[p].astype(BF)


def add_weight_part(message, left, own, cross):
    full = pl.BlockSpec(memory_space=pltpu.VMEM)
    args = [*left, *own, *cross]
    return pl.pallas_call(
        weight_kernel,
        grid=(1,),
        in_specs=[pl.BlockSpec(x.shape, lambda i: (0, 0)) for x in args]
        + [pl.BlockSpec(memory_space=pl.ANY)],
        out_specs=pl.BlockSpec((N // 2, WOUT, 128), lambda i: (0, 0, 0)),
        out_shape=jax.ShapeDtypeStruct(message.shape, BF),
        scratch_shapes=[pltpu.VMEM((N // 2, WOUT, 128), F32)],
        input_output_aliases={len(args): 0},
        compiler_params=pltpu.CompilerParams(vmem_limit_bytes=VMEM_LIMIT),
        name="weight",
    )(*args, message)


def weight_total(parts, rows):
    part = parts.astype(F32).sum(0).astype(BF)
    if lax.axis_size("xl") > 1:
        part = (part.astype(F32) + shifted(part, "xl", 1).astype(F32)).astype(BF)
    part = gathered(part, "y")
    y, height, lanes = part.shape
    part = part.reshape(y, 10, height // 10, lanes).swapaxes(1, 2)
    return part.reshape(-1, 10 * lanes)[:rows].astype(F32)


def shards(
    image_query,
    image_key,
    image_value,
    image_output,
    output_grad,
    image_logsum,
    text_query,
    text_key,
    text_value,
    text_output,
    text_grad,
    text_logsum,
    out_weight,
):
    device = lax.axis_index(SEQ).astype(jnp.int32).reshape(1)
    core = lax.axis_index("core").astype(jnp.int32).reshape(1)
    send = pack(
        device,
        output_grad[0],
        out_weight,
        image_query[0],
        image_key[0],
        image_value[0],
        image_output[0],
        image_logsum[0].T,
    )
    send, upstream, outputs = lax.optimization_barrier((send, output_grad[0], image_output[0]))
    recv = exchange(send, SEQ)
    texts = text_prep(
        device,
        text_query[0],
        text_key[0],
        text_value[0],
        text_output[0],
        text_grad[0],
        text_logsum[0].T,
    )
    upstream, _ = lax.optimization_barrier((upstream, texts[0]))
    operands = weight_operands(upstream, outputs)
    text_out, *state = text_pairs(recv, texts)
    operands, text_out = lax.optimization_barrier((operands, text_out))
    mine = exchange(add_weight_part(text_out, *operands), CHIPS)
    out = image_pairs(recv, state)
    mine, out = lax.optimization_barrier((mine, out))
    text_grads = unpack_text(core, mine, other_core(mine))
    got = exchange(out, SEQ)
    got, text_grads = lax.optimization_barrier((got, text_grads))
    grads = unpack(got)
    weight_grad = weight_total(mine[:, :WOUT], output_grad.shape[2] // N)
    return (*(g[None] for g in grads), *(g[None] for g in text_grads), weight_grad)


def solution(mesh):
    pairs = 2 if mesh.shape["img"] > 1 else 1
    finer = Mesh(
        mesh.devices.reshape(mesh.shape["img"] // pairs, pairs, 4, 2, 2),
        ("y", "xl", "z", "xh", "core"),
    )
    image = P(IMG, SEQ, None)
    text = P(IMG, None, None)
    return jax.shard_map(
        shards,
        mesh=finer,
        in_specs=(image,) * 6 + (text,) * 6 + (P(),),
        out_specs=(image,) * 3 + (text,) * 3 + (P(SEQ, None),),
        check_vma=False,
    )
```

```python
import jax
import jax.numpy as jnp
from jax import lax
from jax.experimental import pallas as pl
from jax.experimental.pallas import tpu as pltpu
from jax.sharding import Mesh
from jax.sharding import PartitionSpec as P

SEQ = ("z", "xh", "core")
CHIPS = ("z", "xh")
IMG = ("y", "xl")
BF = jnp.bfloat16
F32 = jnp.float32
NT = (((1,), (1,)), ((), ()))

N = 16
TOK = 128
S = N * TOK
TXT = 333
TXT_Q = 384
TXT_K = 336
HALF = 176
HALF_Q = 256
SH = N * TOK // 2
W_ROWS = S + TXT_Q
L_ROWS = SH + HALF_Q
SCALE = 0.125
MSG = 400
OUT = 288
W_FOLD = 176
L_FOLD = 96
TOUT = TXT_K + HALF + W_FOLD + L_FOLD
WOUT = 400
VMEM_LIMIT = 56 * 2**20


def iota(shape, dim):
    return lax.broadcasted_iota(jnp.int32, shape, dim)


def thirds(x):
    high = x.astype(BF).astype(F32)
    rest = x - high
    middle = rest.astype(BF).astype(F32)
    return high, middle, rest - middle


def dot(a, b):
    return jnp.dot(a, b, preferred_element_type=F32)


def dot_nt(a, b):
    return lax.dot_general(a, b, NT, preferred_element_type=F32)


def swap_halves(x):
    return pltpu.roll(x, 64, 1)


def picked_sum(pick, x):
    a, b, c = thirds(x)
    pick = pick.astype(BF)
    return dot_nt(pick, a.astype(BF)) + dot_nt(pick, b.astype(BF)) + dot_nt(pick, c.astype(BF))


def picked_rows(pick, x):
    a, b, c = thirds(x)
    pick = pick.astype(BF)
    return dot(pick, a.astype(BF)) + dot(pick, b.astype(BF)) + dot(pick, c.astype(BF))


def stat_rows(lsum, delta, base, row):
    width = lsum.shape[1]
    rows = iota((16, width), 0)
    tile = jnp.zeros((16, width), F32)
    for k, part in enumerate(thirds(lsum)):
        tile = jnp.where(rows == base + k, part[row : row + 1, :], tile)
    for k, part in enumerate(thirds(delta)):
        tile = jnp.where(rows == 8 + base + k, part[row : row + 1, :], tile)
    return tile


def pack_kernel(index, og, w, q, k, v, o, l, send):
    j = pl.program_id(0)
    g = dot(og[...], w[...]).astype(BF).astype(F32)
    qf, kf, vf = q[...].astype(F32), k[...].astype(F32), v[...].astype(F32)
    delta = picked_sum(
        jnp.where(iota((8, 256), 1) // 64 == iota((8, 256), 0), 1.0, 0.0),
        g * o[...].astype(F32),
    )
    lsum = picked_rows(
        jnp.where(iota((8, 20), 1) == 4 * j + iota((8, 20), 0), 1.0, 0.0), l[...]
    )
    low = iota((TOK, 128), 1) < 64

    def packed(a, b, r):
        t = 128 * (r // 2)
        a, b = a[:, t : t + 128], b[:, t : t + 128]
        if r % 2 == 0:
            return jnp.where(low, a, swap_halves(b)).astype(BF)
        return jnp.where(low, swap_halves(a), b).astype(BF)

    @pl.when(j < 4)
    def whole():
        for r in range(4):
            d = 4 * j + r
            send[d, 0:128, :] = packed(qf, g, r)
            send[d, 128:256, :] = packed(kf, vf, r)
            send[d, 384:400, :] = stat_rows(lsum, delta, 0, r).astype(BF)

    @pl.when(j == 4)
    def shared():
        parity = index[0] % 2
        here = iota((16, 128), 1) // 64 == parity
        for r in range(4):
            qg, kv = packed(qf, g, r), packed(kf, vf, r)
            stat = stat_rows(lsum, delta, 4, r)
            moved = swap_halves(stat)
            for qi in range(2):
                mine = jnp.where(here, jnp.where(parity == qi, stat, moved), 0.0)
                for ki in range(2):
                    d = 4 * r + 2 * qi + ki
                    send[d, 256:320, :] = qg[64 * qi : 64 * qi + 64]
                    send[d, 320:384, :] = kv[64 * ki : 64 * ki + 64]
                    send[d, 384:400, :] = (send[d, 384:400, :].astype(F32) + mine).astype(BF)


def pack(index, og, w, q, k, v, o, l):
    depth = og.shape[1]
    column = pl.BlockSpec((TOK, 256), lambda j, s: (0, j))
    return pl.pallas_call(
        pack_kernel,
        grid_spec=pltpu.PrefetchScalarGridSpec(
            num_scalar_prefetch=1,
            grid=(5,),
            in_specs=[
                pl.BlockSpec((TOK, depth), lambda j, s: (0, 0)),
                pl.BlockSpec((depth, 256), lambda j, s: (0, j)),
                column,
                column,
                column,
                column,
                pl.BlockSpec((20, TOK), lambda j, s: (0, 0)),
            ],
            out_specs=pl.BlockSpec((N, MSG, 128), lambda j, s: (0, 0, 0)),
        ),
        out_shape=jax.ShapeDtypeStruct((N, MSG, 128), BF),
        compiler_params=pltpu.CompilerParams(vmem_limit_bytes=VMEM_LIMIT),
        name="pack",
    )(index, og, w, q, k, v, o, l)


def text_kernel(
    index, wq, wk, wv, wo, wg, lq, lk, lv, lo, lg, l, wqg, wkv, wst, lqg, lkv, lst, buf, lbuf
):
    d = index[0]
    for n, ref in enumerate((wq, wk, wv, wo, wg, lq, lk, lv, lo, lg)):
        buf[n] = jnp.zeros(buf.shape[1:], F32)
        buf[n, 0:TXT, :] = ref[...].astype(F32)
    lbuf[...] = jnp.zeros(lbuf.shape, F32)
    lbuf[:, 0:TXT] = l[...]

    def gather(first, odd, q_rows, k_rows):
        q, k, v = buf[first, q_rows, :], buf[first + 1, k_rows, :], buf[first + 2, k_rows, :]
        o, g = buf[first + 3, q_rows, :], buf[first + 4, q_rows, :]

        def pair(a, b):
            low = iota(a.shape, 1) < 64
            left = jnp.where(odd, swap_halves(a), a)
            right = jnp.where(odd, b, swap_halves(b))
            return jnp.where(low, left, right)

        product = o * g
        mine = (iota(product.shape, 1) >= 64) == odd
        return pair(q, g), pair(k, v), jnp.where(mine, product, 0.0)

    qg, kv, product = gather(0, d % 2 == 1, slice(0, TXT_Q), slice(0, TXT_Q))
    ones = jnp.ones((8, 128), F32)
    pick = jnp.where(iota((8, 20), 1) == d, 1.0, 0.0)
    wqg[...] = qg.astype(BF)
    wkv[...] = kv.astype(BF)
    wst[...] = stat_rows(
        picked_rows(pick, lbuf[:, 0:TXT_Q]), picked_sum(ones, product), 0, 0
    ).astype(BF)

    head = 16 + d // 4
    q_rows = pl.ds(pl.multiple_of(HALF * ((d % 4) // 2), 16), HALF_Q)
    k_rows = pl.ds(pl.multiple_of(HALF * (d % 2), 16), HALF_Q)
    qg, kv, product = gather(5, head % 2 == 1, q_rows, k_rows)
    inside = iota((HALF_Q, 128), 0) < HALF
    pick = jnp.where(iota((8, 20), 1) == head, 1.0, 0.0)
    lqg[...] = jnp.where(inside, qg, 0.0).astype(BF)
    lkv[...] = jnp.where(inside, kv, 0.0).astype(BF)
    lsum = picked_rows(pick, lbuf[...])
    lst[...] = stat_rows(
        jnp.where(
            d % 4 < 2, lsum[:, 0:HALF_Q], pltpu.roll(lsum, lsum.shape[1] - HALF, 1)[:, 0:HALF_Q]
        ),
        picked_sum(ones, jnp.where(inside, product, 0.0)),
        4,
        0,
    ).astype(BF)


def text_prep(index, q, k, v, o, g, l):
    whole = pl.BlockSpec((TXT, 128), lambda i, s: (0, s[0] // 2))
    shared = pl.BlockSpec((TXT, 128), lambda i, s: (0, 8 + s[0] // 8))
    shapes = [
        (TXT_Q, 128), (TXT_Q, 128), (16, TXT_Q), (HALF_Q, 128), (HALF_Q, 128), (16, HALF_Q)
    ]
    return pl.pallas_call(
        text_kernel,
        grid_spec=pltpu.PrefetchScalarGridSpec(
            num_scalar_prefetch=1,
            grid=(1,),
            in_specs=[whole] * 5 + [shared] * 5 + [pl.BlockSpec((20, TXT), lambda i, s: (0, 0))],
            out_specs=[pl.BlockSpec(s, lambda i, s_: (0, 0)) for s in shapes],
            scratch_shapes=[
                pltpu.VMEM((10, HALF + HALF_Q, 128), F32),
                pltpu.VMEM((20, 512), F32),
            ],
        ),
        out_shape=[jax.ShapeDtypeStruct(s, BF) for s in shapes],
        compiler_params=pltpu.CompilerParams(vmem_limit_bytes=VMEM_LIMIT),
        name="text_prep",
    )(index, q, k, v, o, g, q, k, v, o, g, l)


def transposed(x):
    return x.astype(F32).T.astype(BF)


class Head:
    def __init__(self, refs):
        self.ka, self.va, self.b0, self.b1, self.qta, self.gta, self.kt, self.dkv, self.dqt = refs

    @staticmethod
    def scratch(rows):
        return [pltpu.VMEM((rows, 128), BF)] * 4 + [
            pltpu.VMEM((128, rows), BF),
            pltpu.VMEM((128, rows), BF),
            pltpu.VMEM((64, rows), BF),
            pltpu.VMEM((rows, 128), F32),
            pltpu.VMEM((64, rows), F32),
        ]

    def fill(self, at, qg, kv, stat, base):
        rows = qg.shape[0]
        lane = iota((rows, 128), 1)
        low = lane < 64
        zero = jnp.zeros((rows, 128), BF)
        here = pl.ds(at, rows)
        kf = kv.astype(F32)
        off = lane - 64 - base
        ka = jnp.where(low, kf * SCALE, jnp.where((off >= 0) & (off < 3), -1.0, 0.0))
        off = lane - 8 - base
        va = jnp.where(low, jnp.where((off >= 0) & (off < 3), -1.0, 0.0), kf)
        self.ka[here, :] = ka.astype(BF)
        self.va[here, :] = va.astype(BF)
        self.b0[here, :] = jnp.where(low, zero, qg)
        self.b1[here, :] = jnp.where(low, qg, zero)
        qgt = transposed(qg)
        self.qta[0:64, here] = qgt[0:64]
        self.qta[64:80, here] = stat
        self.qta[80:128, here] = jnp.zeros((48, rows), BF)
        self.gta[0:16, here] = stat
        self.gta[16:64, here] = jnp.zeros((48, rows), BF)
        self.gta[64:128, here] = qgt[64:128]
        self.kt[:, here] = transposed(kv)[0:64]

    def zero(self):
        self.dkv[...] = jnp.zeros(self.dkv.shape, F32)
        self.dqt[...] = jnp.zeros(self.dqt.shape, F32)

    def block(self, k0, kb, q0, qb):
        ks, qs = pl.ds(k0, kb), pl.ds(q0, qb)
        p = jnp.exp(dot(self.ka[ks, :], self.qta[:, qs]))
        ds = p * dot(self.va[ks, :], self.gta[:, qs])
        p, ds = p.astype(BF), ds.astype(BF)
        self.dkv[ks, :] += dot(p, self.b0[qs, :]) + dot(ds, self.b1[qs, :])
        self.dqt[:, qs] += dot(self.kt[:, ks], ds)

    def blocks(self, k_all, kb, q_all, qb):
        def q_step(i, _):
            q0 = pl.multiple_of(i * qb, 128)

            def k_step(n, _):
                self.block(pl.multiple_of(n * kb, 128), kb, q0, qb)
                return 0

            return lax.fori_loop(0, k_all // kb, k_step, 0)

        lax.fori_loop(0, q_all // qb, q_step, 0)


def fill_whole(w, recv):
    for s in range(N):
        w.fill(TOK * s, recv[s, 0:128, :], recv[s, 128:256, :], recv[s, 384:400, :], 0)


def fill_shared(h, recv):
    for m in range(N // 2):
        a, b = 2 * m, 2 * m + 1
        stat = jnp.where(iota((16, 128), 1) < 64, recv[a, 384:400, :], recv[b, 384:400, :])
        h.fill(
            128 * m,
            jnp.concatenate([recv[a, 256:320, :], recv[b, 256:320, :]], 0),
            jnp.concatenate([recv[a, 320:384, :], recv[b, 320:384, :]], 0),
            stat,
            4,
        )


def text_pairs_kernel(
    recv, wqg, wkv, wst, lqg, lkv, lst, tout, w_dkv, w_dqt, h_dkv, h_dqt, *refs
):
    w, h = Head(refs[:9]), Head(refs[9:])
    fill_whole(w, recv)
    fill_shared(h, recv)
    for m in range(TXT_Q // 128):
        t = slice(128 * m, 128 * m + 128)
        w.fill(S + 128 * m, wqg[t, :], wkv[t, :], wst[:, t], 0)
    for m in range(HALF_Q // 128):
        t = slice(128 * m, 128 * m + 128)
        h.fill(SH + 128 * m, lqg[t, :], lkv[t, :], lst[:, t], 4)
    w.zero()
    h.zero()

    w.block(S, TXT_K, S, TXT_Q)

    def whole_text(n, _):
        at = pl.multiple_of(n * 1024, 1024)
        w.block(at, 1024, S, TXT_Q)
        w.block(S, TXT_K, at, 1024)
        return 0

    lax.fori_loop(0, S // 1024, whole_text, 0)
    h.block(SH, HALF, SH, HALF_Q)
    h.block(0, SH, SH, HALF_Q)
    h.block(SH, HALF, 0, SH)

    tout[:, 0:WOUT, :] = jnp.zeros((N // 2, WOUT, 128), BF)
    w_dkv[...] = w.dkv[0:S, :]
    w_dqt[...] = w.dqt[:, 0:S]
    h_dkv[...] = h.dkv[0:SH, :]
    h_dqt[...] = h.dqt[:, 0:SH]

    factor = jnp.where(iota((128, 128), 1) < 64, SCALE, 1.0)

    def put(at, value):
        value = value.astype(BF)
        for n in range(N // 2):
            tout[n, WOUT + at : WOUT + at + value.shape[0], :] = value

    for m in range(TXT_Q // 128):
        rows = min(128, TXT_K - 128 * m)
        put(128 * m, w.dkv[S + 128 * m : S + 128 * m + rows, :] * factor[:rows])
    put(TXT_K, h.dkv[SH : SH + 128, :] * factor)
    put(TXT_K + 128, h.dkv[SH + 128 : SH + HALF, :] * factor[: HALF - 128])
    for dqt, at, fold in (
        (w.dqt[:, S:], TXT_K + HALF, W_FOLD),
        (h.dqt[:, SH:], TXT_K + HALF + W_FOLD, L_FOLD),
    ):
        part = dqt * SCALE
        both = jnp.concatenate([part, pltpu.roll(part, part.shape[1] - fold, 1)], 0)
        put(at, both[:, 0:256].T[:fold])


STATE = [(S, 128), (64, S), (SH, 128), (64, SH)]


def text_pairs(recv, texts):
    full = pl.BlockSpec(memory_space=pltpu.VMEM)
    return pl.pallas_call(
        text_pairs_kernel,
        in_specs=[full] * 7,
        out_specs=[full] * 5,
        out_shape=[jax.ShapeDtypeStruct((N // 2, WOUT + TOUT, 128), BF)]
        + [jax.ShapeDtypeStruct(s, F32) for s in STATE],
        scratch_shapes=Head.scratch(W_ROWS) + Head.scratch(L_ROWS),
        compiler_params=pltpu.CompilerParams(vmem_limit_bytes=VMEM_LIMIT),
        name="text_pairs",
    )(recv, *texts)


def scales():
    return jnp.where(iota((128, 128), 1) < 64, SCALE, 1.0)


def image_pairs_kernel(recv, a, b, c, d, out, *refs):
    w, h = Head(refs[:9]), Head(refs[9:])
    fill_whole(w, recv)
    fill_shared(h, recv)
    for source, target in ((a, w.dkv), (b, w.dqt), (c, h.dkv), (d, h.dqt)):
        target[...] = source[...]
    h.blocks(SH, 1024, SH, 512)
    w.blocks(S, 1024, S, 512)
    factor = scales()
    for s in range(N):
        out[s, 0:128, :] = (w.dkv[128 * s : 128 * s + 128, :] * factor).astype(BF)
        part = w.dqt[:, 128 * s : 128 * s + 128] * SCALE
        both = jnp.concatenate([part, swap_halves(part)], 0).T
        out[s, 128:192, :] = both[0:64].astype(BF)
        out[s, 192:256, :] = (h.dkv[64 * s : 64 * s + 64, :] * factor[:64]).astype(BF)
    for m in range(N // 2):
        part = h.dqt[:, 128 * m : 128 * m + 128] * SCALE
        both = jnp.concatenate([part, pltpu.roll(part, 96, 1)], 0).T
        out[2 * m, 256:288, :] = both[0:32].astype(BF)
        out[2 * m + 1, 256:288, :] = both[64:96].astype(BF)


def image_pairs(recv, state):
    full = pl.BlockSpec(memory_space=pltpu.VMEM)
    return pl.pallas_call(
        image_pairs_kernel,
        in_specs=[full] * 5,
        out_specs=full,
        out_shape=jax.ShapeDtypeStruct((N, OUT, 128), BF),
        scratch_shapes=Head.scratch(S) + Head.scratch(SH),
        compiler_params=pltpu.CompilerParams(vmem_limit_bytes=VMEM_LIMIT),
        name="image_pairs",
    )(recv, *state)


def lane_pair(even, odd):
    low = iota(even.shape, 1) < 64
    return (
        jnp.where(low, even, swap_halves(odd)),
        jnp.where(low, swap_halves(even), odd),
    )


def unpack_kernel(recv, dq, dk, dv):
    def part(d, rows):
        return recv[d, rows, :].astype(F32)

    for t in range(N // 2):
        lanes = slice(128 * t, 128 * t + 128)
        keys, values = lane_pair(part(2 * t, slice(0, 128)), part(2 * t + 1, slice(0, 128)))
        dk[:, lanes] = keys.astype(BF)
        dv[:, lanes] = values.astype(BF)
        first, second = lane_pair(part(2 * t, slice(128, 192)), part(2 * t + 1, slice(128, 192)))
        dq[0:64, lanes] = first.astype(BF)
        dq[64:128, lanes] = second.astype(BF)
    for t in range(2):
        lanes = slice(1024 + 128 * t, 1024 + 128 * t + 128)
        for half in range(2):
            rows = slice(64 * half, 64 * half + 64)
            keys, values = lane_pair(
                *(
                    part(4 * r + half, slice(192, 256)) + part(4 * r + 2 + half, slice(192, 256))
                    for r in (2 * t, 2 * t + 1)
                )
            )
            dk[rows, lanes] = keys.astype(BF)
            dv[rows, lanes] = values.astype(BF)
            first, second = lane_pair(
                *(
                    part(4 * r + 2 * half, slice(256, 288))
                    + part(4 * r + 2 * half + 1, slice(256, 288))
                    for r in (2 * t, 2 * t + 1)
                )
            )
            dq[64 * half : 64 * half + 32, lanes] = first.astype(BF)
            dq[64 * half + 32 : 64 * half + 64, lanes] = second.astype(BF)


def unpack(recv):
    full = pl.BlockSpec(memory_space=pltpu.VMEM)
    return pl.pallas_call(
        unpack_kernel,
        in_specs=[full],
        out_specs=[full] * 3,
        out_shape=[jax.ShapeDtypeStruct((TOK, 1280), BF)] * 3,
        compiler_params=pltpu.CompilerParams(vmem_limit_bytes=VMEM_LIMIT),
        name="unpack",
    )(recv)


def unpack_text_kernel(core, mine, other, dq, dk, dv):
    odd_core = core[0] == 1

    def part(d, rows):
        rows = slice(WOUT + rows.start, WOUT + rows.stop)
        a, b = mine[d // 2, rows, :].astype(F32), other[d // 2, rows, :].astype(F32)
        return jnp.where(odd_core, b, a) if d % 2 == 0 else jnp.where(odd_core, a, b)

    at = TXT_K + HALF
    whole_q = slice(at, at + W_FOLD)
    for t in range(N // 2):
        lanes = slice(128 * t, 128 * t + 128)
        keys, values = lane_pair(part(2 * t, slice(0, TXT_K)), part(2 * t + 1, slice(0, TXT_K)))
        dk[:, lanes] = keys[:TXT].astype(BF)
        dv[:, lanes] = values[:TXT].astype(BF)
        first, second = lane_pair(part(2 * t, whole_q), part(2 * t + 1, whole_q))
        dq[0:W_FOLD, lanes] = first.astype(BF)
        dq[W_FOLD:TXT, lanes] = second[: TXT - W_FOLD].astype(BF)
    shared = slice(TXT_K, TXT_K + HALF)
    shared_q = slice(at + W_FOLD, at + W_FOLD + L_FOLD)
    for t in range(2):
        lanes = slice(1024 + 128 * t, 1024 + 128 * t + 128)
        for half in range(2):
            begin, end = HALF * half, min(HALF * half + HALF, TXT)
            keys, values = lane_pair(
                *(
                    part(4 * r + half, shared) + part(4 * r + 2 + half, shared)
                    for r in (2 * t, 2 * t + 1)
                )
            )
            dk[begin:end, lanes] = keys[: end - begin].astype(BF)
            dv[begin:end, lanes] = values[: end - begin].astype(BF)
            first, second = lane_pair(
                *(
                    part(4 * r + 2 * half, shared_q) + part(4 * r + 2 * half + 1, shared_q)
                    for r in (2 * t, 2 * t + 1)
                )
            )
            dq[begin : begin + L_FOLD, lanes] = first.astype(BF)
            dq[begin + L_FOLD : end, lanes] = second[: end - begin - L_FOLD].astype(BF)


def unpack_text(core, mine, other):
    full = pl.BlockSpec(memory_space=pltpu.VMEM)
    return pl.pallas_call(
        unpack_text_kernel,
        in_specs=[pl.BlockSpec(memory_space=pltpu.SMEM), full, full],
        out_specs=[full] * 3,
        out_shape=[jax.ShapeDtypeStruct((TXT, 1280), BF)] * 3,
        compiler_params=pltpu.CompilerParams(vmem_limit_bytes=VMEM_LIMIT),
        name="unpack_text",
    )(core, mine, other)


def exchange(x, axes):
    return lax.all_to_all(x, axes, 0, 0, tiled=True)


def other_core(x):
    return lax.ppermute(x, "core", [(0, 1), (1, 0)])


def shifted(x, axis, by):
    size = lax.axis_size(axis)
    return lax.ppermute(x, axis, [(i, (i + by) % size) for i in range(size)])


def gathered(x, axis):
    size, me = lax.axis_size(axis), lax.axis_index(axis)
    out = jnp.zeros((size, *x.shape), x.dtype)
    for by in range(size):
        piece = shifted(x, axis, by) if by else x
        out = lax.dynamic_update_index_in_dim(out, piece, (me - by) % size, 0)
    return out


def weight_operands(og, o):
    chips, y = lax.axis_size(CHIPS), lax.axis_size("y")
    core, me = lax.axis_index("core"), lax.axis_index("y")
    tokens = og.shape[0]
    rows = og.shape[1] // (2 * chips)
    padded = -(-rows // (8 * y)) * 8 * y
    blocks = og.T.reshape(chips, 2, rows, tokens)
    blocks = jnp.pad(blocks, ((0, 0),) * 2 + ((0, padded - rows), (0, 0)))
    blocks = blocks.reshape(chips, 2, y, padded // y, tokens).transpose(1, 2, 0, 3, 4)
    blocks = blocks.reshape(2, y, -1, tokens)
    mine = lax.dynamic_index_in_dim(blocks, core, 0, False)
    theirs = other_core(lax.dynamic_index_in_dim(blocks, 1 - core, 0, False))
    tiles = o.reshape(tokens, -1, 128).swapaxes(0, 1).reshape(-1, 128)
    everyone = jnp.broadcast_to(tiles[None], (y, *tiles.shape))
    both = jnp.concatenate([mine, theirs, everyone], 1)
    pieces = [lax.dynamic_index_in_dim(both, (me + by) % y, 0, False) for by in range(y)]
    return pieces[:1] + [shifted(p, "y", by) for by, p in enumerate(pieces) if by]


def weight_kernel(*refs):
    *operands, out, scratch = refs
    count = len(operands) // 2
    each = WOUT // 10
    rows = each * (N // 2)
    left = jnp.concatenate([x[k * rows : k * rows + rows, :] for x in operands[:count] for k in (0, 1)], 1)
    for t in range(10):
        right = []
        for x, cross in zip(operands[:count], operands[count:]):
            right.append(x[2 * rows + TOK * t : 2 * rows + TOK * t + TOK, :])
            right.append(cross[TOK * t : TOK * t + TOK, :])
        total = dot(left, jnp.concatenate(right, 0))
        for p in range(N // 2):
            scratch[p, each * t : each * t + each, :] = total[each * p : each * p + each]
    for p in range(N // 2):
        out[p] = scratch[p].astype(BF)


def add_weight_part(message, operands, cross):
    args = [*operands, *cross]
    return pl.pallas_call(
        lambda *refs: weight_kernel(*refs[:-3], *refs[-2:]),
        grid=(1,),
        in_specs=[pl.BlockSpec(x.shape, lambda i: (0, 0)) for x in args]
        + [pl.BlockSpec(memory_space=pl.ANY)],
        out_specs=pl.BlockSpec((N // 2, WOUT, 128), lambda i: (0, 0, 0)),
        out_shape=jax.ShapeDtypeStruct(message.shape, BF),
        scratch_shapes=[pltpu.VMEM((N // 2, WOUT, 128), F32)],
        input_output_aliases={len(args): 0},
        compiler_params=pltpu.CompilerParams(vmem_limit_bytes=VMEM_LIMIT),
        name="weight",
    )(*args, message)


def weight_total(parts, rows, after):
    part = parts.astype(F32).sum(0).astype(BF)
    if lax.axis_size("xl") > 1:
        part = (part.astype(F32) + shifted(part, "xl", 1).astype(F32)).astype(BF)
    part, _ = lax.optimization_barrier((part, after))
    part = gathered(part, "y")
    y, height, lanes = part.shape
    part = part.reshape(y, 10, height // 10, lanes).swapaxes(1, 2)
    return part.reshape(-1, 10 * lanes)[:rows].astype(F32)


def shards(
    image_query,
    image_key,
    image_value,
    image_output,
    output_grad,
    image_logsum,
    text_query,
    text_key,
    text_value,
    text_output,
    text_grad,
    text_logsum,
    out_weight,
):
    device = lax.axis_index(SEQ).astype(jnp.int32).reshape(1)
    core = lax.axis_index("core").astype(jnp.int32).reshape(1)
    send = pack(
        device,
        output_grad[0],
        out_weight,
        image_query[0],
        image_key[0],
        image_value[0],
        image_output[0],
        image_logsum[0].T,
    )
    send, upstream = lax.optimization_barrier((send, output_grad[0]))
    recv = exchange(send, SEQ)
    texts = text_prep(
        device,
        text_query[0],
        text_key[0],
        text_value[0],
        text_output[0],
        text_grad[0],
        text_logsum[0].T,
    )
    upstream, outputs, _ = lax.optimization_barrier((upstream, image_output[0], texts[0]))
    operands = weight_operands(upstream, outputs)
    text_out, *state = text_pairs(recv, texts)
    operands, text_out = lax.optimization_barrier((operands, text_out))
    below = operands[0].shape[0] - 10 * TOK
    cross = [other_core(x[below:]) for x in operands]
    mine = exchange(add_weight_part(text_out, operands, cross), CHIPS)
    out = image_pairs(recv, state)
    mine, _ = lax.optimization_barrier((mine, out))
    text_grads = unpack_text(core, mine, other_core(mine))
    got = exchange(out, SEQ)
    got, text_grads = lax.optimization_barrier((got, text_grads))
    grads = unpack(got)
    weight_grad = weight_total(mine[:, :WOUT], output_grad.shape[2] // N, grads)
    return (*(g[None] for g in grads), *(g[None] for g in text_grads), weight_grad)


def solution(mesh):
    pairs = 2 if mesh.shape["img"] > 1 else 1
    finer = Mesh(
        mesh.devices.reshape(mesh.shape["img"] // pairs, pairs, 4, 2, 2),
        ("y", "xl", "z", "xh", "core"),
    )
    image = P(IMG, SEQ, None)
    text = P(IMG, None, None)
    return jax.shard_map(
        shards,
        mesh=finer,
        in_specs=(image,) * 6 + (text,) * 6 + (P(),),
        out_specs=(image,) * 3 + (text,) * 3 + (P(SEQ, None),),
        check_vma=False,
    )
```

```python
import jax
import jax.numpy as jnp
from jax import lax
from jax.experimental import pallas as pl
from jax.experimental.pallas import tpu as pltpu
from jax.sharding import Mesh
from jax.sharding import PartitionSpec as P

SEQ = ("z", "xh", "core")
CHIPS = ("z", "xh")
IMG = ("y", "xl")
BF = jnp.bfloat16
F32 = jnp.float32
NT = (((1,), (1,)), ((), ()))

N = 16
TOK = 128
S = N * TOK
TXT = 333
TXT_Q = 384
TXT_K = 336
HALF = 176
HALF_Q = 256
SH = N * TOK // 2
W_ROWS = S + TXT_Q
L_ROWS = SH + HALF_Q
SCALE = 0.125
MSG = 400
OUT = 288
W_FOLD = 176
L_FOLD = 96
TOUT = TXT_K + HALF + W_FOLD + L_FOLD
WOUT = 400
VMEM_LIMIT = 56 * 2**20


def iota(shape, dim):
    return lax.broadcasted_iota(jnp.int32, shape, dim)


def thirds(x):
    high = x.astype(BF).astype(F32)
    rest = x - high
    middle = rest.astype(BF).astype(F32)
    return high, middle, rest - middle


def dot(a, b):
    return jnp.dot(a, b, preferred_element_type=F32)


def dot_nt(a, b):
    return lax.dot_general(a, b, NT, preferred_element_type=F32)


def swap_halves(x):
    return pltpu.roll(x, 64, 1)


def picked_sum(pick, x):
    a, b, c = thirds(x)
    pick = pick.astype(BF)
    return dot_nt(pick, a.astype(BF)) + dot_nt(pick, b.astype(BF)) + dot_nt(pick, c.astype(BF))


def picked_rows(pick, x):
    a, b, c = thirds(x)
    pick = pick.astype(BF)
    return dot(pick, a.astype(BF)) + dot(pick, b.astype(BF)) + dot(pick, c.astype(BF))


def stat_rows(lsum, delta, base, row):
    width = lsum.shape[1]
    rows = iota((16, width), 0)
    tile = jnp.zeros((16, width), F32)
    for k, part in enumerate(thirds(lsum)):
        tile = jnp.where(rows == base + k, part[row : row + 1, :], tile)
    for k, part in enumerate(thirds(delta)):
        tile = jnp.where(rows == 8 + base + k, part[row : row + 1, :], tile)
    return tile


def pack_kernel(index, og, w, q, k, v, o, l, send):
    j = pl.program_id(0)
    g = dot(og[...], w[...]).astype(BF).astype(F32)
    qf, kf, vf = q[...].astype(F32), k[...].astype(F32), v[...].astype(F32)
    delta = picked_sum(
        jnp.where(iota((8, 256), 1) // 64 == iota((8, 256), 0), 1.0, 0.0),
        g * o[...].astype(F32),
    )
    lsum = picked_rows(
        jnp.where(iota((8, 20), 1) == 4 * j + iota((8, 20), 0), 1.0, 0.0), l[:, 0, :]
    )
    low = iota((TOK, 128), 1) < 64

    def packed(a, b, r):
        t = 128 * (r // 2)
        a, b = a[:, t : t + 128], b[:, t : t + 128]
        if r % 2 == 0:
            return jnp.where(low, a, swap_halves(b)).astype(BF)
        return jnp.where(low, swap_halves(a), b).astype(BF)

    @pl.when(j < 4)
    def whole():
        for r in range(4):
            d = 4 * j + r
            send[d, 0:128, :] = packed(qf, g, r)
            send[d, 128:256, :] = packed(kf, vf, r)
            send[d, 384:400, :] = stat_rows(lsum, delta, 0, r).astype(BF)

    @pl.when(j == 4)
    def shared():
        parity = index[0] % 2
        here = iota((16, 128), 1) // 64 == parity
        for r in range(4):
            qg, kv = packed(qf, g, r), packed(kf, vf, r)
            stat = stat_rows(lsum, delta, 4, r)
            moved = swap_halves(stat)
            for qi in range(2):
                mine = jnp.where(here, jnp.where(parity == qi, stat, moved), 0.0)
                for ki in range(2):
                    d = 4 * r + 2 * qi + ki
                    send[d, 256:320, :] = qg[64 * qi : 64 * qi + 64]
                    send[d, 320:384, :] = kv[64 * ki : 64 * ki + 64]
                    send[d, 384:400, :] = (send[d, 384:400, :].astype(F32) + mine).astype(BF)


def pack(index, og, w, q, k, v, o, l):
    depth = og.shape[1]
    column = pl.BlockSpec((TOK, 256), lambda j, s: (0, j))
    return pl.pallas_call(
        pack_kernel,
        grid_spec=pltpu.PrefetchScalarGridSpec(
            num_scalar_prefetch=1,
            grid=(5,),
            in_specs=[
                pl.BlockSpec((TOK, depth), lambda j, s: (0, 0)),
                pl.BlockSpec((depth, 256), lambda j, s: (0, j)),
                column,
                column,
                column,
                column,
                pl.BlockSpec((20, 1, TOK), lambda j, s: (0, 0, 0)),
            ],
            out_specs=pl.BlockSpec((N, MSG, 128), lambda j, s: (0, 0, 0)),
        ),
        out_shape=jax.ShapeDtypeStruct((N, MSG, 128), BF),
        compiler_params=pltpu.CompilerParams(vmem_limit_bytes=VMEM_LIMIT),
        name="pack",
    )(index, og, w, q, k, v, o, l)


def text_kernel(
    index, wq, wk, wv, wo, wg, lq, lk, lv, lo, lg, l, wqg, wkv, wst, lqg, lkv, lst, buf, lbuf
):
    d = index[0]
    for n, ref in enumerate((wq, wk, wv, wo, wg, lq, lk, lv, lo, lg)):
        buf[n] = jnp.zeros(buf.shape[1:], F32)
        buf[n, 0:TXT, :] = ref[...].astype(F32)
    lbuf[...] = jnp.zeros(lbuf.shape, F32)
    lbuf[:, 0:TXT] = l[:, 0, :]

    def gather(first, odd, q_rows, k_rows):
        q, k, v = buf[first, q_rows, :], buf[first + 1, k_rows, :], buf[first + 2, k_rows, :]
        o, g = buf[first + 3, q_rows, :], buf[first + 4, q_rows, :]

        def pair(a, b):
            low = iota(a.shape, 1) < 64
            left = jnp.where(odd, swap_halves(a), a)
            right = jnp.where(odd, b, swap_halves(b))
            return jnp.where(low, left, right)

        product = o * g
        mine = (iota(product.shape, 1) >= 64) == odd
        return pair(q, g), pair(k, v), jnp.where(mine, product, 0.0)

    qg, kv, product = gather(0, d % 2 == 1, slice(0, TXT_Q), slice(0, TXT_Q))
    ones = jnp.ones((8, 128), F32)
    pick = jnp.where(iota((8, 20), 1) == d, 1.0, 0.0)
    wqg[...] = qg.astype(BF)
    wkv[...] = kv.astype(BF)
    wst[...] = stat_rows(
        picked_rows(pick, lbuf[:, 0:TXT_Q]), picked_sum(ones, product), 0, 0
    ).astype(BF)

    head = 16 + d // 4
    q_rows = pl.ds(pl.multiple_of(HALF * ((d % 4) // 2), 16), HALF_Q)
    k_rows = pl.ds(pl.multiple_of(HALF * (d % 2), 16), HALF_Q)
    qg, kv, product = gather(5, head % 2 == 1, q_rows, k_rows)
    inside = iota((HALF_Q, 128), 0) < HALF
    pick = jnp.where(iota((8, 20), 1) == head, 1.0, 0.0)
    lqg[...] = jnp.where(inside, qg, 0.0).astype(BF)
    lkv[...] = jnp.where(inside, kv, 0.0).astype(BF)
    lsum = picked_rows(pick, lbuf[...])
    lst[...] = stat_rows(
        jnp.where(
            d % 4 < 2, lsum[:, 0:HALF_Q], pltpu.roll(lsum, lsum.shape[1] - HALF, 1)[:, 0:HALF_Q]
        ),
        picked_sum(ones, jnp.where(inside, product, 0.0)),
        4,
        0,
    ).astype(BF)


def text_prep(index, q, k, v, o, g, l):
    whole = pl.BlockSpec((TXT, 128), lambda i, s: (0, s[0] // 2))
    shared = pl.BlockSpec((TXT, 128), lambda i, s: (0, 8 + s[0] // 8))
    shapes = [
        (TXT_Q, 128), (TXT_Q, 128), (16, TXT_Q), (HALF_Q, 128), (HALF_Q, 128), (16, HALF_Q)
    ]
    return pl.pallas_call(
        text_kernel,
        grid_spec=pltpu.PrefetchScalarGridSpec(
            num_scalar_prefetch=1,
            grid=(1,),
            in_specs=[whole] * 5 + [shared] * 5 + [pl.BlockSpec((20, 1, TXT), lambda i, s: (0, 0, 0))],
            out_specs=[pl.BlockSpec(s, lambda i, s_: (0, 0)) for s in shapes],
            scratch_shapes=[
                pltpu.VMEM((10, HALF + HALF_Q, 128), F32),
                pltpu.VMEM((20, 512), F32),
            ],
        ),
        out_shape=[jax.ShapeDtypeStruct(s, BF) for s in shapes],
        compiler_params=pltpu.CompilerParams(vmem_limit_bytes=VMEM_LIMIT),
        name="text_prep",
    )(index, q, k, v, o, g, q, k, v, o, g, l)


def transposed(x):
    return x.astype(F32).T.astype(BF)


class Head:
    def __init__(self, refs):
        self.ka, self.va, self.b0, self.b1, self.qta, self.gta, self.kt, self.dkv, self.dqt = refs

    @staticmethod
    def scratch(rows):
        return [pltpu.VMEM((rows, 128), BF)] * 4 + [
            pltpu.VMEM((128, rows), BF),
            pltpu.VMEM((128, rows), BF),
            pltpu.VMEM((64, rows), BF),
            pltpu.VMEM((rows, 128), F32),
            pltpu.VMEM((64, rows), F32),
        ]

    def fill(self, at, qg, kv, stat, base):
        rows = qg.shape[0]
        lane = iota((rows, 128), 1)
        low = lane < 64
        zero = jnp.zeros((rows, 128), BF)
        here = pl.ds(at, rows)
        kf = kv.astype(F32)
        off = lane - 64 - base
        ka = jnp.where(low, kf * SCALE, jnp.where((off >= 0) & (off < 3), -1.0, 0.0))
        off = lane - 8 - base
        va = jnp.where(low, jnp.where((off >= 0) & (off < 3), -1.0, 0.0), kf)
        self.ka[here, :] = ka.astype(BF)
        self.va[here, :] = va.astype(BF)
        self.b0[here, :] = jnp.where(low, zero, qg)
        self.b1[here, :] = jnp.where(low, qg, zero)
        qgt = transposed(qg)
        self.qta[0:64, here] = qgt[0:64]
        self.qta[64:80, here] = stat
        self.qta[80:128, here] = jnp.zeros((48, rows), BF)
        self.gta[0:16, here] = stat
        self.gta[16:64, here] = jnp.zeros((48, rows), BF)
        self.gta[64:128, here] = qgt[64:128]
        self.kt[:, here] = transposed(kv)[0:64]

    def zero(self):
        self.dkv[...] = jnp.zeros(self.dkv.shape, F32)
        self.dqt[...] = jnp.zeros(self.dqt.shape, F32)

    def block(self, k0, kb, q0, qb):
        ks, qs = pl.ds(k0, kb), pl.ds(q0, qb)
        p = jnp.exp(dot(self.ka[ks, :], self.qta[:, qs]))
        ds = p * dot(self.va[ks, :], self.gta[:, qs])
        p, ds = p.astype(BF), ds.astype(BF)
        self.dkv[ks, :] += dot(p, self.b0[qs, :]) + dot(ds, self.b1[qs, :])
        self.dqt[:, qs] += dot(self.kt[:, ks], ds)

    def blocks(self, k_all, kb, q_all, qb):
        def q_step(i, _):
            q0 = pl.multiple_of(i * qb, 128)

            def k_step(n, _):
                self.block(pl.multiple_of(n * kb, 128), kb, q0, qb)
                return 0

            return lax.fori_loop(0, k_all // kb, k_step, 0)

        lax.fori_loop(0, q_all // qb, q_step, 0)


def fill_whole(w, recv):
    for s in range(N):
        w.fill(TOK * s, recv[s, 0:128, :], recv[s, 128:256, :], recv[s, 384:400, :], 0)


def fill_shared(h, recv):
    for m in range(N // 2):
        a, b = 2 * m, 2 * m + 1
        stat = jnp.where(iota((16, 128), 1) < 64, recv[a, 384:400, :], recv[b, 384:400, :])
        h.fill(
            128 * m,
            jnp.concatenate([recv[a, 256:320, :], recv[b, 256:320, :]], 0),
            jnp.concatenate([recv[a, 320:384, :], recv[b, 320:384, :]], 0),
            stat,
            4,
        )


def text_pairs_kernel(
    recv, wqg, wkv, wst, lqg, lkv, lst, tout, w_dkv, w_dqt, h_dkv, h_dqt, *refs
):
    w, h = Head(refs[:9]), Head(refs[9:])
    fill_whole(w, recv)
    fill_shared(h, recv)
    for m in range(TXT_Q // 128):
        t = slice(128 * m, 128 * m + 128)
        w.fill(S + 128 * m, wqg[t, :], wkv[t, :], wst[:, t], 0)
    for m in range(HALF_Q // 128):
        t = slice(128 * m, 128 * m + 128)
        h.fill(SH + 128 * m, lqg[t, :], lkv[t, :], lst[:, t], 4)
    w.zero()
    h.zero()

    w.block(S, TXT_K, S, TXT_Q)

    def whole_text(n, _):
        at = pl.multiple_of(n * 1024, 1024)
        w.block(at, 1024, S, TXT_Q)
        w.block(S, TXT_K, at, 1024)
        return 0

    lax.fori_loop(0, S // 1024, whole_text, 0)
    h.block(SH, HALF, SH, HALF_Q)
    h.block(0, SH, SH, HALF_Q)
    h.block(SH, HALF, 0, SH)

    tout[:, 0:WOUT, :] = jnp.zeros((N // 2, WOUT, 128), BF)
    w_dkv[...] = w.dkv[0:S, :]
    w_dqt[...] = w.dqt[:, 0:S]
    h_dkv[...] = h.dkv[0:SH, :]
    h_dqt[...] = h.dqt[:, 0:SH]

    factor = jnp.where(iota((128, 128), 1) < 64, SCALE, 1.0)

    def put(at, value):
        value = value.astype(BF)
        for n in range(N // 2):
            tout[n, WOUT + at : WOUT + at + value.shape[0], :] = value

    for m in range(TXT_Q // 128):
        rows = min(128, TXT_K - 128 * m)
        put(128 * m, w.dkv[S + 128 * m : S + 128 * m + rows, :] * factor[:rows])
    put(TXT_K, h.dkv[SH : SH + 128, :] * factor)
    put(TXT_K + 128, h.dkv[SH + 128 : SH + HALF, :] * factor[: HALF - 128])
    for dqt, at, fold in (
        (w.dqt[:, S:], TXT_K + HALF, W_FOLD),
        (h.dqt[:, SH:], TXT_K + HALF + W_FOLD, L_FOLD),
    ):
        part = dqt * SCALE
        both = jnp.concatenate([part, pltpu.roll(part, part.shape[1] - fold, 1)], 0)
        put(at, both[:, 0:256].T[:fold])


STATE = [(S, 128), (64, S), (SH, 128), (64, SH)]


def text_pairs(recv, texts):
    full = pl.BlockSpec(memory_space=pltpu.VMEM)
    return pl.pallas_call(
        text_pairs_kernel,
        in_specs=[full] * 7,
        out_specs=[full] * 5,
        out_shape=[jax.ShapeDtypeStruct((N // 2, WOUT + TOUT, 128), BF)]
        + [jax.ShapeDtypeStruct(s, F32) for s in STATE],
        scratch_shapes=Head.scratch(W_ROWS) + Head.scratch(L_ROWS),
        compiler_params=pltpu.CompilerParams(vmem_limit_bytes=VMEM_LIMIT),
        name="text_pairs",
    )(recv, *texts)


def scales():
    return jnp.where(iota((128, 128), 1) < 64, SCALE, 1.0)


def image_pairs_kernel(recv, a, b, c, d, out, *refs):
    w, h = Head(refs[:9]), Head(refs[9:])
    fill_whole(w, recv)
    fill_shared(h, recv)
    for source, target in ((a, w.dkv), (b, w.dqt), (c, h.dkv), (d, h.dqt)):
        target[...] = source[...]
    h.blocks(SH, 1024, SH, 512)
    w.blocks(S, 1024, S, 512)
    factor = scales()
    for s in range(N):
        out[s, 0:128, :] = (w.dkv[128 * s : 128 * s + 128, :] * factor).astype(BF)
        part = w.dqt[:, 128 * s : 128 * s + 128] * SCALE
        both = jnp.concatenate([part, swap_halves(part)], 0).T
        out[s, 128:192, :] = both[0:64].astype(BF)
        out[s, 192:256, :] = (h.dkv[64 * s : 64 * s + 64, :] * factor[:64]).astype(BF)
    for m in range(N // 2):
        part = h.dqt[:, 128 * m : 128 * m + 128] * SCALE
        both = jnp.concatenate([part, pltpu.roll(part, 96, 1)], 0).T
        out[2 * m, 256:288, :] = both[0:32].astype(BF)
        out[2 * m + 1, 256:288, :] = both[64:96].astype(BF)


def image_pairs(recv, state):
    full = pl.BlockSpec(memory_space=pltpu.VMEM)
    return pl.pallas_call(
        image_pairs_kernel,
        in_specs=[full] * 5,
        out_specs=full,
        out_shape=jax.ShapeDtypeStruct((N, OUT, 128), BF),
        scratch_shapes=Head.scratch(S) + Head.scratch(SH),
        compiler_params=pltpu.CompilerParams(vmem_limit_bytes=VMEM_LIMIT),
        name="image_pairs",
    )(recv, *state)


def lane_pair(even, odd):
    low = iota(even.shape, 1) < 64
    return (
        jnp.where(low, even, swap_halves(odd)),
        jnp.where(low, swap_halves(even), odd),
    )


def unpack_kernel(recv, dq, dk, dv):
    def part(d, rows):
        return recv[d, rows, :].astype(F32)

    for t in range(N // 2):
        lanes = slice(128 * t, 128 * t + 128)
        keys, values = lane_pair(part(2 * t, slice(0, 128)), part(2 * t + 1, slice(0, 128)))
        dk[:, lanes] = keys.astype(BF)
        dv[:, lanes] = values.astype(BF)
        first, second = lane_pair(part(2 * t, slice(128, 192)), part(2 * t + 1, slice(128, 192)))
        dq[0:64, lanes] = first.astype(BF)
        dq[64:128, lanes] = second.astype(BF)
    for t in range(2):
        lanes = slice(1024 + 128 * t, 1024 + 128 * t + 128)
        for half in range(2):
            rows = slice(64 * half, 64 * half + 64)
            keys, values = lane_pair(
                *(
                    part(4 * r + half, slice(192, 256)) + part(4 * r + 2 + half, slice(192, 256))
                    for r in (2 * t, 2 * t + 1)
                )
            )
            dk[rows, lanes] = keys.astype(BF)
            dv[rows, lanes] = values.astype(BF)
            first, second = lane_pair(
                *(
                    part(4 * r + 2 * half, slice(256, 288))
                    + part(4 * r + 2 * half + 1, slice(256, 288))
                    for r in (2 * t, 2 * t + 1)
                )
            )
            dq[64 * half : 64 * half + 32, lanes] = first.astype(BF)
            dq[64 * half + 32 : 64 * half + 64, lanes] = second.astype(BF)


def unpack(recv):
    full = pl.BlockSpec(memory_space=pltpu.VMEM)
    return pl.pallas_call(
        unpack_kernel,
        in_specs=[full],
        out_specs=[full] * 3,
        out_shape=[jax.ShapeDtypeStruct((TOK, 1280), BF)] * 3,
        compiler_params=pltpu.CompilerParams(vmem_limit_bytes=VMEM_LIMIT),
        name="unpack",
    )(recv)


def unpack_text_kernel(core, mine, other, dq, dk, dv):
    odd_core = core[0] == 1

    def part(d, rows):
        rows = slice(WOUT + rows.start, WOUT + rows.stop)
        a, b = mine[d // 2, rows, :].astype(F32), other[d // 2, rows, :].astype(F32)
        return jnp.where(odd_core, b, a) if d % 2 == 0 else jnp.where(odd_core, a, b)

    at = TXT_K + HALF
    whole_q = slice(at, at + W_FOLD)
    for t in range(N // 2):
        lanes = slice(128 * t, 128 * t + 128)
        keys, values = lane_pair(part(2 * t, slice(0, TXT_K)), part(2 * t + 1, slice(0, TXT_K)))
        dk[:, lanes] = keys[:TXT].astype(BF)
        dv[:, lanes] = values[:TXT].astype(BF)
        first, second = lane_pair(part(2 * t, whole_q), part(2 * t + 1, whole_q))
        dq[0:W_FOLD, lanes] = first.astype(BF)
        dq[W_FOLD:TXT, lanes] = second[: TXT - W_FOLD].astype(BF)
    shared = slice(TXT_K, TXT_K + HALF)
    shared_q = slice(at + W_FOLD, at + W_FOLD + L_FOLD)
    for t in range(2):
        lanes = slice(1024 + 128 * t, 1024 + 128 * t + 128)
        for half in range(2):
            begin, end = HALF * half, min(HALF * half + HALF, TXT)
            keys, values = lane_pair(
                *(
                    part(4 * r + half, shared) + part(4 * r + 2 + half, shared)
                    for r in (2 * t, 2 * t + 1)
                )
            )
            dk[begin:end, lanes] = keys[: end - begin].astype(BF)
            dv[begin:end, lanes] = values[: end - begin].astype(BF)
            first, second = lane_pair(
                *(
                    part(4 * r + 2 * half, shared_q) + part(4 * r + 2 * half + 1, shared_q)
                    for r in (2 * t, 2 * t + 1)
                )
            )
            dq[begin : begin + L_FOLD, lanes] = first.astype(BF)
            dq[begin + L_FOLD : end, lanes] = second[: end - begin - L_FOLD].astype(BF)


def unpack_text(core, mine, other):
    full = pl.BlockSpec(memory_space=pltpu.VMEM)
    return pl.pallas_call(
        unpack_text_kernel,
        in_specs=[pl.BlockSpec(memory_space=pltpu.SMEM), full, full],
        out_specs=[full] * 3,
        out_shape=[jax.ShapeDtypeStruct((TXT, 1280), BF)] * 3,
        compiler_params=pltpu.CompilerParams(vmem_limit_bytes=VMEM_LIMIT),
        name="unpack_text",
    )(core, mine, other)


def exchange(x, axes):
    return lax.all_to_all(x, axes, 0, 0, tiled=True)


def other_core(x):
    return lax.ppermute(x, "core", [(0, 1), (1, 0)])


def shifted(x, axis, by):
    size = lax.axis_size(axis)
    return lax.ppermute(x, axis, [(i, (i + by) % size) for i in range(size)])


def gathered(x, axis):
    size, me = lax.axis_size(axis), lax.axis_index(axis)
    out = jnp.zeros((size, *x.shape), x.dtype)
    for by in range(size):
        piece = shifted(x, axis, by) if by else x
        out = lax.dynamic_update_index_in_dim(out, piece, (me - by) % size, 0)
    return out


def weight_operands(og, o):
    chips, y = lax.axis_size(CHIPS), lax.axis_size("y")
    core, me = lax.axis_index("core"), lax.axis_index("y")
    tokens = og.shape[0]
    rows = og.shape[1] // (2 * chips)
    padded = -(-rows // (8 * y)) * 8 * y
    blocks = og.T.reshape(chips, 2, rows, tokens)
    blocks = jnp.pad(blocks, ((0, 0),) * 2 + ((0, padded - rows), (0, 0)))
    blocks = blocks.reshape(chips, 2, y, padded // y, tokens).transpose(1, 2, 0, 3, 4)
    blocks = blocks.reshape(2, y, -1, tokens)
    mine = lax.dynamic_index_in_dim(blocks, core, 0, False)
    theirs = other_core(lax.dynamic_index_in_dim(blocks, 1 - core, 0, False))
    both = jnp.concatenate([mine, theirs], 2)
    pieces = [lax.dynamic_index_in_dim(both, (me + by) % y, 0, False) for by in range(y)]
    left, right = pieces[:1], [o]
    for by in range(1, y):
        right.append(shifted(o, "y", by))
        left.append(shifted(pieces[by], "y", by))
    return left, right


def weight_kernel(*refs):
    *operands, _, out, scratch = refs
    count = len(operands) // 3
    total = None
    for left, own, cross in zip(*(operands[k * count : k * count + count] for k in range(3))):
        term = dot(left[...], jnp.concatenate([own[...], cross[...]], 0))
        total = term if total is None else total + term
    each = WOUT // 10
    for p in range(N // 2):
        for t in range(10):
            scratch[p, each * t : each * t + each, :] = total[
                each * p : each * p + each, 128 * t : 128 * t + 128
            ]
        out[p] = scratch[p].astype(BF)


def add_weight_part(message, left, own, cross):
    args = [*left, *own, *cross]
    return pl.pallas_call(
        weight_kernel,
        grid=(1,),
        in_specs=[pl.BlockSpec(x.shape, lambda i: (0, 0)) for x in args]
        + [pl.BlockSpec(memory_space=pl.ANY)],
        out_specs=pl.BlockSpec((N // 2, WOUT, 128), lambda i: (0, 0, 0)),
        out_shape=jax.ShapeDtypeStruct(message.shape, BF),
        scratch_shapes=[pltpu.VMEM((N // 2, WOUT, 128), F32)],
        input_output_aliases={len(args): 0},
        compiler_params=pltpu.CompilerParams(vmem_limit_bytes=VMEM_LIMIT),
        name="weight",
    )(*args, message)


def weight_total(parts, rows, after):
    part = gathered(parts.astype(F32).sum(0).astype(BF), "y")
    if lax.axis_size("xl") > 1:
        other, _ = lax.optimization_barrier((shifted(part, "xl", 1), after))
        part = part.astype(F32) + other.astype(F32)
    y, height, lanes = part.shape
    part = part.reshape(y, 10, height // 10, lanes).swapaxes(1, 2)
    return part.reshape(-1, 10 * lanes)[:rows].astype(F32)


def shards(
    image_query,
    image_key,
    image_value,
    image_output,
    output_grad,
    image_logsum,
    text_query,
    text_key,
    text_value,
    text_output,
    text_grad,
    text_logsum,
    out_weight,
):
    device = lax.axis_index(SEQ).astype(jnp.int32).reshape(1)
    core = lax.axis_index("core").astype(jnp.int32).reshape(1)
    send = pack(
        device,
        output_grad[0],
        out_weight,
        image_query[0],
        image_key[0],
        image_value[0],
        image_output[0],
        image_logsum.transpose(2, 0, 1),
    )
    send, upstream = lax.optimization_barrier((send, output_grad[0]))
    recv = exchange(send, SEQ)
    texts = text_prep(
        device,
        text_query[0],
        text_key[0],
        text_value[0],
        text_output[0],
        text_grad[0],
        text_logsum.transpose(2, 0, 1),
    )
    upstream, outputs, _ = lax.optimization_barrier((upstream, image_output[0], texts[0]))
    left, own = weight_operands(upstream, outputs)
    text_out, *state = text_pairs(recv, texts)
    cross = [other_core(outputs)]
    left, own, text_out = lax.optimization_barrier((left, own, text_out))
    cross += [other_core(x) for x in own[1:]]
    mine = exchange(add_weight_part(text_out, left, own, cross), CHIPS)
    out = image_pairs(recv, state)
    mine, _ = lax.optimization_barrier((mine, out))
    text_grads = unpack_text(core, mine, other_core(mine))
    got = exchange(out, SEQ)
    got, text_grads = lax.optimization_barrier((got, text_grads))
    grads = unpack(got)
    weight_grad = weight_total(mine[:, :WOUT], output_grad.shape[2] // N, grads)
    return (*(g[None] for g in grads), *(g[None] for g in text_grads), weight_grad)


def solution(mesh):
    pairs = 2 if mesh.shape["img"] > 1 else 1
    finer = Mesh(
        mesh.devices.reshape(mesh.shape["img"] // pairs, pairs, 4, 2, 2),
        ("y", "xl", "z", "xh", "core"),
    )
    image = P(IMG, SEQ, None)
    text = P(IMG, None, None)
    return jax.shard_map(
        shards,
        mesh=finer,
        in_specs=(image,) * 6 + (text,) * 6 + (P(),),
        out_specs=(image,) * 3 + (text,) * 3 + (P(SEQ, None),),
        check_vma=False,
    )
```

```python
import jax
import jax.numpy as jnp
from jax import lax
from jax.experimental import pallas as pl
from jax.experimental.pallas import tpu as pltpu
from jax.sharding import Mesh
from jax.sharding import PartitionSpec as P

SEQ = ("z", "xh", "core")
CHIPS = ("z", "xh")
IMG = ("y", "xl")
BF = jnp.bfloat16
F32 = jnp.float32
NT = (((1,), (1,)), ((), ()))

N = 16
TOK = 128
S = N * TOK
TXT = 333
TXT_Q = 384
TXT_K = 336
HALF = 176
HALF_Q = 256
SH = N * TOK // 2
W_ROWS = S + TXT_Q
L_ROWS = SH + HALF_Q
SCALE = 0.125
MSG = 400
OUT = 288
W_FOLD = 176
L_FOLD = 96
TOUT = TXT_K + HALF + W_FOLD + L_FOLD
WOUT = 400
VMEM_LIMIT = 56 * 2**20


def iota(shape, dim):
    return lax.broadcasted_iota(jnp.int32, shape, dim)


def thirds(x):
    high = x.astype(BF).astype(F32)
    rest = x - high
    middle = rest.astype(BF).astype(F32)
    return high, middle, rest - middle


def dot(a, b):
    return jnp.dot(a, b, preferred_element_type=F32)


def dot_nt(a, b):
    return lax.dot_general(a, b, NT, preferred_element_type=F32)


def swap_halves(x):
    return pltpu.roll(x, 64, 1)


def picked_sum(pick, x):
    a, b, c = thirds(x)
    pick = pick.astype(BF)
    return dot_nt(pick, a.astype(BF)) + dot_nt(pick, b.astype(BF)) + dot_nt(pick, c.astype(BF))


def picked_rows(pick, x):
    a, b, c = thirds(x)
    pick = pick.astype(BF)
    return dot(pick, a.astype(BF)) + dot(pick, b.astype(BF)) + dot(pick, c.astype(BF))


def stat_rows(lsum, delta, base, row):
    width = lsum.shape[1]
    rows = iota((16, width), 0)
    tile = jnp.zeros((16, width), F32)
    for k, part in enumerate(thirds(lsum)):
        tile = jnp.where(rows == base + k, part[row : row + 1, :], tile)
    for k, part in enumerate(thirds(delta)):
        tile = jnp.where(rows == 8 + base + k, part[row : row + 1, :], tile)
    return tile


def pack_kernel(
    index, og_hbm, w_hbm, q_hbm, k_hbm, v_hbm, o_hbm, l, send, og, w, q, k, v, o, acc, sems
):
    depth = w.shape[0]
    chunk = 640
    parts = [(at, min(chunk, depth - at)) for at in range(0, depth, chunk)]
    copies = [
        pltpu.make_async_copy(source, target, sems.at[n])
        for n, (source, target) in enumerate(
            [(k_hbm, k), (v_hbm, v), (og_hbm, og)]
            + [(w_hbm.at[pl.ds(at, size)], w.at[pl.ds(at, size)]) for at, size in parts]
            + [(q_hbm, q), (o_hbm, o)]
        )
    ]
    for copy in copies:
        copy.start()
    low = iota((TOK, 128), 1) < 64

    def packed(a, b, head):
        lanes = slice(128 * (head // 2), 128 * (head // 2) + 128)
        a, b = a[:, lanes].astype(F32), b[:, lanes].astype(F32)
        if head % 2 == 0:
            return jnp.where(low, a, swap_halves(b)).astype(BF)
        return jnp.where(low, swap_halves(a), b).astype(BF)

    copies[0].wait()
    copies[1].wait()
    for d in range(N):
        send[d, 128:256, :] = packed(k, v, d)
    for r in range(4):
        kv = packed(k, v, 16 + r)
        for qi in range(2):
            for ki in range(2):
                send[4 * r + 2 * qi + ki, 320:384, :] = kv[64 * ki : 64 * ki + 64]

    copies[2].wait()
    for n, (at, size) in enumerate(parts):
        copies[3 + n].wait()
        term = dot(og[:, at : at + size], w[at : at + size, :])
        acc[...] = term if n == 0 else acc[...] + term
    copies[-2].wait()
    copies[-1].wait()
    acc[...] = acc[...].astype(BF).astype(F32)
    delta = picked_sum(
        jnp.where(iota((24, 1280), 1) // 64 == iota((24, 1280), 0), 1.0, 0.0),
        acc[...] * o[...].astype(F32),
    )
    lsum = l[:, 0, :]
    here = iota((16, 128), 1) // 64 == index[0] % 2
    for r in range(4):
        qg = packed(q, acc, 16 + r)
        stat = stat_rows(lsum, delta, 4, 16 + r)
        moved = swap_halves(stat)
        for qi in range(2):
            mine = jnp.where(here, jnp.where(index[0] % 2 == qi, stat, moved), 0.0)
            for ki in range(2):
                d = 4 * r + 2 * qi + ki
                send[d, 0:128, :] = packed(q, acc, d)
                send[d, 256:320, :] = qg[64 * qi : 64 * qi + 64]
                send[d, 384:400, :] = (stat_rows(lsum, delta, 0, d) + mine).astype(BF)


def pack(index, og, w, q, k, v, o, l):
    anywhere = pl.BlockSpec(memory_space=pl.ANY)
    full = pl.BlockSpec(memory_space=pltpu.VMEM)
    arrays = [og, w, q, k, v, o]
    return pl.pallas_call(
        pack_kernel,
        in_specs=[pl.BlockSpec(memory_space=pltpu.SMEM)] + [anywhere] * 6 + [full],
        out_specs=full,
        out_shape=jax.ShapeDtypeStruct((N, MSG, 128), BF),
        scratch_shapes=[pltpu.VMEM(x.shape, BF) for x in arrays]
        + [pltpu.VMEM(q.shape, F32), pltpu.SemaphoreType.DMA((5 + -(-w.shape[0] // 640),))],
        compiler_params=pltpu.CompilerParams(vmem_limit_bytes=VMEM_LIMIT),
        name="pack",
    )(index, *arrays, l)


def text_kernel(
    index, wq, wk, wv, wo, wg, lq, lk, lv, lo, lg, l, wqg, wkv, wst, lqg, lkv, lst, buf, lbuf
):
    d = index[0]
    for n, ref in enumerate((wq, wk, wv, wo, wg, lq, lk, lv, lo, lg)):
        buf[n] = jnp.zeros(buf.shape[1:], F32)
        buf[n, 0:TXT, :] = ref[...].astype(F32)
    lbuf[...] = jnp.zeros(lbuf.shape, F32)
    lbuf[:, 0:TXT] = l[:, 0, :]

    def gather(first, odd, q_rows, k_rows):
        q, k, v = buf[first, q_rows, :], buf[first + 1, k_rows, :], buf[first + 2, k_rows, :]
        o, g = buf[first + 3, q_rows, :], buf[first + 4, q_rows, :]

        def pair(a, b):
            low = iota(a.shape, 1) < 64
            left = jnp.where(odd, swap_halves(a), a)
            right = jnp.where(odd, b, swap_halves(b))
            return jnp.where(low, left, right)

        product = o * g
        mine = (iota(product.shape, 1) >= 64) == odd
        return pair(q, g), pair(k, v), jnp.where(mine, product, 0.0)

    qg, kv, product = gather(0, d % 2 == 1, slice(0, TXT_Q), slice(0, TXT_Q))
    ones = jnp.ones((8, 128), F32)
    pick = jnp.where(iota((8, 20), 1) == d, 1.0, 0.0)
    wqg[...] = qg.astype(BF)
    wkv[...] = kv.astype(BF)
    wst[...] = stat_rows(
        picked_rows(pick, lbuf[:, 0:TXT_Q]), picked_sum(ones, product), 0, 0
    ).astype(BF)

    head = 16 + d // 4
    q_rows = pl.ds(pl.multiple_of(HALF * ((d % 4) // 2), 16), HALF_Q)
    k_rows = pl.ds(pl.multiple_of(HALF * (d % 2), 16), HALF_Q)
    qg, kv, product = gather(5, head % 2 == 1, q_rows, k_rows)
    inside = iota((HALF_Q, 128), 0) < HALF
    pick = jnp.where(iota((8, 20), 1) == head, 1.0, 0.0)
    lqg[...] = jnp.where(inside, qg, 0.0).astype(BF)
    lkv[...] = jnp.where(inside, kv, 0.0).astype(BF)
    lsum = picked_rows(pick, lbuf[...])
    lst[...] = stat_rows(
        jnp.where(
            d % 4 < 2, lsum[:, 0:HALF_Q], pltpu.roll(lsum, lsum.shape[1] - HALF, 1)[:, 0:HALF_Q]
        ),
        picked_sum(ones, jnp.where(inside, product, 0.0)),
        4,
        0,
    ).astype(BF)


def text_prep(index, q, k, v, o, g, l):
    whole = pl.BlockSpec((TXT, 128), lambda i, s: (0, s[0] // 2))
    shared = pl.BlockSpec((TXT, 128), lambda i, s: (0, 8 + s[0] // 8))
    shapes = [
        (TXT_Q, 128), (TXT_Q, 128), (16, TXT_Q), (HALF_Q, 128), (HALF_Q, 128), (16, HALF_Q)
    ]
    return pl.pallas_call(
        text_kernel,
        grid_spec=pltpu.PrefetchScalarGridSpec(
            num_scalar_prefetch=1,
            grid=(1,),
            in_specs=[whole] * 5 + [shared] * 5 + [pl.BlockSpec((20, 1, TXT), lambda i, s: (0, 0, 0))],
            out_specs=[pl.BlockSpec(s, lambda i, s_: (0, 0)) for s in shapes],
            scratch_shapes=[
                pltpu.VMEM((10, HALF + HALF_Q, 128), F32),
                pltpu.VMEM((20, 512), F32),
            ],
        ),
        out_shape=[jax.ShapeDtypeStruct(s, BF) for s in shapes],
        compiler_params=pltpu.CompilerParams(vmem_limit_bytes=VMEM_LIMIT),
        name="text_prep",
    )(index, q, k, v, o, g, q, k, v, o, g, l)


def transposed(x):
    return x.astype(F32).T.astype(BF)


class Head:
    def __init__(self, refs):
        self.ka, self.va, self.b0, self.b1, self.qta, self.gta, self.kt, self.dkv, self.dqt = refs

    @staticmethod
    def scratch(rows):
        return [pltpu.VMEM((rows, 128), BF)] * 4 + [
            pltpu.VMEM((128, rows), BF),
            pltpu.VMEM((128, rows), BF),
            pltpu.VMEM((64, rows), BF),
            pltpu.VMEM((rows, 128), F32),
            pltpu.VMEM((64, rows), F32),
        ]

    def fill(self, at, qg, kv, stat, base):
        rows = qg.shape[0]
        lane = iota((rows, 128), 1)
        low = lane < 64
        zero = jnp.zeros((rows, 128), BF)
        here = pl.ds(at, rows)
        kf = kv.astype(F32)
        off = lane - 64 - base
        ka = jnp.where(low, kf * SCALE, jnp.where((off >= 0) & (off < 3), -1.0, 0.0))
        off = lane - 8 - base
        va = jnp.where(low, jnp.where((off >= 0) & (off < 3), -1.0, 0.0), kf)
        self.ka[here, :] = ka.astype(BF)
        self.va[here, :] = va.astype(BF)
        self.b0[here, :] = jnp.where(low, zero, qg)
        self.b1[here, :] = jnp.where(low, qg, zero)
        qgt = transposed(qg)
        self.qta[0:64, here] = qgt[0:64]
        self.qta[64:80, here] = stat
        self.qta[80:128, here] = jnp.zeros((48, rows), BF)
        self.gta[0:16, here] = stat
        self.gta[16:64, here] = jnp.zeros((48, rows), BF)
        self.gta[64:128, here] = qgt[64:128]
        self.kt[:, here] = transposed(kv)[0:64]

    def zero(self):
        self.dkv[...] = jnp.zeros(self.dkv.shape, F32)
        self.dqt[...] = jnp.zeros(self.dqt.shape, F32)

    def block(self, k0, kb, q0, qb):
        ks, qs = pl.ds(k0, kb), pl.ds(q0, qb)
        p = jnp.exp(dot(self.ka[ks, :], self.qta[:, qs]))
        ds = p * dot(self.va[ks, :], self.gta[:, qs])
        p, ds = p.astype(BF), ds.astype(BF)
        self.dkv[ks, :] += dot(p, self.b0[qs, :]) + dot(ds, self.b1[qs, :])
        self.dqt[:, qs] += dot(self.kt[:, ks], ds)

    def blocks(self, k_all, kb, q_all, qb):
        def q_step(i, _):
            q0 = pl.multiple_of(i * qb, 128)

            def k_step(n, _):
                self.block(pl.multiple_of(n * kb, 128), kb, q0, qb)
                return 0

            return lax.fori_loop(0, k_all // kb, k_step, 0)

        lax.fori_loop(0, q_all // qb, q_step, 0)


def fill_whole(w, recv):
    for s in range(N):
        w.fill(TOK * s, recv[s, 0:128, :], recv[s, 128:256, :], recv[s, 384:400, :], 0)


def fill_shared(h, recv):
    for m in range(N // 2):
        a, b = 2 * m, 2 * m + 1
        stat = jnp.where(iota((16, 128), 1) < 64, recv[a, 384:400, :], recv[b, 384:400, :])
        h.fill(
            128 * m,
            jnp.concatenate([recv[a, 256:320, :], recv[b, 256:320, :]], 0),
            jnp.concatenate([recv[a, 320:384, :], recv[b, 320:384, :]], 0),
            stat,
            4,
        )


def text_pairs_kernel(
    recv, wqg, wkv, wst, lqg, lkv, lst, tout, w_dkv, w_dqt, h_dkv, h_dqt, *refs
):
    w, h = Head(refs[:9]), Head(refs[9:])
    fill_whole(w, recv)
    fill_shared(h, recv)
    for m in range(TXT_Q // 128):
        t = slice(128 * m, 128 * m + 128)
        w.fill(S + 128 * m, wqg[t, :], wkv[t, :], wst[:, t], 0)
    for m in range(HALF_Q // 128):
        t = slice(128 * m, 128 * m + 128)
        h.fill(SH + 128 * m, lqg[t, :], lkv[t, :], lst[:, t], 4)
    w.zero()
    h.zero()

    w.block(S, TXT_K, S, TXT_Q)

    def whole_text(n, _):
        at = pl.multiple_of(n * 2048, 2048)
        w.block(at, 2048, S, TXT_Q)
        w.block(S, TXT_K, at, 2048)
        return 0

    lax.fori_loop(0, S // 2048, whole_text, 0)
    h.block(SH, HALF, SH, HALF_Q)
    h.block(0, SH, SH, HALF_Q)
    h.block(SH, HALF, 0, SH)

    tout[:, 0:WOUT, :] = jnp.zeros((N // 2, WOUT, 128), BF)
    w_dkv[...] = w.dkv[0:S, :]
    w_dqt[...] = w.dqt[:, 0:S]
    h_dkv[...] = h.dkv[0:SH, :]
    h_dqt[...] = h.dqt[:, 0:SH]

    factor = jnp.where(iota((128, 128), 1) < 64, SCALE, 1.0)

    def put(at, value):
        value = value.astype(BF)
        for n in range(N // 2):
            tout[n, WOUT + at : WOUT + at + value.shape[0], :] = value

    for m in range(TXT_Q // 128):
        rows = min(128, TXT_K - 128 * m)
        put(128 * m, w.dkv[S + 128 * m : S + 128 * m + rows, :] * factor[:rows])
    put(TXT_K, h.dkv[SH : SH + 128, :] * factor)
    put(TXT_K + 128, h.dkv[SH + 128 : SH + HALF, :] * factor[: HALF - 128])
    for dqt, at, fold in (
        (w.dqt[:, S:], TXT_K + HALF, W_FOLD),
        (h.dqt[:, SH:], TXT_K + HALF + W_FOLD, L_FOLD),
    ):
        part = dqt * SCALE
        both = jnp.concatenate([part, pltpu.roll(part, part.shape[1] - fold, 1)], 0)
        put(at, both[:, 0:256].T[:fold])


STATE = [(S, 128), (64, S), (SH, 128), (64, SH)]


def text_pairs(recv, texts):
    full = pl.BlockSpec(memory_space=pltpu.VMEM)
    return pl.pallas_call(
        text_pairs_kernel,
        in_specs=[full] * 7,
        out_specs=[full] * 5,
        out_shape=[jax.ShapeDtypeStruct((N // 2, WOUT + TOUT, 128), BF)]
        + [jax.ShapeDtypeStruct(s, F32) for s in STATE],
        scratch_shapes=Head.scratch(W_ROWS) + Head.scratch(L_ROWS),
        compiler_params=pltpu.CompilerParams(vmem_limit_bytes=VMEM_LIMIT),
        name="text_pairs",
    )(recv, *texts)


def scales():
    return jnp.where(iota((128, 128), 1) < 64, SCALE, 1.0)


def image_pairs_kernel(recv, a, b, c, d, out, *refs):
    w, h = Head(refs[:9]), Head(refs[9:])
    fill_whole(w, recv)
    fill_shared(h, recv)
    for source, target in ((a, w.dkv), (b, w.dqt), (c, h.dkv), (d, h.dqt)):
        target[...] = source[...]
    h.blocks(SH, 1024, SH, 512)
    w.blocks(S, 1024, S, 512)
    factor = scales()
    for s in range(N):
        out[s, 0:128, :] = (w.dkv[128 * s : 128 * s + 128, :] * factor).astype(BF)
        part = w.dqt[:, 128 * s : 128 * s + 128] * SCALE
        both = jnp.concatenate([part, swap_halves(part)], 0).T
        out[s, 128:192, :] = both[0:64].astype(BF)
        out[s, 192:256, :] = (h.dkv[64 * s : 64 * s + 64, :] * factor[:64]).astype(BF)
    for m in range(N // 2):
        part = h.dqt[:, 128 * m : 128 * m + 128] * SCALE
        both = jnp.concatenate([part, pltpu.roll(part, 96, 1)], 0).T
        out[2 * m, 256:288, :] = both[0:32].astype(BF)
        out[2 * m + 1, 256:288, :] = both[64:96].astype(BF)


def image_pairs(recv, state):
    full = pl.BlockSpec(memory_space=pltpu.VMEM)
    return pl.pallas_call(
        image_pairs_kernel,
        in_specs=[full] * 5,
        out_specs=full,
        out_shape=jax.ShapeDtypeStruct((N, OUT, 128), BF),
        scratch_shapes=Head.scratch(S) + Head.scratch(SH),
        compiler_params=pltpu.CompilerParams(vmem_limit_bytes=VMEM_LIMIT),
        name="image_pairs",
    )(recv, *state)


def lane_pair(even, odd):
    low = iota(even.shape, 1) < 64
    return (
        jnp.where(low, even, swap_halves(odd)),
        jnp.where(low, swap_halves(even), odd),
    )


def unpack_kernel(recv, dq, dk, dv):
    def part(d, rows):
        return recv[d, rows, :].astype(F32)

    for t in range(N // 2):
        lanes = slice(128 * t, 128 * t + 128)
        keys, values = lane_pair(part(2 * t, slice(0, 128)), part(2 * t + 1, slice(0, 128)))
        dk[:, lanes] = keys.astype(BF)
        dv[:, lanes] = values.astype(BF)
        first, second = lane_pair(part(2 * t, slice(128, 192)), part(2 * t + 1, slice(128, 192)))
        dq[0:64, lanes] = first.astype(BF)
        dq[64:128, lanes] = second.astype(BF)
    for t in range(2):
        lanes = slice(1024 + 128 * t, 1024 + 128 * t + 128)
        for half in range(2):
            rows = slice(64 * half, 64 * half + 64)
            keys, values = lane_pair(
                *(
                    part(4 * r + half, slice(192, 256)) + part(4 * r + 2 + half, slice(192, 256))
                    for r in (2 * t, 2 * t + 1)
                )
            )
            dk[rows, lanes] = keys.astype(BF)
            dv[rows, lanes] = values.astype(BF)
            first, second = lane_pair(
                *(
                    part(4 * r + 2 * half, slice(256, 288))
                    + part(4 * r + 2 * half + 1, slice(256, 288))
                    for r in (2 * t, 2 * t + 1)
                )
            )
            dq[64 * half : 64 * half + 32, lanes] = first.astype(BF)
            dq[64 * half + 32 : 64 * half + 64, lanes] = second.astype(BF)


def unpack(recv):
    full = pl.BlockSpec(memory_space=pltpu.VMEM)
    return pl.pallas_call(
        unpack_kernel,
        in_specs=[full],
        out_specs=[full] * 3,
        out_shape=[jax.ShapeDtypeStruct((TOK, 1280), BF)] * 3,
        compiler_params=pltpu.CompilerParams(vmem_limit_bytes=VMEM_LIMIT),
        name="unpack",
    )(recv)


def unpack_text_kernel(core, mine, other, dq, dk, dv):
    odd_core = core[0] == 1

    def part(d, rows):
        rows = slice(WOUT + rows.start, WOUT + rows.stop)
        a, b = mine[d // 2, rows, :].astype(F32), other[d // 2, rows, :].astype(F32)
        return jnp.where(odd_core, b, a) if d % 2 == 0 else jnp.where(odd_core, a, b)

    at = TXT_K + HALF
    whole_q = slice(at, at + W_FOLD)
    for t in range(N // 2):
        lanes = slice(128 * t, 128 * t + 128)
        keys, values = lane_pair(part(2 * t, slice(0, TXT_K)), part(2 * t + 1, slice(0, TXT_K)))
        dk[:, lanes] = keys[:TXT].astype(BF)
        dv[:, lanes] = values[:TXT].astype(BF)
        first, second = lane_pair(part(2 * t, whole_q), part(2 * t + 1, whole_q))
        dq[0:W_FOLD, lanes] = first.astype(BF)
        dq[W_FOLD:TXT, lanes] = second[: TXT - W_FOLD].astype(BF)
    shared = slice(TXT_K, TXT_K + HALF)
    shared_q = slice(at + W_FOLD, at + W_FOLD + L_FOLD)
    for t in range(2):
        lanes = slice(1024 + 128 * t, 1024 + 128 * t + 128)
        for half in range(2):
            begin, end = HALF * half, min(HALF * half + HALF, TXT)
            keys, values = lane_pair(
                *(
                    part(4 * r + half, shared) + part(4 * r + 2 + half, shared)
                    for r in (2 * t, 2 * t + 1)
                )
            )
            dk[begin:end, lanes] = keys[: end - begin].astype(BF)
            dv[begin:end, lanes] = values[: end - begin].astype(BF)
            first, second = lane_pair(
                *(
                    part(4 * r + 2 * half, shared_q) + part(4 * r + 2 * half + 1, shared_q)
                    for r in (2 * t, 2 * t + 1)
                )
            )
            dq[begin : begin + L_FOLD, lanes] = first.astype(BF)
            dq[begin + L_FOLD : end, lanes] = second[: end - begin - L_FOLD].astype(BF)


def unpack_text(core, mine, other):
    full = pl.BlockSpec(memory_space=pltpu.VMEM)
    return pl.pallas_call(
        unpack_text_kernel,
        in_specs=[pl.BlockSpec(memory_space=pltpu.SMEM), full, full],
        out_specs=[full] * 3,
        out_shape=[jax.ShapeDtypeStruct((TXT, 1280), BF)] * 3,
        compiler_params=pltpu.CompilerParams(vmem_limit_bytes=VMEM_LIMIT),
        name="unpack_text",
    )(core, mine, other)


def exchange(x, axes):
    return lax.all_to_all(x, axes, 0, 0, tiled=True)


def other_core(x):
    return lax.ppermute(x, "core", [(0, 1), (1, 0)])


def shifted(x, axis, by):
    size = lax.axis_size(axis)
    return lax.ppermute(x, axis, [(i, (i + by) % size) for i in range(size)])


def gathered(x, axis):
    size, me = lax.axis_size(axis), lax.axis_index(axis)
    out = jnp.zeros((size, *x.shape), x.dtype)
    for by in range(size):
        piece = shifted(x, axis, by) if by else x
        out = lax.dynamic_update_index_in_dim(out, piece, (me - by) % size, 0)
    return out


def weight_operands(og, o):
    chips, y = lax.axis_size(CHIPS), lax.axis_size("y")
    core, me = lax.axis_index("core"), lax.axis_index("y")
    tokens = og.shape[0]
    rows = og.shape[1] // (2 * chips)
    padded = -(-rows // (8 * y)) * 8 * y
    blocks = og.T.reshape(chips, 2, rows, tokens)
    blocks = jnp.pad(blocks, ((0, 0),) * 2 + ((0, padded - rows), (0, 0)))
    blocks = blocks.reshape(chips, 2, y, padded // y, tokens).transpose(1, 2, 0, 3, 4)
    blocks = blocks.reshape(2, y, -1, tokens)
    mine = lax.dynamic_index_in_dim(blocks, core, 0, False)
    theirs = other_core(lax.dynamic_index_in_dim(blocks, 1 - core, 0, False))
    both = jnp.concatenate([mine, theirs], 2)
    pieces = [lax.dynamic_index_in_dim(both, (me + by) % y, 0, False) for by in range(y)]
    left, right = pieces[:1], [o]
    for by in range(1, y):
        right.append(shifted(o, "y", by))
        left.append(shifted(pieces[by], "y", by))
    return left, right


def weight_kernel(*refs):
    *operands, _, out, scratch = refs
    count = len(operands) // 3
    total = None
    for left, own, cross in zip(*(operands[k * count : k * count + count] for k in range(3))):
        term = dot(left[...], jnp.concatenate([own[...], cross[...]], 0))
        total = term if total is None else total + term
    each = WOUT // 10
    for p in range(N // 2):
        for t in range(10):
            scratch[p, each * t : each * t + each, :] = total[
                each * p : each * p + each, 128 * t : 128 * t + 128
            ]
        out[p] = scratch[p].astype(BF)


def add_weight_part(message, left, own, cross):
    args = [*left, *own, *cross]
    return pl.pallas_call(
        weight_kernel,
        grid=(1,),
        in_specs=[pl.BlockSpec(x.shape, lambda i: (0, 0)) for x in args]
        + [pl.BlockSpec(memory_space=pl.ANY)],
        out_specs=pl.BlockSpec((N // 2, WOUT, 128), lambda i: (0, 0, 0)),
        out_shape=jax.ShapeDtypeStruct(message.shape, BF),
        scratch_shapes=[pltpu.VMEM((N // 2, WOUT, 128), F32)],
        input_output_aliases={len(args): 0},
        compiler_params=pltpu.CompilerParams(vmem_limit_bytes=VMEM_LIMIT),
        name="weight",
    )(*args, message)


def weight_total(parts, rows, after):
    part = gathered(parts.astype(F32).sum(0).astype(BF), "y")
    if lax.axis_size("xl") > 1:
        other, _ = lax.optimization_barrier((shifted(part, "xl", 1), after))
        part = part.astype(F32) + other.astype(F32)
    y, height, lanes = part.shape
    part = part.reshape(y, 10, height // 10, lanes).swapaxes(1, 2)
    return part.reshape(-1, 10 * lanes)[:rows].astype(F32)


def shards(
    image_query,
    image_key,
    image_value,
    image_output,
    output_grad,
    image_logsum,
    text_query,
    text_key,
    text_value,
    text_output,
    text_grad,
    text_logsum,
    out_weight,
):
    device = lax.axis_index(SEQ).astype(jnp.int32).reshape(1)
    core = lax.axis_index("core").astype(jnp.int32).reshape(1)
    send = pack(
        device,
        output_grad[0],
        out_weight,
        image_query[0],
        image_key[0],
        image_value[0],
        image_output[0],
        image_logsum.transpose(2, 0, 1),
    )
    send, upstream = lax.optimization_barrier((send, output_grad[0]))
    recv = exchange(send, SEQ)
    texts = text_prep(
        device,
        text_query[0],
        text_key[0],
        text_value[0],
        text_output[0],
        text_grad[0],
        text_logsum.transpose(2, 0, 1),
    )
    upstream, outputs, _ = lax.optimization_barrier((upstream, image_output[0], texts[0]))
    left, own = weight_operands(upstream, outputs)
    text_out, *state = text_pairs(recv, texts)
    cross = [other_core(outputs)]
    left, own, text_out = lax.optimization_barrier((left, own, text_out))
    cross += [other_core(x) for x in own[1:]]
    mine = exchange(add_weight_part(text_out, left, own, cross), CHIPS)
    out = image_pairs(recv, state)
    mine, _ = lax.optimization_barrier((mine, out))
    text_grads = unpack_text(core, mine, other_core(mine))
    got = exchange(out, SEQ)
    got, text_grads = lax.optimization_barrier((got, text_grads))
    grads = unpack(got)
    weight_grad = weight_total(mine[:, :WOUT], output_grad.shape[2] // N, grads)
    return (*(g[None] for g in grads), *(g[None] for g in text_grads), weight_grad)


def solution(mesh):
    pairs = 2 if mesh.shape["img"] > 1 else 1
    finer = Mesh(
        mesh.devices.reshape(mesh.shape["img"] // pairs, pairs, 4, 2, 2),
        ("y", "xl", "z", "xh", "core"),
    )
    image = P(IMG, SEQ, None)
    text = P(IMG, None, None)
    return jax.shard_map(
        shards,
        mesh=finer,
        in_specs=(image,) * 6 + (text,) * 6 + (P(),),
        out_specs=(image,) * 3 + (text,) * 3 + (P(SEQ, None),),
        check_vma=False,
    )
```

```python
import jax
import jax.numpy as jnp
from jax import lax
from jax.experimental import pallas as pl
from jax.experimental.pallas import tpu as pltpu
from jax.sharding import Mesh
from jax.sharding import PartitionSpec as P

SEQ = ("z", "xh", "core")
CHIPS = ("z", "xh")
IMG = ("y", "xl")
BF = jnp.bfloat16
F32 = jnp.float32
NT = (((1,), (1,)), ((), ()))

N = 16
TOK = 128
S = N * TOK
TXT = 333
TXT_Q = 384
TXT_K = 336
HALF = 176
HALF_Q = 256
SH = N * TOK // 2
W_ROWS = S + TXT_Q
L_ROWS = SH + HALF_Q
SCALE = 0.125
MSG = 400
OUT = 288
W_FOLD = 176
L_FOLD = 96
TOUT = TXT_K + HALF + W_FOLD + L_FOLD
WOUT = 400
VMEM_LIMIT = 56 * 2**20


def iota(shape, dim):
    return lax.broadcasted_iota(jnp.int32, shape, dim)


def thirds(x):
    high = x.astype(BF).astype(F32)
    rest = x - high
    middle = rest.astype(BF).astype(F32)
    return high, middle, rest - middle


def dot(a, b):
    return jnp.dot(a, b, preferred_element_type=F32)


def dot_nt(a, b):
    return lax.dot_general(a, b, NT, preferred_element_type=F32)


def swap_halves(x):
    return pltpu.roll(x, 64, 1)


def picked_sum(pick, x):
    a, b, c = thirds(x)
    pick = pick.astype(BF)
    return dot_nt(pick, a.astype(BF)) + dot_nt(pick, b.astype(BF)) + dot_nt(pick, c.astype(BF))


def picked_rows(pick, x):
    a, b, c = thirds(x)
    pick = pick.astype(BF)
    return dot(pick, a.astype(BF)) + dot(pick, b.astype(BF)) + dot(pick, c.astype(BF))


def stat_rows(lsum, delta, base, row):
    width = lsum.shape[1]
    rows = iota((16, width), 0)
    tile = jnp.zeros((16, width), F32)
    for k, part in enumerate(thirds(lsum)):
        tile = jnp.where(rows == base + k, part[row : row + 1, :], tile)
    for k, part in enumerate(thirds(delta)):
        tile = jnp.where(rows == 8 + base + k, part[row : row + 1, :], tile)
    return tile


def pack_kernel(
    index, og_hbm, w_hbm, q_hbm, k_hbm, v_hbm, o_hbm, l, send, og, w, q, k, v, o, acc, sems
):
    depth = w.shape[0]
    chunk = 640
    parts = [(at, min(chunk, depth - at)) for at in range(0, depth, chunk)]
    copies = [
        pltpu.make_async_copy(source, target, sems.at[n])
        for n, (source, target) in enumerate(
            [(k_hbm, k), (v_hbm, v), (og_hbm, og)]
            + [(w_hbm.at[pl.ds(at, size)], w.at[pl.ds(at, size)]) for at, size in parts]
            + [(q_hbm, q), (o_hbm, o)]
        )
    ]
    for copy in copies:
        copy.start()
    low = iota((TOK, 128), 1) < 64

    def packed(a, b, head):
        lanes = slice(128 * (head // 2), 128 * (head // 2) + 128)
        a, b = a[:, lanes].astype(F32), b[:, lanes].astype(F32)
        if head % 2 == 0:
            return jnp.where(low, a, swap_halves(b)).astype(BF)
        return jnp.where(low, swap_halves(a), b).astype(BF)

    copies[0].wait()
    copies[1].wait()
    for d in range(N):
        send[d, 128:256, :] = packed(k, v, d)
    for r in range(4):
        kv = packed(k, v, 16 + r)
        for qi in range(2):
            for ki in range(2):
                send[4 * r + 2 * qi + ki, 320:384, :] = kv[64 * ki : 64 * ki + 64]

    copies[2].wait()
    for n, (at, size) in enumerate(parts):
        copies[3 + n].wait()
        term = dot(og[:, at : at + size], w[at : at + size, :])
        acc[...] = term if n == 0 else acc[...] + term
    copies[-2].wait()
    copies[-1].wait()
    acc[...] = acc[...].astype(BF).astype(F32)
    delta = picked_sum(
        jnp.where(iota((24, 1280), 1) // 64 == iota((24, 1280), 0), 1.0, 0.0),
        acc[...] * o[...].astype(F32),
    )
    lsum = l[:, 0, :]
    here = iota((16, 128), 1) // 64 == index[0] % 2
    for r in range(4):
        qg = packed(q, acc, 16 + r)
        stat = stat_rows(lsum, delta, 4, 16 + r)
        moved = swap_halves(stat)
        for qi in range(2):
            mine = jnp.where(here, jnp.where(index[0] % 2 == qi, stat, moved), 0.0)
            for ki in range(2):
                d = 4 * r + 2 * qi + ki
                send[d, 0:128, :] = packed(q, acc, d)
                send[d, 256:320, :] = qg[64 * qi : 64 * qi + 64]
                send[d, 384:400, :] = (stat_rows(lsum, delta, 0, d) + mine).astype(BF)


def pack(index, og, w, q, k, v, o, l):
    anywhere = pl.BlockSpec(memory_space=pl.ANY)
    full = pl.BlockSpec(memory_space=pltpu.VMEM)
    arrays = [og, w, q, k, v, o]
    return pl.pallas_call(
        pack_kernel,
        in_specs=[pl.BlockSpec(memory_space=pltpu.SMEM)] + [anywhere] * 6 + [full],
        out_specs=full,
        out_shape=jax.ShapeDtypeStruct((N, MSG, 128), BF),
        scratch_shapes=[pltpu.VMEM(x.shape, BF) for x in arrays]
        + [pltpu.VMEM(q.shape, F32), pltpu.SemaphoreType.DMA((5 + -(-w.shape[0] // 640),))],
        compiler_params=pltpu.CompilerParams(vmem_limit_bytes=VMEM_LIMIT),
        name="pack",
    )(index, *arrays, l)


def text_kernel(
    index, wq, wk, wv, wo, wg, lq, lk, lv, lo, lg, l, wqg, wkv, wst, lqg, lkv, lst, buf, lbuf
):
    d = index[0]
    for n, ref in enumerate((wq, wk, wv, wo, wg, lq, lk, lv, lo, lg)):
        buf[n] = jnp.zeros(buf.shape[1:], F32)
        buf[n, 0:TXT, :] = ref[...].astype(F32)
    lbuf[...] = jnp.zeros(lbuf.shape, F32)
    lbuf[:, 0:TXT] = l[:, 0, :]

    def gather(first, odd, q_rows, k_rows):
        q, k, v = buf[first, q_rows, :], buf[first + 1, k_rows, :], buf[first + 2, k_rows, :]
        o, g = buf[first + 3, q_rows, :], buf[first + 4, q_rows, :]

        def pair(a, b):
            low = iota(a.shape, 1) < 64
            left = jnp.where(odd, swap_halves(a), a)
            right = jnp.where(odd, b, swap_halves(b))
            return jnp.where(low, left, right)

        product = o * g
        mine = (iota(product.shape, 1) >= 64) == odd
        return pair(q, g), pair(k, v), jnp.where(mine, product, 0.0)

    qg, kv, product = gather(0, d % 2 == 1, slice(0, TXT_Q), slice(0, TXT_Q))
    ones = jnp.ones((8, 128), F32)
    pick = jnp.where(iota((8, 20), 1) == d, 1.0, 0.0)
    wqg[...] = qg.astype(BF)
    wkv[...] = kv.astype(BF)
    wst[...] = stat_rows(
        picked_rows(pick, lbuf[:, 0:TXT_Q]), picked_sum(ones, product), 0, 0
    ).astype(BF)

    head = 16 + d // 4
    q_rows = pl.ds(pl.multiple_of(HALF * ((d % 4) // 2), 16), HALF_Q)
    k_rows = pl.ds(pl.multiple_of(HALF * (d % 2), 16), HALF_Q)
    qg, kv, product = gather(5, head % 2 == 1, q_rows, k_rows)
    inside = iota((HALF_Q, 128), 0) < HALF
    pick = jnp.where(iota((8, 20), 1) == head, 1.0, 0.0)
    lqg[...] = jnp.where(inside, qg, 0.0).astype(BF)
    lkv[...] = jnp.where(inside, kv, 0.0).astype(BF)
    lsum = picked_rows(pick, lbuf[...])
    lst[...] = stat_rows(
        jnp.where(
            d % 4 < 2, lsum[:, 0:HALF_Q], pltpu.roll(lsum, lsum.shape[1] - HALF, 1)[:, 0:HALF_Q]
        ),
        picked_sum(ones, jnp.where(inside, product, 0.0)),
        4,
        0,
    ).astype(BF)


def text_prep(index, q, k, v, o, g, l):
    whole = pl.BlockSpec((TXT, 128), lambda i, s: (0, s[0] // 2))
    shared = pl.BlockSpec((TXT, 128), lambda i, s: (0, 8 + s[0] // 8))
    shapes = [
        (TXT_Q, 128), (TXT_Q, 128), (16, TXT_Q), (HALF_Q, 128), (HALF_Q, 128), (16, HALF_Q)
    ]
    return pl.pallas_call(
        text_kernel,
        grid_spec=pltpu.PrefetchScalarGridSpec(
            num_scalar_prefetch=1,
            grid=(1,),
            in_specs=[whole] * 5 + [shared] * 5 + [pl.BlockSpec((20, 1, TXT), lambda i, s: (0, 0, 0))],
            out_specs=[pl.BlockSpec(s, lambda i, s_: (0, 0)) for s in shapes],
            scratch_shapes=[
                pltpu.VMEM((10, HALF + HALF_Q, 128), F32),
                pltpu.VMEM((20, 512), F32),
            ],
        ),
        out_shape=[jax.ShapeDtypeStruct(s, BF) for s in shapes],
        compiler_params=pltpu.CompilerParams(vmem_limit_bytes=VMEM_LIMIT),
        name="text_prep",
    )(index, q, k, v, o, g, q, k, v, o, g, l)


def transposed(x):
    return x.astype(F32).T.astype(BF)


class Head:
    def __init__(self, refs):
        self.ka, self.va, self.b0, self.b1, self.qta, self.gta, self.kt, self.dkv, self.dqt = refs

    @staticmethod
    def scratch(rows):
        return [pltpu.VMEM((rows, 128), BF)] * 4 + [
            pltpu.VMEM((128, rows), BF),
            pltpu.VMEM((128, rows), BF),
            pltpu.VMEM((64, rows), BF),
            pltpu.VMEM((rows, 128), F32),
            pltpu.VMEM((64, rows), F32),
        ]

    def fill(self, at, qg, kv, stat, base):
        rows = qg.shape[0]
        lane = iota((rows, 128), 1)
        low = lane < 64
        zero = jnp.zeros((rows, 128), BF)
        here = pl.ds(at, rows)
        kf = kv.astype(F32)
        off = lane - 64 - base
        ka = jnp.where(low, kf * SCALE, jnp.where((off >= 0) & (off < 3), -1.0, 0.0))
        off = lane - 8 - base
        va = jnp.where(low, jnp.where((off >= 0) & (off < 3), -1.0, 0.0), kf)
        self.ka[here, :] = ka.astype(BF)
        self.va[here, :] = va.astype(BF)
        self.b0[here, :] = jnp.where(low, zero, qg)
        self.b1[here, :] = jnp.where(low, qg, zero)
        qgt = transposed(qg)
        self.qta[0:64, here] = qgt[0:64]
        self.qta[64:80, here] = stat
        self.qta[80:128, here] = jnp.zeros((48, rows), BF)
        self.gta[0:16, here] = stat
        self.gta[16:64, here] = jnp.zeros((48, rows), BF)
        self.gta[64:128, here] = qgt[64:128]
        self.kt[:, here] = transposed(kv)[0:64]

    def zero(self):
        self.dkv[...] = jnp.zeros(self.dkv.shape, F32)
        self.dqt[...] = jnp.zeros(self.dqt.shape, F32)

    def block(self, k0, kb, q0, qb):
        ks, qs = pl.ds(k0, kb), pl.ds(q0, qb)
        p = jnp.exp(dot(self.ka[ks, :], self.qta[:, qs]))
        ds = p * dot(self.va[ks, :], self.gta[:, qs])
        p, ds = p.astype(BF), ds.astype(BF)
        self.dkv[ks, :] += dot(p, self.b0[qs, :]) + dot(ds, self.b1[qs, :])
        self.dqt[:, qs] += dot(self.kt[:, ks], ds)

    def blocks(self, k_all, kb, q_all, qb):
        def q_step(i, _):
            q0 = pl.multiple_of(i * qb, 128)

            def k_step(n, _):
                self.block(pl.multiple_of(n * kb, 128), kb, q0, qb)
                return 0

            return lax.fori_loop(0, k_all // kb, k_step, 0)

        lax.fori_loop(0, q_all // qb, q_step, 0)


def fill_whole(w, recv):
    for s in range(N):
        w.fill(TOK * s, recv[s, 0:128, :], recv[s, 128:256, :], recv[s, 384:400, :], 0)


def fill_shared(h, recv):
    for m in range(N // 2):
        a, b = 2 * m, 2 * m + 1
        stat = jnp.where(iota((16, 128), 1) < 64, recv[a, 384:400, :], recv[b, 384:400, :])
        h.fill(
            128 * m,
            jnp.concatenate([recv[a, 256:320, :], recv[b, 256:320, :]], 0),
            jnp.concatenate([recv[a, 320:384, :], recv[b, 320:384, :]], 0),
            stat,
            4,
        )


def text_pairs_kernel(
    recv, wqg, wkv, wst, lqg, lkv, lst, message, w_dkv, w_dqt, h_dkv, h_dqt, tout, sems, *refs
):
    w, h = Head(refs[:9]), Head(refs[9:])
    fill_whole(w, recv)
    fill_shared(h, recv)
    for m in range(TXT_Q // 128):
        t = slice(128 * m, 128 * m + 128)
        w.fill(S + 128 * m, wqg[t, :], wkv[t, :], wst[:, t], 0)
    for m in range(HALF_Q // 128):
        t = slice(128 * m, 128 * m + 128)
        h.fill(SH + 128 * m, lqg[t, :], lkv[t, :], lst[:, t], 4)
    w.zero()
    h.zero()

    w.block(S, TXT_K, S, TXT_Q)

    def whole_text(n, _):
        at = pl.multiple_of(n * 2048, 2048)
        w.block(at, 2048, S, TXT_Q)
        w.block(S, TXT_K, at, 2048)
        return 0

    lax.fori_loop(0, S // 2048, whole_text, 0)
    h.block(SH, HALF, SH, HALF_Q)
    h.block(0, SH, SH, HALF_Q)
    h.block(SH, HALF, 0, SH)

    w_dkv[...] = w.dkv[0:S, :]
    w_dqt[...] = w.dqt[:, 0:S]
    h_dkv[...] = h.dkv[0:SH, :]
    h_dqt[...] = h.dqt[:, 0:SH]

    factor = jnp.where(iota((128, 128), 1) < 64, SCALE, 1.0)

    def put(at, value):
        tout[at : at + value.shape[0], :] = value.astype(BF)

    for m in range(TXT_Q // 128):
        rows = min(128, TXT_K - 128 * m)
        put(128 * m, w.dkv[S + 128 * m : S + 128 * m + rows, :] * factor[:rows])
    put(TXT_K, h.dkv[SH : SH + 128, :] * factor)
    put(TXT_K + 128, h.dkv[SH + 128 : SH + HALF, :] * factor[: HALF - 128])
    for dqt, at, fold in (
        (w.dqt[:, S:], TXT_K + HALF, W_FOLD),
        (h.dqt[:, SH:], TXT_K + HALF + W_FOLD, L_FOLD),
    ):
        part = dqt * SCALE
        both = jnp.concatenate([part, pltpu.roll(part, part.shape[1] - fold, 1)], 0)
        put(at, both[:, 0:256].T[:fold])
    copies = [
        pltpu.make_async_copy(tout, message.at[n, pl.ds(WOUT, TOUT)], sems.at[n])
        for n in range(N // 2)
    ]
    for copy in copies:
        copy.start()
    for copy in copies:
        copy.wait()


STATE = [(S, 128), (64, S), (SH, 128), (64, SH)]


def text_pairs(recv, texts):
    full = pl.BlockSpec(memory_space=pltpu.VMEM)
    return pl.pallas_call(
        text_pairs_kernel,
        in_specs=[full] * 7,
        out_specs=[pl.BlockSpec(memory_space=pl.ANY)] + [full] * 4,
        out_shape=[jax.ShapeDtypeStruct((N // 2, WOUT + TOUT, 128), BF)]
        + [jax.ShapeDtypeStruct(s, F32) for s in STATE],
        scratch_shapes=[pltpu.VMEM((TOUT, 128), BF), pltpu.SemaphoreType.DMA((N // 2,))]
        + Head.scratch(W_ROWS)
        + Head.scratch(L_ROWS),
        compiler_params=pltpu.CompilerParams(vmem_limit_bytes=VMEM_LIMIT),
        name="text_pairs",
    )(recv, *texts)


def scales():
    return jnp.where(iota((128, 128), 1) < 64, SCALE, 1.0)


def image_pairs_kernel(recv, a, b, c, d, out, *refs):
    w, h = Head(refs[:9]), Head(refs[9:])
    fill_whole(w, recv)
    fill_shared(h, recv)
    for source, target in ((a, w.dkv), (b, w.dqt), (c, h.dkv), (d, h.dqt)):
        target[...] = source[...]
    h.blocks(SH, 1024, SH, 512)
    w.blocks(S, 1024, S, 512)
    factor = scales()
    for s in range(N):
        out[s, 0:128, :] = (w.dkv[128 * s : 128 * s + 128, :] * factor).astype(BF)
        part = w.dqt[:, 128 * s : 128 * s + 128] * SCALE
        both = jnp.concatenate([part, swap_halves(part)], 0).T
        out[s, 128:192, :] = both[0:64].astype(BF)
        out[s, 192:256, :] = (h.dkv[64 * s : 64 * s + 64, :] * factor[:64]).astype(BF)
    for m in range(N // 2):
        part = h.dqt[:, 128 * m : 128 * m + 128] * SCALE
        both = jnp.concatenate([part, pltpu.roll(part, 96, 1)], 0).T
        out[2 * m, 256:288, :] = both[0:32].astype(BF)
        out[2 * m + 1, 256:288, :] = both[64:96].astype(BF)


def image_pairs(recv, state):
    full = pl.BlockSpec(memory_space=pltpu.VMEM)
    return pl.pallas_call(
        image_pairs_kernel,
        in_specs=[full] * 5,
        out_specs=full,
        out_shape=jax.ShapeDtypeStruct((N, OUT, 128), BF),
        scratch_shapes=Head.scratch(S) + Head.scratch(SH),
        compiler_params=pltpu.CompilerParams(vmem_limit_bytes=VMEM_LIMIT),
        name="image_pairs",
    )(recv, *state)


def lane_pair(even, odd):
    low = iota(even.shape, 1) < 64
    return (
        jnp.where(low, even, swap_halves(odd)),
        jnp.where(low, swap_halves(even), odd),
    )


def unpack_kernel(recv, dq, dk, dv):
    def part(d, rows):
        return recv[d, rows, :].astype(F32)

    for t in range(N // 2):
        lanes = slice(128 * t, 128 * t + 128)
        keys, values = lane_pair(part(2 * t, slice(0, 128)), part(2 * t + 1, slice(0, 128)))
        dk[:, lanes] = keys.astype(BF)
        dv[:, lanes] = values.astype(BF)
        first, second = lane_pair(part(2 * t, slice(128, 192)), part(2 * t + 1, slice(128, 192)))
        dq[0:64, lanes] = first.astype(BF)
        dq[64:128, lanes] = second.astype(BF)
    for t in range(2):
        lanes = slice(1024 + 128 * t, 1024 + 128 * t + 128)
        for half in range(2):
            rows = slice(64 * half, 64 * half + 64)
            keys, values = lane_pair(
                *(
                    part(4 * r + half, slice(192, 256)) + part(4 * r + 2 + half, slice(192, 256))
                    for r in (2 * t, 2 * t + 1)
                )
            )
            dk[rows, lanes] = keys.astype(BF)
            dv[rows, lanes] = values.astype(BF)
            first, second = lane_pair(
                *(
                    part(4 * r + 2 * half, slice(256, 288))
                    + part(4 * r + 2 * half + 1, slice(256, 288))
                    for r in (2 * t, 2 * t + 1)
                )
            )
            dq[64 * half : 64 * half + 32, lanes] = first.astype(BF)
            dq[64 * half + 32 : 64 * half + 64, lanes] = second.astype(BF)


def unpack(recv):
    full = pl.BlockSpec(memory_space=pltpu.VMEM)
    return pl.pallas_call(
        unpack_kernel,
        in_specs=[full],
        out_specs=[full] * 3,
        out_shape=[jax.ShapeDtypeStruct((TOK, 1280), BF)] * 3,
        compiler_params=pltpu.CompilerParams(vmem_limit_bytes=VMEM_LIMIT),
        name="unpack",
    )(recv)


def unpack_text_kernel(core, mine, other, dq, dk, dv):
    odd_core = core[0] == 1

    def part(d, rows):
        rows = slice(WOUT + rows.start, WOUT + rows.stop)
        a, b = mine[d // 2, rows, :].astype(F32), other[d // 2, rows, :].astype(F32)
        return jnp.where(odd_core, b, a) if d % 2 == 0 else jnp.where(odd_core, a, b)

    at = TXT_K + HALF
    whole_q = slice(at, at + W_FOLD)
    for t in range(N // 2):
        lanes = slice(128 * t, 128 * t + 128)
        keys, values = lane_pair(part(2 * t, slice(0, TXT_K)), part(2 * t + 1, slice(0, TXT_K)))
        dk[:, lanes] = keys[:TXT].astype(BF)
        dv[:, lanes] = values[:TXT].astype(BF)
        first, second = lane_pair(part(2 * t, whole_q), part(2 * t + 1, whole_q))
        dq[0:W_FOLD, lanes] = first.astype(BF)
        dq[W_FOLD:TXT, lanes] = second[: TXT - W_FOLD].astype(BF)
    shared = slice(TXT_K, TXT_K + HALF)
    shared_q = slice(at + W_FOLD, at + W_FOLD + L_FOLD)
    for t in range(2):
        lanes = slice(1024 + 128 * t, 1024 + 128 * t + 128)
        for half in range(2):
            begin, end = HALF * half, min(HALF * half + HALF, TXT)
            keys, values = lane_pair(
                *(
                    part(4 * r + half, shared) + part(4 * r + 2 + half, shared)
                    for r in (2 * t, 2 * t + 1)
                )
            )
            dk[begin:end, lanes] = keys[: end - begin].astype(BF)
            dv[begin:end, lanes] = values[: end - begin].astype(BF)
            first, second = lane_pair(
                *(
                    part(4 * r + 2 * half, shared_q) + part(4 * r + 2 * half + 1, shared_q)
                    for r in (2 * t, 2 * t + 1)
                )
            )
            dq[begin : begin + L_FOLD, lanes] = first.astype(BF)
            dq[begin + L_FOLD : end, lanes] = second[: end - begin - L_FOLD].astype(BF)


def unpack_text(core, mine, other):
    full = pl.BlockSpec(memory_space=pltpu.VMEM)
    return pl.pallas_call(
        unpack_text_kernel,
        in_specs=[pl.BlockSpec(memory_space=pltpu.SMEM), full, full],
        out_specs=[full] * 3,
        out_shape=[jax.ShapeDtypeStruct((TXT, 1280), BF)] * 3,
        compiler_params=pltpu.CompilerParams(vmem_limit_bytes=VMEM_LIMIT),
        name="unpack_text",
    )(core, mine, other)


def exchange(x, axes):
    return lax.all_to_all(x, axes, 0, 0, tiled=True)


def other_core(x):
    return lax.ppermute(x, "core", [(0, 1), (1, 0)])


def shifted(x, axis, by):
    size = lax.axis_size(axis)
    return lax.ppermute(x, axis, [(i, (i + by) % size) for i in range(size)])


def gathered(x, axis):
    size, me = lax.axis_size(axis), lax.axis_index(axis)
    out = jnp.zeros((size, *x.shape), x.dtype)
    for by in range(size):
        piece = shifted(x, axis, by) if by else x
        out = lax.dynamic_update_index_in_dim(out, piece, (me - by) % size, 0)
    return out


def weight_operands(og, o):
    chips, y = lax.axis_size(CHIPS), lax.axis_size("y")
    core, me = lax.axis_index("core"), lax.axis_index("y")
    tokens = og.shape[0]
    rows = og.shape[1] // (2 * chips)
    padded = -(-rows // (8 * y)) * 8 * y
    blocks = og.T.reshape(chips, 2, rows, tokens)
    blocks = jnp.pad(blocks, ((0, 0),) * 2 + ((0, padded - rows), (0, 0)))
    blocks = blocks.reshape(chips, 2, y, padded // y, tokens).transpose(1, 2, 0, 3, 4)
    blocks = blocks.reshape(2, y, -1, tokens)
    mine = lax.dynamic_index_in_dim(blocks, core, 0, False)
    theirs = other_core(lax.dynamic_index_in_dim(blocks, 1 - core, 0, False))
    both = jnp.concatenate([mine, theirs], 2)
    pieces = [lax.dynamic_index_in_dim(both, (me + by) % y, 0, False) for by in range(y)]
    left, right = pieces[:1], [o]
    for by in range(1, y):
        right.append(shifted(o, "y", by))
        left.append(shifted(pieces[by], "y", by))
    return left, right


def weight_kernel(*refs):
    *operands, _, out, scratch = refs
    count = len(operands) // 3
    total = None
    for left, own, cross in zip(*(operands[k * count : k * count + count] for k in range(3))):
        term = dot(left[...], jnp.concatenate([own[...], cross[...]], 0))
        total = term if total is None else total + term
    each = WOUT // 10
    for p in range(N // 2):
        for t in range(10):
            scratch[p, each * t : each * t + each, :] = total[
                each * p : each * p + each, 128 * t : 128 * t + 128
            ]
        out[p] = scratch[p].astype(BF)


def add_weight_part(message, left, own, cross):
    args = [*left, *own, *cross]
    return pl.pallas_call(
        weight_kernel,
        grid=(1,),
        in_specs=[pl.BlockSpec(x.shape, lambda i: (0, 0)) for x in args]
        + [pl.BlockSpec(memory_space=pl.ANY)],
        out_specs=pl.BlockSpec((N // 2, WOUT, 128), lambda i: (0, 0, 0)),
        out_shape=jax.ShapeDtypeStruct(message.shape, BF),
        scratch_shapes=[pltpu.VMEM((N // 2, WOUT, 128), F32)],
        input_output_aliases={len(args): 0},
        compiler_params=pltpu.CompilerParams(vmem_limit_bytes=VMEM_LIMIT),
        name="weight",
    )(*args, message)


def across(x, by):
    y, xl = lax.axis_size("y"), lax.axis_size("xl")
    pairs = [
        (i * xl + j, (i + by) % y * xl + (j + 1) % xl) for i in range(y) for j in range(xl)
    ]
    return lax.ppermute(x, IMG, pairs)


def placed(pieces, axis):
    size, me = lax.axis_size(axis), lax.axis_index(axis)
    out = jnp.zeros((size, *pieces[0].shape), pieces[0].dtype)
    for by, piece in enumerate(pieces):
        out = lax.dynamic_update_index_in_dim(out, piece, (me - by) % size, 0)
    return out


def weight_total(part, others, rows):
    if others:
        part = part.astype(F32) + placed(others, "y").astype(F32)
    y, height, lanes = part.shape
    part = part.reshape(y, 10, height // 10, lanes).swapaxes(1, 2)
    return part.reshape(-1, 10 * lanes)[:rows].astype(F32)


def shards(
    image_query,
    image_key,
    image_value,
    image_output,
    output_grad,
    image_logsum,
    text_query,
    text_key,
    text_value,
    text_output,
    text_grad,
    text_logsum,
    out_weight,
):
    device = lax.axis_index(SEQ).astype(jnp.int32).reshape(1)
    core = lax.axis_index("core").astype(jnp.int32).reshape(1)
    send = pack(
        device,
        output_grad[0],
        out_weight,
        image_query[0],
        image_key[0],
        image_value[0],
        image_output[0],
        image_logsum.transpose(2, 0, 1),
    )
    send, upstream = lax.optimization_barrier((send, output_grad[0]))
    recv = exchange(send, SEQ)
    texts = text_prep(
        device,
        text_query[0],
        text_key[0],
        text_value[0],
        text_output[0],
        text_grad[0],
        text_logsum.transpose(2, 0, 1),
    )
    upstream, outputs, _ = lax.optimization_barrier((upstream, image_output[0], texts[0]))
    left, own = weight_operands(upstream, outputs)
    text_out, *state = text_pairs(recv, texts)
    cross = [other_core(outputs)]
    left, own, text_out = lax.optimization_barrier((left, own, text_out))
    cross += [other_core(x) for x in own[1:]]
    mine = exchange(add_weight_part(text_out, left, own, cross), CHIPS)
    out = image_pairs(recv, state)
    mine, _ = lax.optimization_barrier((mine, out))
    text_grads = unpack_text(core, mine, other_core(mine))
    got = exchange(out, SEQ)
    part = mine[:, :WOUT].astype(F32).sum(0).astype(BF)
    both_sides = lax.axis_size("xl") > 1
    others = [across(part, by) for by in range(lax.axis_size("y")) if both_sides]
    part = gathered(part, "y")
    got, text_grads, part = lax.optimization_barrier((got, text_grads, part))
    grads = unpack(got)
    others, _ = lax.optimization_barrier((others, grads))
    weight_grad = weight_total(part, others, output_grad.shape[2] // N)
    return (*(g[None] for g in grads), *(g[None] for g in text_grads), weight_grad)


def solution(mesh):
    pairs = 2 if mesh.shape["img"] > 1 else 1
    finer = Mesh(
        mesh.devices.reshape(mesh.shape["img"] // pairs, pairs, 4, 2, 2),
        ("y", "xl", "z", "xh", "core"),
    )
    image = P(IMG, SEQ, None)
    text = P(IMG, None, None)
    return jax.shard_map(
        shards,
        mesh=finer,
        in_specs=(image,) * 6 + (text,) * 6 + (P(),),
        out_specs=(image,) * 3 + (text,) * 3 + (P(SEQ, None),),
        check_vma=False,
    )
```
